128 devices in a mesh: tm: 16 (over y, x), lane: 8 (over z, core).
Axes of the slice: x: 4, y: 4, z: 4, core: 2. Of those that a mesh axis runs over, the one named last changes fastest.
Arguments:
- replay: bfloat16 [8, 16, 1024, 1024], P('lane', 'tm'), may hold values from -6 to 6
- block_owner: int32 [16, 8, 8, 1], P('tm'), may hold values from 0 to 7; in each aligned block of 8 rows (0 to 7, 8 to 15, ..., all dimensions but the last counted through in order) at most 2 rows name the same one
- block_slot: int32 [16, 8, 8], P('tm'), may hold values from 0 to 3
- block_fill: int32 [8, 16, 8], P('lane', 'tm'), may hold values from 64 to 256
- log_decay: float32 [8, 16, 32768], P('lane', None, 'tm'), may hold values from -2 to 0
- resets: int32 [8, 32768], P('lane', 'tm'), may hold values from 0 to 1, as said below
- cotangent: bfloat16 [8, 32768, 1024], P('lane', 'tm'), may hold values from -6 to 6
- w_in: bfloat16 [1024, 1024], replicated, may hold values from -0.1875 to 0.1875
- w_bc: bfloat16 [1024, 128], replicated, may hold values from -0.01171875 to 0.01171875
- w_out: bfloat16 [1024, 1024], replicated, may hold values from -0.1875 to 0.1875
Outputs:
- grad_in: float32 [1024, 1024], P(('tm', 'lane'))
- grad_bc: float32 [1024, 128], P(('tm', 'lane'))
- grad_out: float32 [1024, 1024], P(('tm', 'lane'))
The draws below stay inside these ranges and needn't reach their ends.
Inputs may be any that keep to these rules, and one draw needn't show every extreme that they name: `block_owner`: among the 8 blocks of one segment on one time shard, no owner is named more than 2 times. `resets`: exactly one step of each segment is flagged.
All inputs are finite; a program needn't handle non-finite values.
Results may differ from the reference program's by a relative error of at most 0.0057.
Values may be sent and summed in bfloat16 or wider, within the bound.
No kernel may reach another device: no remote copies, remote signals or barrier semaphores. Data moves between devices by JAX's collectives and lax.ppermute only.
A program may use at most 192 MiB of HBM per device.

```python
import math
import jax
import jax.numpy as jnp
import numpy as np
from jax import lax

D = 1024
HEAD = 64
STATE = 64
BLOCK = 256
BUFCH = 4
TOK_DEV = 2048
HEADS = 16
BLOCKS = 8
SEGMENT_COUNT = 8
SHARDS = 16
SEGMENT_STEPS = 32768
ROWS = 262144
CAP = 2


def draw_log_decay(key, part):
    random_keys_split = jax.random.split(key, 6)
    keep_share = 0.5
    sluggish_heads = jax.random.uniform(random_keys_split[0], (SEGMENT_COUNT, HEADS, 1)) < keep_share
    slow_rate = jax.random.uniform(random_keys_split[1], (SEGMENT_COUNT, HEADS, 1), jnp.float32, 0.2, 1.0) / SEGMENT_STEPS
    fast_rate = jax.random.uniform(random_keys_split[2], (SEGMENT_COUNT, HEADS, 1), jnp.float32, 10.0, 17.0) / BLOCK
    baseline_rate = jnp.where(sluggish_heads, slow_rate, fast_rate)
    jaggedness_level = jnp.exp(jax.random.uniform(random_keys_split[3], (SEGMENT_COUNT, HEADS, SEGMENT_STEPS), jnp.float32, math.log(0.5), math.log(2.0)))
    spike_position = jax.random.randint(random_keys_split[4], (SEGMENT_COUNT, 2), 0, SEGMENT_STEPS)
    spike_strike = jnp.any(lax.broadcasted_iota(jnp.int32, (SEGMENT_COUNT, 2, SEGMENT_STEPS), 2) == spike_position[:, :, None], axis=1)
    spike_penalty = jnp.log(jax.random.uniform(random_keys_split[5], (SEGMENT_COUNT, 1, SEGMENT_STEPS), jnp.float32, 0.6, 0.8))
    spike_decline = jnp.where(spike_strike[:, None, :] & sluggish_heads, spike_penalty, 0.0)
    return -baseline_rate * jaggedness_level + spike_decline


def draw_resets(key, part):
    reset_at = jax.random.randint(key, (SEGMENT_COUNT,), 1, SEGMENT_STEPS)
    return (lax.broadcasted_iota(jnp.int32, (SEGMENT_COUNT, SEGMENT_STEPS), 1) == reset_at[:, None]).astype(jnp.int32)


def place_ends(array, rng, least, high):
    longest = array.shape.index(max(array.shape))
    spots = []
    for shift in (0, 1):
        where = [jax.random.randint(jax.random.fold_in(rng, axis), (), 0, length) for axis, length in enumerate(array.shape)]
        where[longest] = (where[longest] + shift) % array.shape[longest]
        spots.append(tuple(where))
    return array.at[spots[0]].set(least).at[spots[1]].set(high)


def shard_levels(stream_key, dims, pieces, low, largest):
    level = 1.0
    for dim, shards_of in pieces:
        draws = jax.random.uniform(jax.random.fold_in(jax.random.fold_in(stream_key, 6), dim), (shards_of,), jnp.float32, low / len(pieces), largest / len(pieces))
        level = level * jnp.repeat(jnp.exp(draws), dims[dim] // shards_of).reshape((-1,) + (1,) * (len(dims) - 1 - dim))
    return level


def shared_out(key, own, number, rows, number_of, top, bound, skew):
    ranking = jax.random.permutation(key, number_of)
    heavy_load, usual = portions_of(number_of, rows * top, bound, skew, True), portions_of(number_of, rows * top, bound, skew, False)
    places = jnp.arange(number_of)

    def named(sizes, turn):
        used = int((sizes > 0).sum())
        fixed = max(1, used // 4)
        passed = fixed + (places - fixed + turn * (used - fixed)) % max(1, number_of - fixed)
        return jnp.zeros((number_of,), jnp.int32).at[ranking[jnp.where(places < fixed, places, passed)]].set(jnp.asarray(sizes, jnp.int32))

    sizes = jnp.where(number % 4 == 0, named(heavy_load, number // 4), named(usual, number - number // 4 - 1))
    mixed = jax.random.permutation(jax.random.fold_in(own, 3), number_of)
    giver, taker = mixed[0:number_of // 2 * 2:2], mixed[1:number_of // 2 * 2:2]
    margin = jnp.minimum(sizes[giver] - 1, bound - sizes[taker]) // 2
    margin = jnp.where((giver == ranking[0]) | (taker == ranking[0]) | (sizes[taker] == 0), 0, jnp.maximum(margin, 0))
    passed = jax.random.randint(jax.random.fold_in(own, 4), (number_of // 2,), 0, 1 << 20) % (margin + 1)
    sizes = sizes.at[giver].add(-passed).at[taker].add(passed)
    items = jnp.searchsorted(jnp.cumsum(sizes), jnp.arange(rows * top), side="right").astype(jnp.int32)
    grid = items.reshape(top, rows).T
    grid = grid[jax.random.permutation(jax.random.fold_in(own, 1), rows)]
    turn = jax.random.randint(jax.random.fold_in(own, 2), (rows, 1), 0, top)
    return jnp.take_along_axis(grid, (jnp.arange(top)[None, :] + turn) % top, axis=1)


def portions_of(amount, total, bound, lean, full):
    weights = [(1 << 20) // math.isqrt(standing ** lean) + 1 for standing in range(1, amount + 1)]
    largest = bound if full else min(bound, max(-(-total // amount), total * weights[0] // sum(weights)))
    least = 1 if total - largest >= amount - 1 else 0
    counts, spare = [largest] + [least] * (amount - 1), total - largest - least * (amount - 1)
    while spare > 0:
        movable = [i for i in range(1, amount) if counts[i] < largest] or [i for i in range(1, amount) if counts[i] < bound]
        whole, left = sum([weights[i] for i in movable]), spare
        for i in movable:
            more = min(bound - counts[i], max(1, left * weights[i] // whole), spare)
            counts[i] = counts[i] + more
            spare = spare - more
    return np.array(counts)


def normal_values(own_key, dims, scale, bound, cuts=(), kind=jnp.bfloat16):
    values = jax.random.normal(own_key, dims, jnp.float32) * scale
    if len(cuts) > 0:
        values = shard_levels(own_key, dims, cuts, -0.22, 0.18) * values
    return jnp.clip(values, min=-bound, max=bound).astype(kind)


def setup_inputs(seed: int = 0) -> dict:
    streams_of = jax.random.split(jax.random.key(seed), 11)
    replay = normal_values(streams_of[0], (SEGMENT_COUNT, SHARDS, BUFCH * BLOCK, D), 1.0, 6.0, ((0, 8), (1, 16)))
    block_owner_keys = jax.random.split(jax.random.fold_in(streams_of[1], 1), SHARDS * SEGMENT_COUNT * BLOCKS // BLOCKS)
    block_owner_turns = jax.random.permutation(jax.random.fold_in(streams_of[1], 3), SHARDS * SEGMENT_COUNT * BLOCKS // BLOCKS)
    block_owner = jax.vmap(lambda own, number: shared_out(jax.random.fold_in(streams_of[1], 2), own, number, BLOCKS, SEGMENT_COUNT, 1, CAP, 2))(block_owner_keys, block_owner_turns).reshape((SHARDS, SEGMENT_COUNT, BLOCKS, 1))
    block_slot = place_ends(jax.random.randint(streams_of[2], (SHARDS, SEGMENT_COUNT, BLOCKS), 0, BUFCH), jax.random.fold_in(streams_of[2], 1), 0, BUFCH - 1).astype(jnp.int32)
    block_fill = place_ends(jax.random.randint(streams_of[3], (SEGMENT_COUNT, SHARDS, BLOCKS), BLOCK // 4, BLOCK + 1), jax.random.fold_in(streams_of[3], 1), BLOCK // 4, BLOCK).astype(jnp.int32)
    log_decay = draw_log_decay(jax.random.fold_in(streams_of[10], 71), 0)
    resets = draw_resets(jax.random.fold_in(streams_of[10], 71), 0)
    cotangent = normal_values(streams_of[6], (SEGMENT_COUNT, SEGMENT_STEPS, D), 1.0, 6.0, ((0, 8), (1, 16)))
    w_in = normal_values(streams_of[7], (D, D), D ** -0.5, 0.1875)
    w_bc = normal_values(streams_of[8], (D, 2 * STATE), (4 * D * STATE) ** -0.5, 0.01171875)
    w_out = normal_values(streams_of[9], (D, D), D ** -0.5, 0.1875)
    return {"replay": replay, "block_owner": block_owner, "block_slot": block_slot, "block_fill": block_fill, "log_decay": log_decay, "resets": resets, "cotangent": cotangent, "w_in": w_in, "w_bc": w_bc, "w_out": w_out}


def decay_matrix(log_rate, episode_flags):
    cumulated = jnp.cumsum(log_rate, axis=1)
    counted = jnp.cumsum(episode_flags)
    extent = log_rate.shape[1]
    row_pos = lax.broadcasted_iota(jnp.int32, (extent, extent), 0)
    col_pos = lax.broadcasted_iota(jnp.int32, (extent, extent), 1)
    linked = (counted[:, None] == counted[None, :]) & (col_pos <= row_pos)
    spread = jnp.where(linked[None], cumulated[:, :, None] - cumulated[:, None, :], 0.0)
    return jnp.where(linked[None], jnp.exp(spread), 0.0)

def edge_weights(log_rate, episode_flags):
    cumulated = jnp.cumsum(log_rate, axis=1)
    counted = jnp.cumsum(episode_flags)
    opening = jnp.where(counted[None, :] == 0, jnp.exp(cumulated), 0.0)
    closing = jnp.where(counted[None, :] == counted[-1], jnp.exp(cumulated[:, -1:] - cumulated), 0.0)
    return (opening, closing)

def product(spec, left_op, right_op):
    return jnp.einsum(spec, left_op.astype(jnp.float32), right_op.astype(jnp.float32))

def block_grads(block_items):
    inner_proj, write_keys, read_keys, upstream, log_rate, episode_flags, opening, closing, weighted_in, weighted_out, start_state, end_adjoint = block_items
    extent = inner_proj.shape[0]
    decays = decay_matrix(log_rate, episode_flags)
    scores = jnp.dot(read_keys, write_keys.T, preferred_element_type=jnp.float32)
    mixing = (decays * scores[None]).astype(jnp.bfloat16)
    state_bf = start_state.astype(jnp.bfloat16)
    adjoint_bf = end_adjoint.astype(jnp.bfloat16)
    carried = product('in,hpn->ihp', read_keys, state_bf)
    readout = product('hij,jhp->ihp', mixing, inner_proj) + opening.T[:, :, None] * carried
    pairing = product('ihp,jhp->hij', upstream, inner_proj)
    blended = (decays * pairing).astype(jnp.bfloat16)
    returned = product('jn,hpn->jhp', write_keys, adjoint_bf)
    grad_inner = product('hij,ihp->jhp', mixing, upstream) + closing.T[:, :, None] * returned
    grad_write = product('hij,in->jn', blended, read_keys) + product('jhp,hpn->jn', weighted_in, adjoint_bf)
    grad_read = product('hij,jn->in', blended, write_keys) + product('ihp,hpn->in', weighted_out, state_bf)
    return (readout.astype(jnp.bfloat16).reshape(extent, -1), grad_inner.astype(jnp.bfloat16).reshape(extent, -1), jnp.concatenate([grad_write, grad_read], axis=1).astype(jnp.bfloat16))

def advance(carried_in, block_items):
    current, gained = carried_in
    block_factor, pushed = block_items
    return ((block_factor[:, None, None] * current + pushed, gained * block_factor), (current, gained))

def reference(replay, block_owner, block_slot, block_fill, log_decay, resets, cotangent, w_in, w_bc, w_out):
    num_heads = D // HEAD
    stacked = replay.reshape(SEGMENT_COUNT, SHARDS, BUFCH, BLOCK, D)
    owners = block_owner[..., 0].astype(jnp.int32)
    shard_ids = lax.broadcasted_iota(jnp.int32, owners.shape, 0)
    taken = stacked[owners, shard_ids, block_slot.astype(jnp.int32)]
    delivered_all = jnp.transpose(taken, (1, 0, 2, 3, 4)).reshape(SEGMENT_COUNT, SEGMENT_STEPS, D)
    usable = (lax.broadcasted_iota(jnp.int32, (SEGMENT_COUNT, SHARDS, TOK_DEV // BLOCK, BLOCK), 3) < block_fill[..., None]).reshape(SEGMENT_COUNT, SEGMENT_STEPS)
    delivered_all = jnp.where(usable[..., None], delivered_all, jnp.zeros((), delivered_all.dtype))
    masked_all = jnp.where(usable[..., None], cotangent, jnp.zeros((), cotangent.dtype))
    block_total = SEGMENT_STEPS // BLOCK

    def per_lane(summed, lane_items):
        delivered, masked, rates, episode_flags = lane_items
        inner_proj = jnp.dot(delivered, w_in, preferred_element_type=jnp.float32).astype(jnp.bfloat16)
        projected = jnp.dot(delivered, w_bc, preferred_element_type=jnp.float32).astype(jnp.bfloat16)
        upstream = jnp.dot(masked, w_out.T, preferred_element_type=jnp.float32).astype(jnp.bfloat16)
        inner_b = inner_proj.reshape(block_total, BLOCK, num_heads, HEAD)
        upstream_b = upstream.reshape(block_total, BLOCK, num_heads, HEAD)
        write_b = projected[:, :STATE].reshape(block_total, BLOCK, STATE)
        read_b = projected[:, STATE:].reshape(block_total, BLOCK, STATE)
        rates_b = jnp.transpose(rates.reshape(num_heads, block_total, BLOCK), (1, 0, 2))
        flags_b = episode_flags.reshape(block_total, BLOCK)
        opening, closing = jax.vmap(edge_weights)(rates_b, flags_b)
        factor = opening[:, :, -1]
        weighted_in = (jnp.transpose(closing, (0, 2, 1))[..., None] * inner_b).astype(jnp.bfloat16)
        weighted_out = (jnp.transpose(opening, (0, 2, 1))[..., None] * upstream_b).astype(jnp.bfloat16)
        push_fwd = product('kjhp,kjn->khpn', weighted_in, write_b)
        push_bwd = product('kihp,kin->khpn', weighted_out, read_b)
        zero_state = jnp.zeros((num_heads, HEAD, STATE), jnp.float32)
        unit_gain = jnp.ones((num_heads,), jnp.float32)
        starts = lax.scan(advance, (zero_state, unit_gain), (factor, push_fwd))[1][0]
        ends = lax.scan(advance, (zero_state, unit_gain), (factor, push_bwd), reverse=True)[1][0]
        readout, grad_inner, grad_keys = lax.map(block_grads, (inner_b, write_b, read_b, upstream_b, rates_b, flags_b, opening, closing, weighted_in, weighted_out, starts, ends))
        readout = readout.reshape(SEGMENT_STEPS, D)
        grad_inner = grad_inner.reshape(SEGMENT_STEPS, D)
        grad_keys = grad_keys.reshape(SEGMENT_STEPS, 2 * STATE)
        terms = jnp.concatenate([jnp.dot(delivered.T, grad_inner, preferred_element_type=jnp.float32), jnp.dot(delivered.T, grad_keys, preferred_element_type=jnp.float32), jnp.dot(readout.T, masked, preferred_element_type=jnp.float32)], axis=1)
        return (summed + terms, None)
    initial = jnp.zeros((D, 2 * D + 2 * STATE), jnp.float32)
    summed = lax.scan(per_lane, initial, (delivered_all, masked_all, log_decay, resets))[0]
    summed = summed * (1.0 / math.sqrt(ROWS))
    return (summed[:, :D], summed[:, D:D + 2 * STATE], summed[:, D + 2 * STATE:])
```

```python
import math

import jax
import jax.numpy as jnp
from jax import lax
from jax.experimental import pallas as pl
from jax.experimental.pallas import tpu as pltpu
from jax.sharding import Mesh
from jax.sharding import PartitionSpec as P

D = 1024
HEAD = 64
HEADS = 16
STATE = 64
BLOCK = 256
BUFCH = 4
TM = ("y", "x")
LOG2E = math.log2(math.e)
FAR = -1e4
F32, BF16 = jnp.float32, jnp.bfloat16
CNT, OPEN, CLOSE = 16, 32, 48
NT = (((1,), (1,)), ((), ()))
TN = (((0,), (0,)), ((), ()))
NN = (((1,), (0,)), ((), ()))
VMEM_LIMIT = 56 * 1024 * 1024


def mm(a, b, dims=NN):
    return lax.dot_general(a, b, dims, preferred_element_type=F32)


def split(x):
    high = x.astype(BF16)
    return jnp.concatenate([high, (x - high.astype(F32)).astype(BF16)], axis=1)


def spread_matrix(base):
    row = lax.broadcasted_iota(jnp.int32, (2 * 128, D), 0) & 127
    head = lax.broadcasted_iota(jnp.int32, (2 * 128, D), 1) >> 6
    return jnp.where(row == head + base, 1.0, 0.0).astype(BF16)


def call(kernel, name, out_shape, grid_spec, flops, nbytes):
    return pl.pallas_call(
        kernel,
        out_shape=out_shape,
        grid_spec=grid_spec,
        name=name,
        compiler_params=pltpu.CompilerParams(vmem_limit_bytes=VMEM_LIMIT),
        cost_estimate=pl.CostEstimate(flops=flops, bytes_accessed=nbytes, transcendentals=0),
    )


def shape(dims, kind):
    return jax.ShapeDtypeStruct(dims, kind)


def valid_rows(fill, width):
    return lax.broadcasted_iota(jnp.int32, (BLOCK, width), 0) < fill


def upstream_kernel(fill, decay, resets, cot, w_out, up, rows, cols, gain):
    b = pl.program_id(0)
    upper = lax.broadcasted_iota(jnp.int32, (BLOCK, BLOCK), 0) <= lax.broadcasted_iota(
        jnp.int32, (BLOCK, BLOCK), 1
    )
    upper = jnp.where(upper, 1.0, 0.0)
    both = jnp.concatenate(
        [decay[...] * LOG2E, jnp.broadcast_to(resets[0].astype(F32), (8, BLOCK))], axis=0
    )
    summed = lax.dot_general(
        both, upper, NN, precision=lax.Precision.HIGHEST, preferred_element_type=F32
    )
    cum, count = summed[:HEADS], summed[HEADS : HEADS + 8]
    two = jnp.concatenate([count, count], axis=0)
    opening = jnp.where(two == 0.0, jnp.exp2(cum), 0.0)
    last = jnp.broadcast_to(cum[:, BLOCK - 1 :], (HEADS, BLOCK))
    last_two = jnp.broadcast_to(two[:, BLOCK - 1 :], (HEADS, BLOCK))
    closing = jnp.where(two == last_two, jnp.exp2(last - cum), 0.0)
    table = jnp.concatenate(
        [cum, two, opening, closing, jnp.zeros((64, BLOCK), F32)], axis=0
    )
    rows[...] = table[:32]
    turned = table.T
    cols[...] = turned
    end = jnp.broadcast_to(turned[BLOCK - 1 :], (8, 128))

    @pl.when(b == 0)
    def _():
        gain[...] = end

    @pl.when(b > 0)
    def _():
        gain[...] = gain[...] * end

    masked = jnp.where(valid_rows(fill[b], D), cot[0], jnp.zeros((), BF16))
    up[...] = mm(masked, w_out[...], NT).astype(BF16)


def project_kernel(
    place, fill, rows, w_in, w_bc, up, cols, inner, keys, starts, pushed, gains, total, spread_o, spread_c, state
):
    b = pl.program_id(0)

    @pl.when(b == 0)
    def _():
        spread_o[...] = spread_matrix(OPEN)
        spread_c[...] = spread_matrix(CLOSE)
        state[...] = jnp.zeros_like(state)

    taken = jnp.where(valid_rows(fill[b], D), rows[0], jnp.zeros((), BF16))
    x = mm(taken, w_in[...]).astype(BF16)
    k = mm(taken, w_bc[...]).astype(BF16)
    inner[...] = x
    keys[...] = k
    parts = split(cols[...])
    opening = mm(parts, spread_o[...])
    closing = mm(parts, spread_c[...])
    into = (closing * x.astype(F32)).astype(BF16)
    out = (opening * up[...].astype(F32)).astype(BF16)
    turned = k.astype(F32).T.astype(BF16)
    push_in = mm(turned[:STATE], into)
    push_out = mm(turned[STATE:], out)
    factor = opening[BLOCK - 1 :]
    before = jnp.where(b == 0, 1.0, state[128:129])
    starts[0] = state[:64]
    pushed[0] = push_out
    gains[0] = jnp.concatenate(
        [jnp.broadcast_to(factor, (8, D)), jnp.broadcast_to(before, (8, D))], axis=0
    )
    state[:64] = state[:64] * factor + push_in
    state[64:128] = state[64:128] + before * push_out
    state[128:] = jnp.broadcast_to(before * factor, (8, D))

    @pl.when(b == pl.num_programs(0) - 1)
    def _():
        total[...] = state[:128].astype(BF16)


def inside_kernel(inner, keys, up, rows, cols, ro, gi, pair):
    at = lax.broadcasted_iota(jnp.int32, (BLOCK, BLOCK), 0)
    to = lax.broadcasted_iota(jnp.int32, (BLOCK, BLOCK), 1)
    linked = (to <= at) & (cols[:, CNT : CNT + 1] == rows[CNT : CNT + 1, :])
    bias = jnp.where(linked, 0.0, FAR)
    k = keys[...]
    scores = mm(k[:, STATE:], k[:, :STATE], NT)
    left = lax.broadcasted_iota(jnp.int32, (BLOCK, 128), 1) < HEAD
    zero = jnp.zeros((), BF16)
    paired = jnp.zeros((BLOCK, BLOCK), F32)
    for q in range(HEADS // 2):
        lanes = slice(128 * q, 128 * q + 128)
        x, u = inner[:, lanes], up[:, lanes]
        readout = grad = None
        for s in range(2):
            h = 2 * q + s
            mine = left if s == 0 else ~left
            xs, us = jnp.where(mine, x, zero), jnp.where(mine, u, zero)
            decays = jnp.exp2(cols[:, h : h + 1] - rows[h : h + 1, :] + bias)
            mixing = (decays * scores).astype(BF16)
            paired = paired + decays * mm(us, x, NT)
            r, g = mm(mixing, xs), mm(mixing, us, TN)
            readout = r if s == 0 else readout + r
            grad = g if s == 0 else grad + g
        ro[:, lanes] = readout.astype(BF16)
        gi[:, lanes] = grad.astype(BF16)
    pair[0] = paired.astype(BF16)


def scan_kernel(which, terms, gain, entering, forth, wide):
    wide[...] = mm(split(gain[...]), spread_matrix(OPEN))
    shards = terms.shape[0]
    state = jnp.zeros((8, D), F32)
    for t in range(shards):
        forth[t] = state
        state = state * wide[t : t + 1] + terms[t].astype(F32)
    back = jnp.zeros((8, D), F32)
    ahead = jnp.full((8, D), which[0], jnp.int32) < shards // 2
    for t in reversed(range(shards)):
        entering[t] = jnp.where(ahead, forth[t], back).astype(BF16)
        back = back * wide[t : t + 1] + terms[t].astype(F32)


def gradient_kernel(
    place, fill, rows, cot, inner, up, keys, cols, ro, gi, pair, starts, pushed, gains, enter,
    grads, acc_in, acc_bc, acc_out, spread_o, spread_c, finish,
):
    step = pl.program_id(0)
    last = pl.num_programs(0) - 1
    b = last - step

    @pl.when(step == 0)
    def _():
        spread_o[...] = spread_matrix(OPEN)
        spread_c[...] = spread_matrix(CLOSE)
        finish[...] = enter[64:].astype(F32)
        acc_in[...] = jnp.zeros_like(acc_in)
        acc_bc[...] = jnp.zeros_like(acc_bc)
        acc_out[...] = jnp.zeros_like(acc_out)

    factor, before = gains[0, 0:1], gains[0, 8:9]
    start = (starts[0] + before * enter[:64].astype(F32)).astype(BF16)
    end = finish[...].astype(BF16)
    finish[...] = finish[...] * factor + pushed[0]
    parts = split(cols[...])
    opening = mm(parts, spread_o[...])
    closing = mm(parts, spread_c[...])
    k = keys[...]
    write, read = k[:, :STATE], k[:, STATE:]
    readout = (ro[...].astype(F32) + opening * mm(read, start)).astype(BF16)
    grad = (gi[...].astype(F32) + closing * mm(write, end)).astype(BF16)
    into = (closing * inner[...].astype(F32)).astype(BF16)
    out = (opening * up[...].astype(F32)).astype(BF16)
    g = pair[0]
    grad_write = mm(g, read, TN) + mm(into, end, NT)
    grad_read = mm(g, write) + mm(out, start, NT)
    grad_keys = jnp.concatenate([grad_write, grad_read], axis=1).astype(BF16)
    wide = valid_rows(fill[b], D)
    taken = jnp.where(wide, rows[0], jnp.zeros((), BF16))
    masked = jnp.where(wide, cot[0], jnp.zeros((), BF16))
    acc_in[...] += mm(taken, grad, TN)
    acc_bc[...] += mm(taken, grad_keys, TN)
    acc_out[...] += mm(readout, masked, TN)

    @pl.when(step == last)
    def _():
        scale = 1.0 / 512.0
        grads[:, :D] = (acc_in[...] * scale).astype(BF16)
        grads[:, D : D + 128] = (acc_bc[...] * scale).astype(BF16)
        grads[:, D + 128 :] = (acc_out[...] * scale).astype(BF16)


def on_device(
    replay, block_owner, block_slot, block_fill, log_decay, resets, cotangent, w_in, w_bc, w_out
):
    shards = lax.axis_size(TM)
    my_lane = lax.axis_index(("z", "c"))
    blocks = block_fill.shape[2]
    steps = blocks * BLOCK
    fill = block_fill[0, 0]
    owner = lax.dynamic_index_in_dim(block_owner[0, :, :, 0], my_lane, 0, keepdims=False)
    slot = lax.dynamic_index_in_dim(block_slot[0], my_lane, 0, keepdims=False)
    place = owner * BUFCH + slot

    gathered = lax.all_gather(replay[0, 0], ("z", "c"), axis=0, tiled=True)
    gathered = gathered.reshape(-1, BLOCK, D)

    whole = lambda *dims: pl.BlockSpec(dims, lambda b, *_: (0,) * len(dims))
    tall = lambda width: pl.BlockSpec((BLOCK, width), lambda b, *_: (b, 0))
    lead = lambda *dims: pl.BlockSpec((1, *dims), lambda b, *_: (b,) + (0,) * len(dims))
    table_rows = pl.BlockSpec((32, BLOCK), lambda b, *_: (0, b))

    up, rows, cols, gain = call(
        upstream_kernel,
        "upstream",
        (shape((steps, D), BF16), shape((32, steps), F32), shape((steps, 128), F32), shape((8, 128), F32)),
        pltpu.PrefetchScalarGridSpec(
            num_scalar_prefetch=1,
            grid=(blocks,),
            in_specs=[
                pl.BlockSpec((HEADS, BLOCK), lambda b, *_: (0, b)),
                pl.BlockSpec((1, 1, BLOCK), lambda b, *_: (b, 0, 0)),
                pl.BlockSpec((1, BLOCK, D), lambda b, *_: (0, b, 0)),
                whole(D, D),
            ],
            out_specs=[tall(D), table_rows, tall(128), whole(8, 128)],
        ),
        2 * steps * D * D,
        12 << 20,
    )(fill, log_decay[0], resets.reshape(blocks, 1, BLOCK), cotangent, w_out)
    all_gain = lax.all_gather(gain[:1], TM, axis=0, tiled=True)

    picked = pl.BlockSpec((1, BLOCK, D), lambda b, place, *_: (place[b], 0, 0))
    inner, keys, starts, pushed, gains, total = call(
        project_kernel,
        "project",
        (
            shape((steps, D), BF16),
            shape((steps, 128), BF16),
            shape((blocks, STATE, D), F32),
            shape((blocks, STATE, D), F32),
            shape((blocks, 16, D), F32),
            shape((128, D), BF16),
        ),
        pltpu.PrefetchScalarGridSpec(
            num_scalar_prefetch=2,
            grid=(blocks,),
            in_specs=[picked, whole(D, D), whole(D, 128), tall(D), tall(128)],
            out_specs=[tall(D), tall(128), lead(STATE, D), lead(STATE, D), lead(16, D), whole(128, D)],
            scratch_shapes=[
                pltpu.VMEM((256, D), BF16),
                pltpu.VMEM((256, D), BF16),
                pltpu.VMEM((136, D), F32),
            ],
        ),
        2 * steps * D * (D + 128 + 128 + 256),
        20 << 20,
    )(place, fill, gathered, w_in, w_bc, up, cols)

    ro, gi, pair = call(
        inside_kernel,
        "inside",
        (shape((steps, D), BF16), shape((steps, D), BF16), shape((blocks, BLOCK, BLOCK), BF16)),
        pl.GridSpec(
            grid=(blocks,),
            in_specs=[tall(D), tall(128), tall(D), table_rows, tall(128)],
            out_specs=[tall(D), tall(D), lead(BLOCK, BLOCK)],
        ),
        2 * blocks * HEADS * 3 * BLOCK**3,
        18 << 20,
    )(inner, keys, up, rows, cols)

    terms = lax.all_to_all(total.reshape(shards, 8, D), TM, 0, 0)
    entering = call(
        scan_kernel,
        "scan",
        shape((shards, 8, D), BF16),
        pltpu.PrefetchScalarGridSpec(
            num_scalar_prefetch=1,
            grid=(1,),
            in_specs=[whole(shards, 8, D), whole(shards, 128)],
            out_specs=whole(shards, 8, D),
            scratch_shapes=[pltpu.VMEM((shards, 8, D), F32), pltpu.VMEM((shards, D), F32)],
        ),
        1 << 20,
        1 << 20,
    )(lax.axis_index(TM).reshape(1), terms, all_gain)
    enter = lax.all_to_all(entering, TM, 0, 0).reshape(128, D)

    back = lambda spec: pl.BlockSpec(
        spec.block_shape, lambda s, *refs: spec.index_map(blocks - 1 - s, *refs)
    )
    grads = call(
        gradient_kernel,
        "gradient",
        shape((D, 2 * D + 128), BF16),
        pltpu.PrefetchScalarGridSpec(
            num_scalar_prefetch=2,
            grid=(blocks,),
            in_specs=[
                back(s)
                for s in (
                    picked,
                    pl.BlockSpec((1, BLOCK, D), lambda b, *_: (0, b, 0)),
                    tall(D),
                    tall(D),
                    tall(128),
                    tall(128),
                    tall(D),
                    tall(D),
                    lead(BLOCK, BLOCK),
                    lead(STATE, D),
                    lead(STATE, D),
                    lead(16, D),
                    whole(128, D),
                )
            ],
            out_specs=whole(D, 2 * D + 128),
            scratch_shapes=[
                pltpu.VMEM((D, D), F32),
                pltpu.VMEM((D, 128), F32),
                pltpu.VMEM((D, D), F32),
                pltpu.VMEM((256, D), BF16),
                pltpu.VMEM((256, D), BF16),
                pltpu.VMEM((STATE, D), F32),
            ],
        ),
        2 * steps * D * (2 * D + 128 + 512),
        40 << 20,
    )(place, fill, gathered, cotangent, inner, up, keys, cols, ro, gi, pair, starts, pushed, gains, enter)

    lanes = lax.axis_size(("z", "c"))
    part = grads.reshape(shards, lanes, 8, -1).transpose(1, 0, 2, 3)
    part = lax.all_to_all(part, ("z", "c"), 0, 0).astype(F32).sum(0)
    part = lax.all_to_all(part.astype(BF16), TM, 0, 0).astype(F32).sum(0)
    return (part[:, :D], part[:, D : D + 128], part[:, D + 128 :])


def solution(mesh):
    torus = Mesh(mesh.devices.reshape(4, 4, 4, 2), ("y", "x", "z", "c"))
    lane = ("z", "c")
    every = TM + lane
    return jax.shard_map(
        on_device,
        mesh=torus,
        in_specs=(
            P(lane, TM, None, None),
            P(TM, None, None, None),
            P(TM, None, None),
            P(lane, TM, None),
            P(lane, None, TM),
            P(lane, TM),
            P(lane, TM, None),
            P(),
            P(),
            P(),
        ),
        out_specs=(P(every, None), P(every, None), P(every, None)),
        check_vma=False,
    )
```

```python
import math

import jax
import jax.numpy as jnp
from jax import lax
from jax.experimental import pallas as pl
from jax.experimental.pallas import tpu as pltpu
from jax.sharding import Mesh
from jax.sharding import PartitionSpec as P

D = 1024
HEAD = 64
HEADS = 16
STATE = 64
BLOCK = 256
BUFCH = 4
TM = ("y", "x")
LOG2E = math.log2(math.e)
FAR = -1e4
F32, BF16 = jnp.float32, jnp.bfloat16
CNT, OPEN, CLOSE = 16, 32, 48
NT = (((1,), (1,)), ((), ()))
TN = (((0,), (0,)), ((), ()))
NN = (((1,), (0,)), ((), ()))
VMEM_LIMIT = 56 * 1024 * 1024


def mm(a, b, dims=NN):
    return lax.dot_general(a, b, dims, preferred_element_type=F32)


def split(x):
    high = x.astype(BF16)
    return jnp.concatenate([high, (x - high.astype(F32)).astype(BF16)], axis=1)


def spread_matrix(base):
    row = lax.broadcasted_iota(jnp.int32, (2 * 128, D), 0) & 127
    head = lax.broadcasted_iota(jnp.int32, (2 * 128, D), 1) >> 6
    return jnp.where(row == head + base, 1.0, 0.0).astype(BF16)


def call(kernel, name, out_shape, grid_spec, flops, nbytes):
    return pl.pallas_call(
        kernel,
        out_shape=out_shape,
        grid_spec=grid_spec,
        name=name,
        compiler_params=pltpu.CompilerParams(vmem_limit_bytes=VMEM_LIMIT),
        cost_estimate=pl.CostEstimate(flops=flops, bytes_accessed=nbytes, transcendentals=0),
    )


def shape(dims, kind):
    return jax.ShapeDtypeStruct(dims, kind)


def valid_rows(fill, width):
    return lax.broadcasted_iota(jnp.int32, (BLOCK, width), 0) < fill


def upstream_kernel(fill, decay, resets, cot, w_out, up, rows, cols, ends, gain):
    b = pl.program_id(0)
    upper = lax.broadcasted_iota(jnp.int32, (BLOCK, BLOCK), 0) <= lax.broadcasted_iota(
        jnp.int32, (BLOCK, BLOCK), 1
    )
    upper = jnp.where(upper, 1.0, 0.0)
    both = jnp.concatenate(
        [decay[...] * LOG2E, jnp.broadcast_to(resets[0].astype(F32), (8, BLOCK))], axis=0
    )
    summed = lax.dot_general(
        both, upper, NN, precision=lax.Precision.HIGHEST, preferred_element_type=F32
    )
    cum, count = summed[:HEADS], summed[HEADS : HEADS + 8]
    two = jnp.concatenate([count, count], axis=0)
    opening = jnp.where(two == 0.0, jnp.exp2(cum), 0.0)
    last = jnp.broadcast_to(cum[:, BLOCK - 1 :], (HEADS, BLOCK))
    last_two = jnp.broadcast_to(two[:, BLOCK - 1 :], (HEADS, BLOCK))
    closing = jnp.where(two == last_two, jnp.exp2(last - cum), 0.0)
    table = jnp.concatenate(
        [cum, two, opening, closing, jnp.zeros((64, BLOCK), F32)], axis=0
    )
    rows[...] = table[:32]
    turned = table.T
    cols[...] = turned
    end = jnp.broadcast_to(turned[BLOCK - 1 :], (8, 128))
    ends[0] = end

    @pl.when(b == 0)
    def _():
        gain[...] = end

    @pl.when(b > 0)
    def _():
        gain[...] = gain[...] * end

    masked = jnp.where(valid_rows(fill[b], D), cot[0], jnp.zeros((), BF16))
    up[...] = mm(masked, w_out[...], NT).astype(BF16)


def inside(inner, keys, up, rows, cols, ro, gi, pair):
    at = lax.broadcasted_iota(jnp.int32, (BLOCK, BLOCK), 0)
    to = lax.broadcasted_iota(jnp.int32, (BLOCK, BLOCK), 1)
    linked = (to <= at) & (cols[:, CNT : CNT + 1] == rows[CNT : CNT + 1, :])
    bias = jnp.where(linked, 0.0, FAR)
    k = keys[...]
    scores = mm(k[:, STATE:], k[:, :STATE], NT)
    left = lax.broadcasted_iota(jnp.int32, (BLOCK, 128), 1) < HEAD
    zero = jnp.zeros((), BF16)
    paired = jnp.zeros((BLOCK, BLOCK), F32)
    for q in range(HEADS // 2):
        lanes = slice(128 * q, 128 * q + 128)
        x, u = inner[:, lanes], up[:, lanes]
        readout = grad = None
        for s in range(2):
            h = 2 * q + s
            mine = left if s == 0 else ~left
            xs, us = jnp.where(mine, x, zero), jnp.where(mine, u, zero)
            decays = jnp.exp2(cols[:, h : h + 1] - rows[h : h + 1, :] + bias)
            mixing = (decays * scores).astype(BF16)
            paired = paired + decays * mm(us, x, NT)
            r, g = mm(mixing, xs), mm(mixing, us, TN)
            readout = r if s == 0 else readout + r
            grad = g if s == 0 else grad + g
        ro[:, lanes] = readout.astype(BF16)
        gi[:, lanes] = grad.astype(BF16)
    pair[0] = paired.astype(BF16)


def stage_kernel(count, number, block, source, index, fill, *refs):
    picks = refs[:number]
    w_in, w_bc, up, rows, cols = refs[number : number + 5]
    outs = refs[-10:]
    taken, inner, keys, ro, gi, pair, push_in, push_out, spread_o, spread_c = outs
    i = pl.program_id(0)

    @pl.when(i == 0)
    def _():
        spread_o[...] = spread_matrix(OPEN)
        spread_c[...] = spread_matrix(CLOSE)

    @pl.when(i < count[0])
    def _():
        raw = picks[0][...]
        for n in range(1, number):
            raw = jnp.where(jnp.full((BLOCK, D), source[i], jnp.int32) == n, picks[n][...], raw)
        got = jnp.where(valid_rows(fill[jnp.minimum(block[i], fill.shape[0] - 1)], D), raw, jnp.zeros((), BF16))
        taken[...] = got
        x = mm(got, w_in[...]).astype(BF16)
        k = mm(got, w_bc[...]).astype(BF16)
        inner[...] = x
        keys[...] = k
        parts = split(cols[...])
        opening = mm(parts, spread_o[...])
        closing = mm(parts, spread_c[...])
        into = (closing * x.astype(F32)).astype(BF16)
        out = (opening * up[...].astype(F32)).astype(BF16)
        turned = k.astype(F32).T.astype(BF16)
        push_in[0] = mm(turned[:STATE], into)
        push_out[0] = mm(turned[STATE:], out)
        inside(inner, keys, up, rows, cols, ro, gi, pair)


def local_kernel(push_in, push_out, ends, starts, gains, total, spread_o, state):
    b = pl.program_id(0)

    @pl.when(b == 0)
    def _():
        spread_o[...] = spread_matrix(OPEN)
        state[...] = jnp.zeros_like(state)

    factor = mm(split(ends[0]), spread_o[...])
    before = jnp.where(b == 0, 1.0, state[128:])
    starts[0] = state[:64]
    gains[0] = jnp.concatenate([factor, before], axis=0)
    state[:64] = state[:64] * factor[:1] + push_in[0]
    state[64:128] = state[64:128] + before[:1] * push_out[0]
    state[128:] = before * factor

    @pl.when(b == pl.num_programs(0) - 1)
    def _():
        total[...] = state[:128].astype(BF16)


def scan_kernel(which, terms, gain, entering, forth, wide):
    wide[...] = mm(split(gain[...]), spread_matrix(OPEN))
    shards = terms.shape[0]
    state = jnp.zeros((8, D), F32)
    for t in range(shards):
        forth[t] = state
        state = state * wide[t : t + 1] + terms[t].astype(F32)
    back = jnp.zeros((8, D), F32)
    ahead = jnp.full((8, D), which[0], jnp.int32) < shards // 2
    for t in reversed(range(shards)):
        entering[t] = jnp.where(ahead, forth[t], back).astype(BF16)
        back = back * wide[t : t + 1] + terms[t].astype(F32)


def store_halves(core, acc, keep, give):
    scale = 1.0 / 512.0
    for ref, c in ((keep, core[0]), (give, 1 - core[0])):
        ref[...] = (acc[:, c] * scale).reshape(ref.shape).astype(BF16)


def readout_kernel(core, fill, cot, keys, cols, ro, starts, gains, enter, keep, give, acc, spread_o):
    b = pl.program_id(0)

    @pl.when(b == 0)
    def _():
        spread_o[...] = spread_matrix(OPEN)
        acc[...] = jnp.zeros_like(acc)

    start = (starts[0] + gains[0, 8:9] * enter[:64].astype(F32)).astype(BF16)
    opening = mm(split(cols[...]), spread_o[...])
    readout = (ro[...].astype(F32) + opening * mm(keys[:, STATE:], start)).astype(BF16)
    masked = jnp.where(valid_rows(fill[b], D), cot[0], jnp.zeros((), BF16))
    acc[...] += mm(readout, masked, TN).reshape(acc.shape)

    @pl.when(b == pl.num_programs(0) - 1)
    def _():
        store_halves(core, acc, keep, give)


def gradient_kernel(
    core, taken, inner, up, keys, cols, gi, pair, starts, push_out, gains, enter,
    keep, give, acc, spread_o, spread_c, finish,
):
    step = pl.program_id(0)

    @pl.when(step == 0)
    def _():
        spread_o[...] = spread_matrix(OPEN)
        spread_c[...] = spread_matrix(CLOSE)
        finish[...] = enter[64:].astype(F32)
        acc[...] = jnp.zeros_like(acc)

    factor, before = gains[0, 0:1], gains[0, 8:9]
    start = (starts[0] + before * enter[:64].astype(F32)).astype(BF16)
    end = finish[...].astype(BF16)
    finish[...] = finish[...] * factor + push_out[0]
    parts = split(cols[...])
    opening = mm(parts, spread_o[...])
    closing = mm(parts, spread_c[...])
    k = keys[...]
    write, read = k[:, :STATE], k[:, STATE:]
    grad = (gi[...].astype(F32) + closing * mm(write, end)).astype(BF16)
    into = (closing * inner[...].astype(F32)).astype(BF16)
    out = (opening * up[...].astype(F32)).astype(BF16)
    g = pair[0]
    grad_write = mm(g, read, TN) + mm(into, end, NT)
    grad_read = mm(g, write) + mm(out, start, NT)
    grad_keys = jnp.concatenate([grad_write, grad_read], axis=1).astype(BF16)
    both = jnp.concatenate([grad, grad_keys], axis=1)
    acc[...] += mm(taken[...], both, TN).reshape(acc.shape)

    @pl.when(step == pl.num_programs(0) - 1)
    def _():
        store_halves(core, acc, keep, give)


def ring(axis, by):
    size = lax.axis_size(axis)
    return [(k, (k + by) % size) for k in range(size)]


def meet(part, axis, dim):
    me, size = lax.axis_index(axis), lax.axis_size(axis)
    pick = lambda k: lax.dynamic_index_in_dim(part, (me + k) % size, dim, keepdims=False)
    total = pick(0).astype(F32)
    for k in (1, size - 1, *range(2, size - 1)):
        total = total + lax.ppermute(pick(k), axis, ring(axis, k)).astype(F32)
    return total


def summed(keep, give, cut):
    got = lax.ppermute(give, "c", ring("c", 1))
    half = (keep.astype(F32) + got.astype(F32)).astype(BF16)
    half = half.reshape(*(lax.axis_size(n) for n in ("y", "x", "z")), 8, -1)
    a, b = half[..., :cut], half[..., cut:]
    a, b = meet(a, "x", 1).astype(BF16), meet(b, "y", 0).astype(BF16)
    a, b = meet(a, "y", 0).astype(BF16), meet(b, "x", 0).astype(BF16)
    return meet(jnp.concatenate([a, b], axis=-1), "z", 0)


def on_device(
    replay, block_owner, block_slot, block_fill, log_decay, resets, cotangent, w_in, w_bc, w_out
):
    shards = lax.axis_size(TM)
    core, z = lax.axis_index("c"), lax.axis_index("z")
    my_lane = z * 2 + core
    blocks = block_fill.shape[2]
    steps = blocks * BLOCK
    fill = block_fill[0, 0]
    owner = lax.dynamic_index_in_dim(block_owner[0, :, :, 0], my_lane, 0, keepdims=False)
    slot = lax.dynamic_index_in_dim(block_slot[0], my_lane, 0, keepdims=False)

    mine = replay[0, 0].reshape(BUFCH, BLOCK, D)
    swap = lambda v: lax.ppermute(v, "c", ring("c", 1))
    up_z = lambda v: lax.ppermute(v, "z", ring("z", 1))
    down_z = lambda v: lax.ppermute(v, "z", ring("z", -1))
    below, above = up_z(mine), down_z(mine)
    other = swap(mine)
    away = (owner // 2 - z) % 4
    same = owner % 2 == core
    stage = jnp.where(away == 0, 0, jnp.where(away == 2, 3, jnp.where(same, 1, 2)))
    source = jnp.where(
        away == 0,
        jnp.where(same, 0, 1),
        jnp.where(away == 2, slot // 2 + jnp.where(same, 0, 2), jnp.where(away == 3, 0, 1)),
    )
    index = jnp.where(away == 2, slot % 2, slot)
    ids = jnp.arange(blocks)
    rank = jnp.sum((stage[None] == stage[:, None]) & (ids[None] < ids[:, None]), axis=1)
    counts = jnp.sum(stage[None] == jnp.arange(4)[:, None], axis=1)
    most = 4
    turn = jnp.minimum(jnp.arange(most)[None], counts[:, None] - 1)
    chosen = (stage[None, None] == jnp.arange(4)[:, None, None]) & (rank[None, None] == turn[:, :, None])
    of = lambda v: jnp.sum(jnp.where(chosen, v[None, None], 0), axis=2)
    block = jnp.where(counts[:, None] > 0, of(ids), blocks).astype(jnp.int32)
    source, index = of(source).astype(jnp.int32), of(index).astype(jnp.int32)
    counts = counts.astype(jnp.int32)

    whole = lambda *dims: pl.BlockSpec(dims, lambda b, *_: (0,) * len(dims))
    tall = lambda width: pl.BlockSpec((BLOCK, width), lambda b, *_: (b, 0))
    lead = lambda *dims: pl.BlockSpec((1, *dims), lambda b, *_: (b,) + (0,) * len(dims))
    table_rows = pl.BlockSpec((32, BLOCK), lambda b, *_: (0, b))
    vmem = lambda kind, *dims: pltpu.VMEM(dims, kind)

    up, rows, cols, ends, gain = call(
        upstream_kernel,
        "upstream",
        (
            shape((steps, D), BF16),
            shape((32, steps), F32),
            shape((steps, 128), F32),
            shape((blocks, 8, 128), F32),
            shape((8, 128), F32),
        ),
        pltpu.PrefetchScalarGridSpec(
            num_scalar_prefetch=1,
            grid=(blocks,),
            in_specs=[
                pl.BlockSpec((HEADS, BLOCK), lambda b, *_: (0, b)),
                pl.BlockSpec((1, 1, BLOCK), lambda b, *_: (b, 0, 0)),
                pl.BlockSpec((1, BLOCK, D), lambda b, *_: (0, b, 0)),
                whole(D, D),
            ],
            out_specs=[tall(D), table_rows, tall(128), lead(8, 128), whole(8, 128)],
        ),
        2 * steps * D * D,
        12 << 20,
    )(fill, log_decay[0], resets.reshape(blocks, 1, BLOCK), cotangent, w_out)
    all_gain = lax.all_gather(gain[:1], TM, axis=0, tiled=True)
    up, all_gain = lax.optimization_barrier((up, all_gain))

    room = steps + BLOCK
    made = None
    for s in range(4):
        if s == 0:
            sources = (mine, other)
        elif s == 1:
            below, above, made = lax.optimization_barrier((below, above, made))
            far_low, far_high = up_z(below[:2]), down_z(above[2:])
            sources, later = (below, above), (swap(below), swap(above))
        elif s == 2:
            sources = later
        else:
            far_low, far_high, made = lax.optimization_barrier((far_low, far_high, made))
            sources = (far_low, far_high, swap(far_low), swap(far_high))
        number = len(sources)
        at = lambda i, block, *_: block[i]
        inside_at = lambda i, block, *_: jnp.minimum(block[i], blocks - 1)
        out_rows = lambda width: pl.BlockSpec((BLOCK, width), lambda i, block, *_: (block[i], 0))
        out_lead = lambda *dims: pl.BlockSpec((1, *dims), lambda i, block, *_: (block[i], 0, 0))
        in_rows = lambda width: pl.BlockSpec(
            (BLOCK, width), lambda i, block, *_: (jnp.minimum(block[i], blocks - 1), 0)
        )
        pick = lambda n: pl.BlockSpec(
            (pl.squeezed, BLOCK, D),
            lambda i, block, source, index, *_: (jnp.where(source[i] == n, index[i], 0), 0, 0),
        )
        kept = [] if made is None else list(made)
        body = lambda block, source, index, fill, count, *refs, number=number: stage_kernel(
            count, number, block, source, index, fill, *refs
        )
        made = pl.pallas_call(
            body,
            out_shape=(
                shape((room, D), BF16),
                shape((room, D), BF16),
                shape((room, 128), BF16),
                shape((room, D), BF16),
                shape((room, D), BF16),
                shape((blocks + 1, BLOCK, BLOCK), BF16),
                shape((blocks + 1, STATE, D), F32),
                shape((blocks + 1, STATE, D), F32),
            ),
            grid_spec=pltpu.PrefetchScalarGridSpec(
                num_scalar_prefetch=5,
                grid=(most,),
                in_specs=[pick(n) for n in range(number)]
                + [
                    whole(D, D),
                    whole(D, 128),
                    in_rows(D),
                    pl.BlockSpec((32, BLOCK), lambda i, block, *_: (0, jnp.minimum(block[i], blocks - 1))),
                    in_rows(128),
                ]
                + [pl.BlockSpec(memory_space=pl.ANY)] * len(kept),
                out_specs=[
                    out_rows(D),
                    out_rows(D),
                    out_rows(128),
                    out_rows(D),
                    out_rows(D),
                    out_lead(BLOCK, BLOCK),
                    out_lead(STATE, D),
                    out_lead(STATE, D),
                ],
                scratch_shapes=[vmem(BF16, 256, D), vmem(BF16, 256, D)],
            ),
            input_output_aliases={5 + number + 5 + n: n for n in range(len(kept))},
            name=f"stage_{s}",
            compiler_params=pltpu.CompilerParams(vmem_limit_bytes=VMEM_LIMIT),
            cost_estimate=pl.CostEstimate(
                flops=4 * BLOCK * D * (D + 1024) + 4 * HEADS * 3 * BLOCK**3,
                bytes_accessed=16 << 20,
                transcendentals=0,
            ),
        )(block[s], source[s], index[s], fill, counts[s : s + 1], *sources, w_in, w_bc, up, rows, cols, *kept)
    taken, inner, keys, ro, gi, pair, push_in, push_out = made

    starts, gains, total = call(
        local_kernel,
        "local",
        (shape((blocks, STATE, D), F32), shape((blocks, 16, D), F32), shape((128, D), BF16)),
        pl.GridSpec(
            grid=(blocks,),
            in_specs=[lead(STATE, D), lead(STATE, D), lead(8, 128)],
            out_specs=[lead(STATE, D), lead(16, D), whole(128, D)],
            scratch_shapes=[vmem(BF16, 256, D), vmem(F32, 136, D)],
        ),
        1 << 24,
        7 << 20,
    )(push_in, push_out, ends)

    terms = lax.all_to_all(total.reshape(shards, 8, D), TM, 0, 0)
    entering = call(
        scan_kernel,
        "scan",
        shape((shards, 8, D), BF16),
        pltpu.PrefetchScalarGridSpec(
            num_scalar_prefetch=1,
            grid=(1,),
            in_specs=[whole(shards, 8, D), whole(shards, 128)],
            out_specs=whole(shards, 8, D),
            scratch_shapes=[vmem(F32, shards, 8, D), vmem(F32, shards, D)],
        ),
        1 << 20,
        1 << 20,
    )(lax.axis_index(TM).reshape(1), terms, all_gain)
    enter = lax.all_to_all(entering, TM, 0, 0).reshape(128, D)

    own_core = core.reshape(1)
    keep_out, give_out = call(
        readout_kernel,
        "readout",
        (shape((D // 2, D), BF16), shape((D // 2, D), BF16)),
        pltpu.PrefetchScalarGridSpec(
            num_scalar_prefetch=2,
            grid=(blocks,),
            in_specs=[
                pl.BlockSpec((1, BLOCK, D), lambda b, *_: (0, b, 0)),
                tall(128),
                tall(128),
                tall(D),
                lead(STATE, D),
                lead(16, D),
                whole(128, D),
            ],
            out_specs=[whole(D // 2, D), whole(D // 2, D)],
            scratch_shapes=[vmem(F32, D // 16, 2, 8, D), vmem(BF16, 256, D)],
        ),
        2 * steps * D * (D + 256),
        14 << 20,
    )(own_core, fill, cotangent, keys, cols, ro, starts, gains, enter)

    back = lambda spec: pl.BlockSpec(
        spec.block_shape, lambda s, *refs: spec.index_map(blocks - 1 - s, *refs)
    )
    wide = D + 128
    keep_in, give_in = call(
        gradient_kernel,
        "gradient",
        (shape((D // 2, wide), BF16), shape((D // 2, wide), BF16)),
        pltpu.PrefetchScalarGridSpec(
            num_scalar_prefetch=1,
            grid=(blocks,),
            in_specs=[
                back(s)
                for s in (
                    tall(D),
                    tall(D),
                    tall(D),
                    tall(128),
                    tall(128),
                    tall(D),
                    lead(BLOCK, BLOCK),
                    lead(STATE, D),
                    lead(STATE, D),
                    lead(16, D),
                    whole(128, D),
                )
            ],
            out_specs=[whole(D // 2, wide), whole(D // 2, wide)],
            scratch_shapes=[
                vmem(F32, D // 16, 2, 8, wide),
                vmem(BF16, 256, D),
                vmem(BF16, 256, D),
                vmem(F32, STATE, D),
            ],
        ),
        2 * steps * D * (D + 1024),
        26 << 20,
    )(own_core, taken, inner, up, keys, cols, gi, pair, starts, push_out, gains, enter)

    grad_out = summed(keep_out, give_out, 512)
    grad_in = summed(keep_in, give_in, 640)
    return (grad_in[:, :D], grad_in[:, D:], grad_out)


def solution(mesh):
    torus = Mesh(mesh.devices.reshape(4, 4, 4, 2), ("y", "x", "z", "c"))
    lane = ("z", "c")
    every = TM + lane
    return jax.shard_map(
        on_device,
        mesh=torus,
        in_specs=(
            P(lane, TM, None, None),
            P(TM, None, None, None),
            P(TM, None, None),
            P(lane, TM, None),
            P(lane, None, TM),
            P(lane, TM),
            P(lane, TM, None),
            P(),
            P(),
            P(),
        ),
        out_specs=(P(every, None), P(every, None), P(every, None)),
        check_vma=False,
    )
```

```python
import math

import jax
import jax.numpy as jnp
from jax import lax
from jax.experimental import pallas as pl
from jax.experimental.pallas import tpu as pltpu
from jax.sharding import Mesh
from jax.sharding import PartitionSpec as P

D = 1024
HEAD = 64
HEADS = 16
STATE = 64
BLOCK = 256
BUFCH = 4
TM = ("y", "x")
LOG2E = math.log2(math.e)
FAR = -1e4
F32, BF16 = jnp.float32, jnp.bfloat16
CNT, OPEN, CLOSE = 16, 32, 48
NT = (((1,), (1,)), ((), ()))
TN = (((0,), (0,)), ((), ()))
NN = (((1,), (0,)), ((), ()))
VMEM_LIMIT = 56 * 1024 * 1024


def mm(a, b, dims=NN):
    return lax.dot_general(a, b, dims, preferred_element_type=F32)


def split(x):
    high = x.astype(BF16)
    return jnp.concatenate([high, (x - high.astype(F32)).astype(BF16)], axis=1)


def spread_matrix():
    row = lax.broadcasted_iota(jnp.int32, (2 * 128, D), 0) & 127
    head = lax.broadcasted_iota(jnp.int32, (2 * 128, D), 1) >> 6
    return jnp.where(row == head, 1.0, 0.0).astype(BF16)


def spread(table, base, matrix):
    return mm(split(pltpu.roll(table, 128 - base, 1)), matrix)


def call(kernel, name, out_shape, grid_spec, flops, nbytes):
    return pl.pallas_call(
        kernel,
        out_shape=out_shape,
        grid_spec=grid_spec,
        name=name,
        compiler_params=pltpu.CompilerParams(vmem_limit_bytes=VMEM_LIMIT),
        cost_estimate=pl.CostEstimate(flops=flops, bytes_accessed=nbytes, transcendentals=0),
    )


def shape(dims, kind):
    return jax.ShapeDtypeStruct(dims, kind)


def valid_rows(fill, width):
    return lax.broadcasted_iota(jnp.int32, (BLOCK, width), 0) < fill


def upstream_kernel(fill, decay, resets, cot, w_out, up, rows, cols, ends):
    b = pl.program_id(0)
    upper = lax.broadcasted_iota(jnp.int32, (BLOCK, BLOCK), 0) <= lax.broadcasted_iota(
        jnp.int32, (BLOCK, BLOCK), 1
    )
    upper = jnp.where(upper, 1.0, 0.0)
    both = jnp.concatenate(
        [decay[...] * LOG2E, jnp.broadcast_to(resets[0].astype(F32), (8, BLOCK))], axis=0
    )
    summed = lax.dot_general(
        both, upper, NN, precision=lax.Precision.HIGHEST, preferred_element_type=F32
    )
    cum, count = summed[:HEADS], summed[HEADS : HEADS + 8]
    two = jnp.concatenate([count, count], axis=0)
    opening = jnp.where(two == 0.0, jnp.exp2(cum), 0.0)
    last = jnp.broadcast_to(cum[:, BLOCK - 1 :], (HEADS, BLOCK))
    last_two = jnp.broadcast_to(two[:, BLOCK - 1 :], (HEADS, BLOCK))
    closing = jnp.where(two == last_two, jnp.exp2(last - cum), 0.0)
    table = jnp.concatenate(
        [cum, two, opening, closing, jnp.zeros((64, BLOCK), F32)], axis=0
    )
    rows[...] = table[:32]
    turned = table.T
    cols[...] = turned
    ends[0] = jnp.broadcast_to(turned[BLOCK - 1 :], (8, 128))
    masked = jnp.where(valid_rows(fill[b], D), cot[0], jnp.zeros((), BF16))
    up[...] = mm(masked, w_out[...], NT).astype(BF16)


def inside(inner, keys, up, rows, cols, ro, gi, pair):
    at = lax.broadcasted_iota(jnp.int32, (BLOCK, BLOCK), 0)
    to = lax.broadcasted_iota(jnp.int32, (BLOCK, BLOCK), 1)
    linked = (to <= at) & (cols[:, CNT : CNT + 1] == rows[CNT : CNT + 1, :])
    bias = jnp.where(linked, 0.0, FAR)
    k = keys[...]
    scores = mm(k[:, STATE:], k[:, :STATE], NT)
    left = lax.broadcasted_iota(jnp.int32, (BLOCK, 128), 1) < HEAD
    zero = jnp.zeros((), BF16)
    paired = jnp.zeros((BLOCK, BLOCK), F32)
    for q in range(HEADS // 2):
        lanes = slice(128 * q, 128 * q + 128)
        x, u = inner[:, lanes], up[:, lanes]
        readout = grad = None
        for s in range(2):
            h = 2 * q + s
            mine = left if s == 0 else ~left
            xs, us = jnp.where(mine, x, zero), jnp.where(mine, u, zero)
            decays = jnp.exp2(cols[:, h : h + 1] - rows[h : h + 1, :] + bias)
            mixing = (decays * scores).astype(BF16)
            paired = paired + decays * mm(us, x, NT)
            r, g = mm(mixing, xs), mm(mixing, us, TN)
            readout = r if s == 0 else readout + r
            grad = g if s == 0 else grad + g
        ro[:, lanes] = readout.astype(BF16)
        gi[:, lanes] = grad.astype(BF16)
    pair[0] = paired.astype(BF16)


def stage_kernel(count, number, block, source, index, fill, *refs):
    picks = refs[:number]
    w_in, w_bc, up, rows, cols = refs[number : number + 5]
    outs = refs[-9:]
    taken, inner, keys, ro, gi, pair, push_in, push_out, matrix = outs
    i = pl.program_id(0)

    @pl.when(i == 0)
    def _():
        matrix[...] = spread_matrix()

    @pl.when(i < count[0])
    def _():
        raw = picks[0][...]
        for n in range(1, number):
            raw = jnp.where(jnp.full((BLOCK, D), source[i], jnp.int32) == n, picks[n][...], raw)
        got = jnp.where(valid_rows(fill[jnp.minimum(block[i], fill.shape[0] - 1)], D), raw, jnp.zeros((), BF16))
        taken[...] = got
        x = mm(got, w_in[...]).astype(BF16)
        k = mm(got, w_bc[...]).astype(BF16)
        inner[...] = x
        keys[...] = k
        table = cols[...]
        opening = spread(table, OPEN, matrix[...])
        closing = spread(table, CLOSE, matrix[...])
        into = (closing * x.astype(F32)).astype(BF16)
        out = (opening * up[...].astype(F32)).astype(BF16)
        turned = k.astype(F32).T.astype(BF16)
        push_in[0] = mm(turned[:STATE], into)
        push_out[0] = mm(turned[STATE:], out)
        inside(inner, keys, up, rows, cols, ro, gi, pair)


def local_kernel(push_in, push_out, ends, starts, gains, total, factors, state):
    b = pl.program_id(0)

    @pl.when(b == 0)
    def _():
        table = ends[...].reshape(factors.shape[0], 128)
        factors[...] = spread(table, OPEN, spread_matrix())
        state[...] = jnp.zeros_like(state)

    factor = factors[pl.ds(b * 8, 8)]
    before = jnp.where(b == 0, 1.0, state[128:])
    starts[0] = state[:64]
    gains[0] = jnp.concatenate([factor, before], axis=0)
    state[:64] = state[:64] * factor[:1] + push_in[0]
    state[64:128] = state[64:128] + before[:1] * push_out[0]
    state[128:] = before * factor

    @pl.when(b == pl.num_programs(0) - 1)
    def _():
        gain = state[128:]
        high = gain.astype(BF16).astype(F32)
        top = lax.broadcasted_iota(jnp.int32, gain.shape, 0) == 0
        gain = jnp.where(top, high, gain - high)
        for n in range(total.shape[0]):
            total[n] = jnp.concatenate([state[8 * n : 8 * n + 8], gain], axis=0).astype(BF16)


def scan_kernel(which, terms, entering, forth):
    shards = terms.shape[0]
    part = lambda t: terms[t].astype(F32)
    gain = lambda v: v[8:9] + v[9:10]
    state = jnp.zeros((8, D), F32)
    for t in range(shards):
        forth[t] = state
        v = part(t)
        state = state * gain(v) + v[:8]
    back = jnp.zeros((8, D), F32)
    ahead = jnp.full((8, D), which[0], jnp.int32) < shards // 2
    for t in reversed(range(shards)):
        entering[t] = jnp.where(ahead, forth[t], back).astype(BF16)
        v = part(t)
        back = back * gain(v) + v[:8]


def store_halves(core, acc, keep, give):
    scale = 1.0 / 512.0
    keep[...] = (acc[:, core[0]] * scale).reshape(keep.shape)
    give[...] = (acc[:, 1 - core[0]] * scale).reshape(give.shape).astype(BF16)


def readout_kernel(core, fill, cot, keys, cols, ro, starts, gains, enter, keep, give, acc, left, right, matrix):
    step = pl.program_id(0)

    @pl.when(step == 0)
    def _():
        matrix[...] = spread_matrix()
        acc[...] = jnp.zeros_like(acc)

    for n in range(2):
        at = slice(n * BLOCK, n * BLOCK + BLOCK)
        start = (starts[n] + gains[n, 8:9] * enter[:64].astype(F32)).astype(BF16)
        opening = spread(cols[at], OPEN, matrix[...])
        left[at] = (ro[at].astype(F32) + opening * mm(keys[at, STATE:], start)).astype(BF16)
        right[at] = jnp.where(valid_rows(fill[2 * step + n], D), cot[0, at], jnp.zeros((), BF16))
    acc[...] += mm(left[...], right[...], TN).reshape(acc.shape)

    @pl.when(step == pl.num_programs(0) - 1)
    def _():
        store_halves(core, acc, keep, give)


def gradient_kernel(
    core, taken, inner, up, keys, cols, gi, pair, starts, push_out, gains, enter,
    keep, give, acc, right, finish, matrix,
):
    step = pl.program_id(0)

    @pl.when(step == 0)
    def _():
        matrix[...] = spread_matrix()
        finish[...] = enter[64:].astype(F32)
        acc[...] = jnp.zeros_like(acc)

    for n in (1, 0):
        at = slice(n * BLOCK, n * BLOCK + BLOCK)
        factor, before = gains[n, 0:1], gains[n, 8:9]
        start = (starts[n] + before * enter[:64].astype(F32)).astype(BF16)
        end = finish[...].astype(BF16)
        finish[...] = finish[...] * factor + push_out[n]
        table = cols[at]
        opening = spread(table, OPEN, matrix[...])
        closing = spread(table, CLOSE, matrix[...])
        k = keys[at]
        write, read = k[:, :STATE], k[:, STATE:]
        right[at, :D] = (gi[at].astype(F32) + closing * mm(write, end)).astype(BF16)
        into = (closing * inner[at].astype(F32)).astype(BF16)
        out = (opening * up[at].astype(F32)).astype(BF16)
        g = pair[n]
        grad_write = mm(g, read, TN) + mm(into, end, NT)
        grad_read = mm(g, write) + mm(out, start, NT)
        right[at, D:] = jnp.concatenate([grad_write, grad_read], axis=1).astype(BF16)
    acc[...] += mm(taken[...], right[...], TN).reshape(acc.shape)

    @pl.when(step == pl.num_programs(0) - 1)
    def _():
        store_halves(core, acc, keep, give)


def ring(axis, by):
    size = lax.axis_size(axis)
    return [(k, (k + by) % size) for k in range(size)]


CHIPS = ("y", "x", "z")


def over_chip(keep, give):
    got = lax.ppermute(give, "c", ring("c", 1))
    half = (keep + got.astype(F32)).astype(BF16)
    return half.reshape(lax.axis_size(CHIPS), 8, -1)


def over_chips(half):
    return lax.all_to_all(half, CHIPS, 0, 0).astype(F32).sum(0)


def on_device(
    replay, block_owner, block_slot, block_fill, log_decay, resets, cotangent, w_in, w_bc, w_out
):
    shards = lax.axis_size(TM)
    core, z = lax.axis_index("c"), lax.axis_index("z")
    my_lane = z * 2 + core
    blocks = block_fill.shape[2]
    steps = blocks * BLOCK
    fill = block_fill[0, 0]
    owner = lax.dynamic_index_in_dim(block_owner[0, :, :, 0], my_lane, 0, keepdims=False)
    slot = lax.dynamic_index_in_dim(block_slot[0], my_lane, 0, keepdims=False)

    mine = replay[0, 0].reshape(BUFCH, BLOCK, D)
    swap = lambda v: lax.ppermute(v, "c", ring("c", 1))
    up_z = lambda v: lax.ppermute(v, "z", ring("z", 1))
    down_z = lambda v: lax.ppermute(v, "z", ring("z", -1))
    first, second = mine[:2], mine[2:]
    below_a, above_a = up_z(first), down_z(second)
    other = swap(mine)
    away = (owner // 2 - z) % 4
    same = owner % 2 == core
    low = slot < 2
    stage = jnp.where(away == 0, 0, jnp.where(away == 2, 3, jnp.where((away == 3) == low, 1, 2)))
    side = jnp.where(away == 2, jnp.where(low, 0, 1), jnp.where(away == 3, 0, 1))
    source = jnp.where(away == 0, jnp.where(same, 0, 1), side + jnp.where(same, 0, 2))
    index = jnp.where(away == 0, slot, slot % 2)
    ids = jnp.arange(blocks)
    rank = jnp.sum((stage[None] == stage[:, None]) & (ids[None] < ids[:, None]), axis=1)
    counts = jnp.sum(stage[None] == jnp.arange(4)[:, None], axis=1)
    most = (4, blocks, blocks, 4)
    turn = jnp.minimum(jnp.arange(blocks)[None], counts[:, None] - 1)
    chosen = (stage[None, None] == jnp.arange(4)[:, None, None]) & (rank[None, None] == turn[:, :, None])
    of = lambda v: jnp.sum(jnp.where(chosen, v[None, None], 0), axis=2)
    block = jnp.where(counts[:, None] > 0, of(ids), blocks).astype(jnp.int32)
    source, index = of(source).astype(jnp.int32), of(index).astype(jnp.int32)
    counts = counts.astype(jnp.int32)

    whole = lambda *dims: pl.BlockSpec(dims, lambda b, *_: (0,) * len(dims))
    tall = lambda width: pl.BlockSpec((BLOCK, width), lambda b, *_: (b, 0))
    lead = lambda *dims: pl.BlockSpec((1, *dims), lambda b, *_: (b,) + (0,) * len(dims))
    table_rows = pl.BlockSpec((32, BLOCK), lambda b, *_: (0, b))
    vmem = lambda kind, *dims: pltpu.VMEM(dims, kind)

    up, rows, cols, ends = call(
        upstream_kernel,
        "upstream",
        (
            shape((steps, D), BF16),
            shape((32, steps), F32),
            shape((steps, 128), F32),
            shape((blocks, 8, 128), F32),
        ),
        pltpu.PrefetchScalarGridSpec(
            num_scalar_prefetch=1,
            grid=(blocks,),
            in_specs=[
                pl.BlockSpec((HEADS, BLOCK), lambda b, *_: (0, b)),
                pl.BlockSpec((1, 1, BLOCK), lambda b, *_: (b, 0, 0)),
                pl.BlockSpec((1, BLOCK, D), lambda b, *_: (0, b, 0)),
                whole(D, D),
            ],
            out_specs=[tall(D), table_rows, tall(128), lead(8, 128)],
        ),
        2 * steps * D * D,
        12 << 20,
    )(fill, log_decay[0], resets.reshape(blocks, 1, BLOCK), cotangent, w_out)

    room = steps + BLOCK
    made = None
    for s in range(4):
        if s == 0:
            sources = (mine, other)
        elif s == 1:
            below_a, above_a, second, first, made = lax.optimization_barrier(
                (below_a, above_a, second, first, made)
            )
            below_b, above_b = up_z(second), down_z(first)
            sources = (below_a, above_a, swap(below_a), swap(above_a))
        elif s == 2:
            below_b, above_b, below_a, above_a, made = lax.optimization_barrier(
                (below_b, above_b, below_a, above_a, made)
            )
            far_low, far_high = up_z(below_a), down_z(above_a)
            sources = (below_b, above_b, swap(below_b), swap(above_b))
        else:
            far_low, far_high, made = lax.optimization_barrier((far_low, far_high, made))
            sources = (far_low, far_high, swap(far_low), swap(far_high))
        number = len(sources)
        at = lambda i, block, *_: block[i]
        inside_at = lambda i, block, *_: jnp.minimum(block[i], blocks - 1)
        out_rows = lambda width: pl.BlockSpec((BLOCK, width), lambda i, block, *_: (block[i], 0))
        out_lead = lambda *dims: pl.BlockSpec((1, *dims), lambda i, block, *_: (block[i], 0, 0))
        in_rows = lambda width: pl.BlockSpec(
            (BLOCK, width), lambda i, block, *_: (jnp.minimum(block[i], blocks - 1), 0)
        )
        pick = lambda n: pl.BlockSpec(
            (pl.squeezed, BLOCK, D),
            lambda i, block, source, index, *_: (jnp.where(source[i] == n, index[i], 0), 0, 0),
        )
        kept = [] if made is None else list(made)
        body = lambda block, source, index, fill, count, *refs, number=number: stage_kernel(
            count, number, block, source, index, fill, *refs
        )
        made = pl.pallas_call(
            body,
            out_shape=(
                shape((room, D), BF16),
                shape((room, D), BF16),
                shape((room, 128), BF16),
                shape((room, D), BF16),
                shape((room, D), BF16),
                shape((blocks + 1, BLOCK, BLOCK), BF16),
                shape((blocks + 1, STATE, D), F32),
                shape((blocks + 1, STATE, D), F32),
            ),
            grid_spec=pltpu.PrefetchScalarGridSpec(
                num_scalar_prefetch=5,
                grid=(most[s],),
                in_specs=[pick(n) for n in range(number)]
                + [
                    whole(D, D),
                    whole(D, 128),
                    in_rows(D),
                    pl.BlockSpec((32, BLOCK), lambda i, block, *_: (0, jnp.minimum(block[i], blocks - 1))),
                    in_rows(128),
                ]
                + [pl.BlockSpec(memory_space=pl.ANY)] * len(kept),
                out_specs=[
                    out_rows(D),
                    out_rows(D),
                    out_rows(128),
                    out_rows(D),
                    out_rows(D),
                    out_lead(BLOCK, BLOCK),
                    out_lead(STATE, D),
                    out_lead(STATE, D),
                ],
                scratch_shapes=[vmem(BF16, 256, D)],
            ),
            input_output_aliases={5 + number + 5 + n: n for n in range(len(kept))},
            name=f"stage_{s}",
            compiler_params=pltpu.CompilerParams(vmem_limit_bytes=VMEM_LIMIT),
            cost_estimate=pl.CostEstimate(
                flops=4 * BLOCK * D * (D + 1024) + 4 * HEADS * 3 * BLOCK**3,
                bytes_accessed=16 << 20,
                transcendentals=0,
            ),
        )(block[s], source[s], index[s], fill, counts[s : s + 1], *sources, w_in, w_bc, up, rows, cols, *kept)
    taken, inner, keys, ro, gi, pair, push_in, push_out = made

    starts, gains, total = call(
        local_kernel,
        "local",
        (shape((blocks, STATE, D), F32), shape((blocks, 16, D), F32), shape((shards, 16, D), BF16)),
        pl.GridSpec(
            grid=(blocks,),
            in_specs=[lead(STATE, D), lead(STATE, D), whole(blocks, 8, 128)],
            out_specs=[lead(STATE, D), lead(16, D), whole(shards, 16, D)],
            scratch_shapes=[vmem(F32, blocks * 8, D), vmem(F32, 136, D)],
        ),
        1 << 24,
        7 << 20,
    )(push_in, push_out, ends)

    terms = lax.all_to_all(total, TM, 0, 0)
    entering = call(
        scan_kernel,
        "scan",
        shape((shards, 8, D), BF16),
        pltpu.PrefetchScalarGridSpec(
            num_scalar_prefetch=1,
            grid=(1,),
            in_specs=[whole(shards, 16, D)],
            out_specs=whole(shards, 8, D),
            scratch_shapes=[vmem(F32, shards, 8, D)],
        ),
        1 << 20,
        1 << 20,
    )(lax.axis_index(TM).reshape(1), terms)
    enter = lax.all_to_all(entering, TM, 0, 0).reshape(128, D)

    own_core = core.reshape(1)
    two = lambda width: pl.BlockSpec((2 * BLOCK, width), lambda b, *_: (b, 0))
    pairs = lambda *dims: pl.BlockSpec((2, *dims), lambda b, *_: (b, 0, 0))
    keep_out, give_out = call(
        readout_kernel,
        "readout",
        (shape((D // 2, D), F32), shape((D // 2, D), BF16)),
        pltpu.PrefetchScalarGridSpec(
            num_scalar_prefetch=2,
            grid=(blocks // 2,),
            in_specs=[
                pl.BlockSpec((1, 2 * BLOCK, D), lambda b, *_: (0, b, 0)),
                two(128),
                two(128),
                two(D),
                pairs(STATE, D),
                pairs(16, D),
                whole(128, D),
            ],
            out_specs=[whole(D // 2, D), whole(D // 2, D)],
            scratch_shapes=[
                vmem(F32, D // 16, 2, 8, D),
                vmem(BF16, 2 * BLOCK, D),
                vmem(BF16, 2 * BLOCK, D),
                vmem(BF16, 256, D),
            ],
        ),
        2 * steps * D * (D + 256),
        14 << 20,
    )(own_core, fill, cotangent, keys, cols, ro, starts, gains, enter)

    half_out, enter = lax.optimization_barrier((over_chip(keep_out, give_out), enter))
    back = lambda spec: pl.BlockSpec(
        spec.block_shape, lambda s, *refs: spec.index_map(blocks // 2 - 1 - s, *refs)
    )
    wide = D + 128
    keep_in, give_in = call(
        gradient_kernel,
        "gradient",
        (shape((D // 2, wide), F32), shape((D // 2, wide), BF16)),
        pltpu.PrefetchScalarGridSpec(
            num_scalar_prefetch=1,
            grid=(blocks // 2,),
            in_specs=[
                back(s)
                for s in (
                    two(D),
                    two(D),
                    two(D),
                    two(128),
                    two(128),
                    two(D),
                    pairs(BLOCK, BLOCK),
                    pairs(STATE, D),
                    pairs(STATE, D),
                    pairs(16, D),
                    whole(128, D),
                )
            ],
            out_specs=[whole(D // 2, wide), whole(D // 2, wide)],
            scratch_shapes=[
                vmem(F32, D // 16, 2, 8, wide),
                vmem(BF16, 2 * BLOCK, wide),
                vmem(F32, STATE, D),
                vmem(BF16, 256, D),
            ],
        ),
        2 * steps * D * (D + 1024),
        26 << 20,
    )(own_core, taken, inner, up, keys, cols, gi, pair, starts, push_out, gains, enter)

    grad_out = over_chips(half_out)
    grad_in = over_chips(over_chip(keep_in, give_in))
    return (grad_in[:, :D], grad_in[:, D:], grad_out)


def solution(mesh):
    torus = Mesh(mesh.devices.reshape(4, 4, 4, 2), ("y", "x", "z", "c"))
    lane = ("z", "c")
    every = TM + lane
    return jax.shard_map(
        on_device,
        mesh=torus,
        in_specs=(
            P(lane, TM, None, None),
            P(TM, None, None, None),
            P(TM, None, None),
            P(lane, TM, None),
            P(lane, None, TM),
            P(lane, TM),
            P(lane, TM, None),
            P(),
            P(),
            P(),
        ),
        out_specs=(P(every, None), P(every, None), P(every, None)),
        check_vma=False,
    )
```

```python
import math

import jax
import jax.numpy as jnp
from jax import lax
from jax.experimental import pallas as pl
from jax.experimental.pallas import tpu as pltpu
from jax.sharding import Mesh
from jax.sharding import PartitionSpec as P

D = 1024
HEAD = 64
HEADS = 16
STATE = 64
BLOCK = 256
BUFCH = 4
TM = ("y", "x")
LOG2E = math.log2(math.e)
FAR = -1e4
F32, BF16 = jnp.float32, jnp.bfloat16
CNT, OPEN, CLOSE = 16, 32, 48
NT = (((1,), (1,)), ((), ()))
TN = (((0,), (0,)), ((), ()))
NN = (((1,), (0,)), ((), ()))
VMEM_LIMIT = 56 * 1024 * 1024


def mm(a, b, dims=NN):
    return lax.dot_general(a, b, dims, preferred_element_type=F32)


def split(x):
    high = x.astype(BF16)
    return jnp.concatenate([high, (x - high.astype(F32)).astype(BF16)], axis=1)


def spread_matrix():
    row = lax.broadcasted_iota(jnp.int32, (2 * 128, D), 0) & 127
    head = lax.broadcasted_iota(jnp.int32, (2 * 128, D), 1) >> 6
    return jnp.where(row == head, 1.0, 0.0).astype(BF16)


def spread(table, base, matrix):
    return mm(split(pltpu.roll(table, 128 - base, 1)), matrix)


def call(kernel, name, out_shape, grid_spec, flops, nbytes):
    return pl.pallas_call(
        kernel,
        out_shape=out_shape,
        grid_spec=grid_spec,
        name=name,
        compiler_params=pltpu.CompilerParams(vmem_limit_bytes=VMEM_LIMIT),
        cost_estimate=pl.CostEstimate(flops=flops, bytes_accessed=nbytes, transcendentals=0),
    )


def shape(dims, kind):
    return jax.ShapeDtypeStruct(dims, kind)


def valid_rows(fill, width):
    return lax.broadcasted_iota(jnp.int32, (BLOCK, width), 0) < fill


def upstream_kernel(fill, decay, resets, cot, w_out, up, rows, cols, ends):
    b = pl.program_id(0)
    upper = lax.broadcasted_iota(jnp.int32, (BLOCK, BLOCK), 0) <= lax.broadcasted_iota(
        jnp.int32, (BLOCK, BLOCK), 1
    )
    upper = jnp.where(upper, 1.0, 0.0)
    both = jnp.concatenate(
        [decay[...] * LOG2E, jnp.broadcast_to(resets[0].astype(F32), (8, BLOCK))], axis=0
    )
    summed = lax.dot_general(
        both, upper, NN, precision=lax.Precision.HIGHEST, preferred_element_type=F32
    )
    cum, count = summed[:HEADS], summed[HEADS : HEADS + 8]
    two = jnp.concatenate([count, count], axis=0)
    opening = jnp.where(two == 0.0, jnp.exp2(cum), 0.0)
    last = jnp.broadcast_to(cum[:, BLOCK - 1 :], (HEADS, BLOCK))
    last_two = jnp.broadcast_to(two[:, BLOCK - 1 :], (HEADS, BLOCK))
    closing = jnp.where(two == last_two, jnp.exp2(last - cum), 0.0)
    table = jnp.concatenate(
        [cum, two, opening, closing, jnp.zeros((64, BLOCK), F32)], axis=0
    )
    rows[...] = table[:32]
    turned = table.T
    cols[...] = turned
    ends[0] = jnp.broadcast_to(turned[BLOCK - 1 :], (8, 128))
    masked = jnp.where(valid_rows(fill[b], D), cot[0], jnp.zeros((), BF16))
    up[...] = mm(masked, w_out[...], NT).astype(BF16)


def inside(inner, keys, up, rows, cols, ro, gi, pair):
    at = lax.broadcasted_iota(jnp.int32, (BLOCK, BLOCK), 0)
    to = lax.broadcasted_iota(jnp.int32, (BLOCK, BLOCK), 1)
    linked = (to <= at) & (cols[:, CNT : CNT + 1] == rows[CNT : CNT + 1, :])
    bias = jnp.where(linked, 0.0, FAR)
    k = keys[...]
    scores = mm(k[:, STATE:], k[:, :STATE], NT)
    left = lax.broadcasted_iota(jnp.int32, (BLOCK, 128), 1) < HEAD
    zero = jnp.zeros((), BF16)
    paired = jnp.zeros((BLOCK, BLOCK), F32)
    for q in range(HEADS // 2):
        lanes = slice(128 * q, 128 * q + 128)
        x, u = inner[:, lanes], up[:, lanes]
        readout = grad = None
        for s in range(2):
            h = 2 * q + s
            mine = left if s == 0 else ~left
            xs, us = jnp.where(mine, x, zero), jnp.where(mine, u, zero)
            decays = jnp.exp2(cols[:, h : h + 1] - rows[h : h + 1, :] + bias)
            mixing = (decays * scores).astype(BF16)
            paired = paired + decays * mm(us, x, NT)
            r, g = mm(mixing, xs), mm(mixing, us, TN)
            readout = r if s == 0 else readout + r
            grad = g if s == 0 else grad + g
        ro[:, lanes] = readout.astype(BF16)
        gi[:, lanes] = grad.astype(BF16)
    pair[0] = paired.astype(BF16)


def stage_kernel(count, number, block, source, index, fill, *refs):
    picks = refs[:number]
    w_in, w_bc, up, rows, cols = refs[number : number + 5]
    outs = refs[-9:]
    taken, inner, keys, ro, gi, pair, push_in, push_out, matrix = outs
    i = pl.program_id(0)

    @pl.when(i == 0)
    def _():
        matrix[...] = spread_matrix()

    @pl.when(i < count[0])
    def _():
        raw = picks[0][...]
        for n in range(1, number):
            raw = jnp.where(jnp.full((BLOCK, D), source[i], jnp.int32) == n, picks[n][...], raw)
        got = jnp.where(valid_rows(fill[jnp.minimum(block[i], fill.shape[0] - 1)], D), raw, jnp.zeros((), BF16))
        taken[...] = got
        x = mm(got, w_in[...]).astype(BF16)
        k = mm(got, w_bc[...]).astype(BF16)
        inner[...] = x
        keys[...] = k
        table = cols[...]
        opening = spread(table, OPEN, matrix[...])
        closing = spread(table, CLOSE, matrix[...])
        into = (closing * x.astype(F32)).astype(BF16)
        out = (opening * up[...].astype(F32)).astype(BF16)
        turned = k.astype(F32).T.astype(BF16)
        push_in[0] = mm(turned[:STATE], into)
        push_out[0] = mm(turned[STATE:], out)
        inside(inner, keys, up, rows, cols, ro, gi, pair)


def local_kernel(push_in, push_out, ends, starts, gains, total, factors, state):
    b = pl.program_id(0)

    @pl.when(b == 0)
    def _():
        table = ends[...].reshape(factors.shape[0], 128)
        factors[...] = spread(table, OPEN, spread_matrix())
        state[:128] = jnp.zeros((128, D), F32)
        state[128:] = jnp.ones((8, D), F32)

    each = starts.shape[0]
    for n in range(each):
        factor = factors[pl.ds((b * each + n) * 8, 8)]
        before = state[128:]
        starts[n] = state[:64]
        gains[n] = jnp.concatenate([factor, before], axis=0)
        state[:64] = state[:64] * factor[:1] + push_in[n]
        state[64:128] = state[64:128] + before[:1] * push_out[n]
        state[128:] = before * factor

    @pl.when(b == pl.num_programs(0) - 1)
    def _():
        gain = state[128:]
        high = gain.astype(BF16).astype(F32)
        top = lax.broadcasted_iota(jnp.int32, gain.shape, 0) == 0
        gain = jnp.where(top, high, gain - high)
        for n in range(total.shape[0]):
            total[n] = jnp.concatenate([state[8 * n : 8 * n + 8], gain], axis=0).astype(BF16)


def scan_kernel(which, terms, entering, forth):
    shards = terms.shape[0]
    part = lambda t: terms[t].astype(F32)
    gain = lambda v: v[8:9] + v[9:10]
    state = jnp.zeros((8, D), F32)
    for t in range(shards):
        forth[t] = state
        v = part(t)
        state = state * gain(v) + v[:8]
    back = jnp.zeros((8, D), F32)
    ahead = jnp.full((8, D), which[0], jnp.int32) < shards // 2
    for t in reversed(range(shards)):
        entering[t] = jnp.where(ahead, forth[t], back).astype(BF16)
        v = part(t)
        back = back * gain(v) + v[:8]


def store_halves(core, acc, keep, give):
    scale = 1.0 / 512.0
    keep[...] = (acc[:, core[0]] * scale).reshape(keep.shape)
    give[...] = (acc[:, 1 - core[0]] * scale).reshape(give.shape).astype(BF16)


def readout_kernel(core, fill, cot, keys, cols, ro, starts, gains, enter, keep, give, acc, left, right, matrix):
    step = pl.program_id(0)

    @pl.when(step == 0)
    def _():
        matrix[...] = spread_matrix()
        acc[...] = jnp.zeros_like(acc)

    for n in range(2):
        at = slice(n * BLOCK, n * BLOCK + BLOCK)
        start = (starts[n] + gains[n, 8:9] * enter[:64].astype(F32)).astype(BF16)
        opening = spread(cols[at], OPEN, matrix[...])
        left[at] = (ro[at].astype(F32) + opening * mm(keys[at, STATE:], start)).astype(BF16)
        right[at] = jnp.where(valid_rows(fill[2 * step + n], D), cot[0, at], jnp.zeros((), BF16))
    acc[...] += mm(left[...], right[...], TN).reshape(acc.shape)

    @pl.when(step == pl.num_programs(0) - 1)
    def _():
        store_halves(core, acc, keep, give)


def gradient_kernel(
    core, taken, inner, up, keys, cols, gi, pair, starts, push_out, gains, enter,
    keep, give, acc, right, finish, matrix,
):
    step = pl.program_id(0)

    @pl.when(step == 0)
    def _():
        matrix[...] = spread_matrix()
        finish[...] = enter[64:].astype(F32)
        acc[...] = jnp.zeros_like(acc)

    for n in (1, 0):
        at = slice(n * BLOCK, n * BLOCK + BLOCK)
        factor, before = gains[n, 0:1], gains[n, 8:9]
        start = (starts[n] + before * enter[:64].astype(F32)).astype(BF16)
        end = finish[...].astype(BF16)
        finish[...] = finish[...] * factor + push_out[n]
        table = cols[at]
        opening = spread(table, OPEN, matrix[...])
        closing = spread(table, CLOSE, matrix[...])
        k = keys[at]
        write, read = k[:, :STATE], k[:, STATE:]
        right[at, :D] = (gi[at].astype(F32) + closing * mm(write, end)).astype(BF16)
        into = (closing * inner[at].astype(F32)).astype(BF16)
        out = (opening * up[at].astype(F32)).astype(BF16)
        g = pair[n]
        grad_write = mm(g, read, TN) + mm(into, end, NT)
        grad_read = mm(g, write) + mm(out, start, NT)
        right[at, D:] = jnp.concatenate([grad_write, grad_read], axis=1).astype(BF16)
    acc[...] += mm(taken[...], right[...], TN).reshape(acc.shape)

    @pl.when(step == pl.num_programs(0) - 1)
    def _():
        store_halves(core, acc, keep, give)


def ring(axis, by):
    size = lax.axis_size(axis)
    return [(k, (k + by) % size) for k in range(size)]


CHIPS = ("y", "x", "z")


def over_chip(keep, give):
    got = lax.ppermute(give, "c", ring("c", 1))
    half = (keep + got.astype(F32)).astype(BF16)
    return half.reshape(lax.axis_size(CHIPS), 8, -1)


def over_chips(half):
    return lax.all_to_all(half, CHIPS, 0, 0).astype(F32).sum(0)


def on_device(
    replay, block_owner, block_slot, block_fill, log_decay, resets, cotangent, w_in, w_bc, w_out
):
    shards = lax.axis_size(TM)
    core, z = lax.axis_index("c"), lax.axis_index("z")
    my_lane = z * 2 + core
    blocks = block_fill.shape[2]
    steps = blocks * BLOCK
    fill = block_fill[0, 0]
    owner = lax.dynamic_index_in_dim(block_owner[0, :, :, 0], my_lane, 0, keepdims=False)
    slot = lax.dynamic_index_in_dim(block_slot[0], my_lane, 0, keepdims=False)

    mine = replay[0, 0].reshape(BUFCH, BLOCK, D)
    swap = lambda v: lax.ppermute(v, "c", ring("c", 1))
    up_z = lambda v: lax.ppermute(v, "z", ring("z", 1))
    down_z = lambda v: lax.ppermute(v, "z", ring("z", -1))
    first, second = mine[:2], mine[2:]
    below_a, above_a = up_z(first), down_z(second)
    other = swap(mine)
    away = (owner // 2 - z) % 4
    same = owner % 2 == core
    low = slot < 2
    stage = jnp.where(away == 0, 0, jnp.where(away == 2, 3, jnp.where((away == 3) == low, 1, 2)))
    side = jnp.where(away == 2, jnp.where(low, 0, 1), jnp.where(away == 3, 0, 1))
    source = jnp.where(away == 0, jnp.where(same, 0, 1), side + jnp.where(same, 0, 2))
    index = jnp.where(away == 0, slot, slot % 2)
    ids = jnp.arange(blocks)
    rank = jnp.sum((stage[None] == stage[:, None]) & (ids[None] < ids[:, None]), axis=1)
    counts = jnp.sum(stage[None] == jnp.arange(4)[:, None], axis=1)
    most = (4, blocks, blocks, 4)
    turn = jnp.minimum(jnp.arange(blocks)[None], counts[:, None] - 1)
    chosen = (stage[None, None] == jnp.arange(4)[:, None, None]) & (rank[None, None] == turn[:, :, None])
    of = lambda v: jnp.sum(jnp.where(chosen, v[None, None], 0), axis=2)
    block = jnp.where(counts[:, None] > 0, of(ids), blocks).astype(jnp.int32)
    source, index = of(source).astype(jnp.int32), of(index).astype(jnp.int32)
    counts = counts.astype(jnp.int32)

    whole = lambda *dims: pl.BlockSpec(dims, lambda b, *_: (0,) * len(dims))
    tall = lambda width: pl.BlockSpec((BLOCK, width), lambda b, *_: (b, 0))
    lead = lambda *dims: pl.BlockSpec((1, *dims), lambda b, *_: (b,) + (0,) * len(dims))
    table_rows = pl.BlockSpec((32, BLOCK), lambda b, *_: (0, b))
    vmem = lambda kind, *dims: pltpu.VMEM(dims, kind)

    up, rows, cols, ends = call(
        upstream_kernel,
        "upstream",
        (
            shape((steps, D), BF16),
            shape((32, steps), F32),
            shape((steps, 128), F32),
            shape((blocks, 8, 128), F32),
        ),
        pltpu.PrefetchScalarGridSpec(
            num_scalar_prefetch=1,
            grid=(blocks,),
            in_specs=[
                pl.BlockSpec((HEADS, BLOCK), lambda b, *_: (0, b)),
                pl.BlockSpec((1, 1, BLOCK), lambda b, *_: (b, 0, 0)),
                pl.BlockSpec((1, BLOCK, D), lambda b, *_: (0, b, 0)),
                whole(D, D),
            ],
            out_specs=[tall(D), table_rows, tall(128), lead(8, 128)],
        ),
        2 * steps * D * D,
        12 << 20,
    )(fill, log_decay[0], resets.reshape(blocks, 1, BLOCK), cotangent, w_out)

    room = steps + BLOCK
    made = None
    for s in range(4):
        if s == 0:
            below_a, above_a, second, first, up = lax.optimization_barrier(
                (below_a, above_a, second, first, up)
            )
            below_b, above_b = up_z(second), down_z(first)
            sources, later = (mine, other), (below_a, above_a, swap(below_a), swap(above_a))
        elif s == 1:
            sources = later
        elif s == 2:
            below_b, above_b, below_a, above_a, made = lax.optimization_barrier(
                (below_b, above_b, below_a, above_a, made)
            )
            far_low, far_high = up_z(below_a), down_z(above_a)
            sources = (below_b, above_b, swap(below_b), swap(above_b))
        else:
            far_low, far_high, made = lax.optimization_barrier((far_low, far_high, made))
            sources = (far_low, far_high, swap(far_low), swap(far_high))
        number = len(sources)
        at = lambda i, block, *_: block[i]
        inside_at = lambda i, block, *_: jnp.minimum(block[i], blocks - 1)
        out_rows = lambda width: pl.BlockSpec((BLOCK, width), lambda i, block, *_: (block[i], 0))
        out_lead = lambda *dims: pl.BlockSpec((1, *dims), lambda i, block, *_: (block[i], 0, 0))
        in_rows = lambda width: pl.BlockSpec(
            (BLOCK, width), lambda i, block, *_: (jnp.minimum(block[i], blocks - 1), 0)
        )
        pick = lambda n: pl.BlockSpec(
            (pl.squeezed, BLOCK, D),
            lambda i, block, source, index, *_: (jnp.where(source[i] == n, index[i], 0), 0, 0),
        )
        kept = [] if made is None else list(made)
        body = lambda block, source, index, fill, count, *refs, number=number: stage_kernel(
            count, number, block, source, index, fill, *refs
        )
        made = pl.pallas_call(
            body,
            out_shape=(
                shape((room, D), BF16),
                shape((room, D), BF16),
                shape((room, 128), BF16),
                shape((room, D), BF16),
                shape((room, D), BF16),
                shape((blocks + 1, BLOCK, BLOCK), BF16),
                shape((blocks + 1, STATE, D), F32),
                shape((blocks + 1, STATE, D), F32),
            ),
            grid_spec=pltpu.PrefetchScalarGridSpec(
                num_scalar_prefetch=5,
                grid=(most[s],),
                in_specs=[pick(n) for n in range(number)]
                + [
                    whole(D, D),
                    whole(D, 128),
                    in_rows(D),
                    pl.BlockSpec((32, BLOCK), lambda i, block, *_: (0, jnp.minimum(block[i], blocks - 1))),
                    in_rows(128),
                ]
                + [pl.BlockSpec(memory_space=pl.ANY)] * len(kept),
                out_specs=[
                    out_rows(D),
                    out_rows(D),
                    out_rows(128),
                    out_rows(D),
                    out_rows(D),
                    out_lead(BLOCK, BLOCK),
                    out_lead(STATE, D),
                    out_lead(STATE, D),
                ],
                scratch_shapes=[vmem(BF16, 256, D)],
            ),
            input_output_aliases={5 + number + 5 + n: n for n in range(len(kept))},
            name=f"stage_{s}",
            compiler_params=pltpu.CompilerParams(vmem_limit_bytes=VMEM_LIMIT),
            cost_estimate=pl.CostEstimate(
                flops=4 * BLOCK * D * (D + 1024) + 4 * HEADS * 3 * BLOCK**3,
                bytes_accessed=16 << 20,
                transcendentals=0,
            ),
        )(block[s], source[s], index[s], fill, counts[s : s + 1], *sources, w_in, w_bc, up, rows, cols, *kept)
    taken, inner, keys, ro, gi, pair, push_in, push_out = made

    some = lambda *dims: pl.BlockSpec((blocks // 2, *dims), lambda b, *_: (b, 0, 0))
    starts, gains, total = call(
        local_kernel,
        "local",
        (shape((blocks, STATE, D), F32), shape((blocks, 16, D), F32), shape((shards, 16, D), BF16)),
        pl.GridSpec(
            grid=(2,),
            in_specs=[some(STATE, D), some(STATE, D), whole(blocks, 8, 128)],
            out_specs=[some(STATE, D), some(16, D), whole(shards, 16, D)],
            scratch_shapes=[vmem(F32, blocks * 8, D), vmem(F32, 136, D)],
        ),
        1 << 24,
        7 << 20,
    )(push_in, push_out, ends)

    terms = lax.all_to_all(total, TM, 0, 0)
    entering = call(
        scan_kernel,
        "scan",
        shape((shards, 8, D), BF16),
        pltpu.PrefetchScalarGridSpec(
            num_scalar_prefetch=1,
            grid=(1,),
            in_specs=[whole(shards, 16, D)],
            out_specs=whole(shards, 8, D),
            scratch_shapes=[vmem(F32, shards, 8, D)],
        ),
        1 << 20,
        1 << 20,
    )(lax.axis_index(TM).reshape(1), terms)
    enter = lax.all_to_all(entering, TM, 0, 0).reshape(128, D)

    own_core = core.reshape(1)
    two = lambda width: pl.BlockSpec((2 * BLOCK, width), lambda b, *_: (b, 0))
    pairs = lambda *dims: pl.BlockSpec((2, *dims), lambda b, *_: (b, 0, 0))
    keep_out, give_out = call(
        readout_kernel,
        "readout",
        (shape((D // 2, D), F32), shape((D // 2, D), BF16)),
        pltpu.PrefetchScalarGridSpec(
            num_scalar_prefetch=2,
            grid=(blocks // 2,),
            in_specs=[
                pl.BlockSpec((1, 2 * BLOCK, D), lambda b, *_: (0, b, 0)),
                two(128),
                two(128),
                two(D),
                pairs(STATE, D),
                pairs(16, D),
                whole(128, D),
            ],
            out_specs=[whole(D // 2, D), whole(D // 2, D)],
            scratch_shapes=[
                vmem(F32, D // 16, 2, 8, D),
                vmem(BF16, 2 * BLOCK, D),
                vmem(BF16, 2 * BLOCK, D),
                vmem(BF16, 256, D),
            ],
        ),
        2 * steps * D * (D + 256),
        14 << 20,
    )(own_core, fill, cotangent, keys, cols, ro, starts, gains, enter)

    half_out, enter = lax.optimization_barrier((over_chip(keep_out, give_out), enter))
    back = lambda spec: pl.BlockSpec(
        spec.block_shape, lambda s, *refs: spec.index_map(blocks // 2 - 1 - s, *refs)
    )
    wide = D + 128
    keep_in, give_in = call(
        gradient_kernel,
        "gradient",
        (shape((D // 2, wide), F32), shape((D // 2, wide), BF16)),
        pltpu.PrefetchScalarGridSpec(
            num_scalar_prefetch=1,
            grid=(blocks // 2,),
            in_specs=[
                back(s)
                for s in (
                    two(D),
                    two(D),
                    two(D),
                    two(128),
                    two(128),
                    two(D),
                    pairs(BLOCK, BLOCK),
                    pairs(STATE, D),
                    pairs(STATE, D),
                    pairs(16, D),
                    whole(128, D),
                )
            ],
            out_specs=[whole(D // 2, wide), whole(D // 2, wide)],
            scratch_shapes=[
                vmem(F32, D // 16, 2, 8, wide),
                vmem(BF16, 2 * BLOCK, wide),
                vmem(F32, STATE, D),
                vmem(BF16, 256, D),
            ],
        ),
        2 * steps * D * (D + 1024),
        26 << 20,
    )(own_core, taken, inner, up, keys, cols, gi, pair, starts, push_out, gains, enter)

    got_out = lax.all_to_all(half_out, CHIPS, 0, 0)
    got_out, keep_in, give_in = lax.optimization_barrier((got_out, keep_in, give_in))
    grad_out = got_out.astype(F32).sum(0)
    grad_in = over_chips(over_chip(keep_in, give_in))
    return (grad_in[:, :D], grad_in[:, D:], grad_out)


def solution(mesh):
    torus = Mesh(mesh.devices.reshape(4, 4, 4, 2), ("y", "x", "z", "c"))
    lane = ("z", "c")
    every = TM + lane
    return jax.shard_map(
        on_device,
        mesh=torus,
        in_specs=(
            P(lane, TM, None, None),
            P(TM, None, None, None),
            P(TM, None, None),
            P(lane, TM, None),
            P(lane, None, TM),
            P(lane, TM),
            P(lane, TM, None),
            P(),
            P(),
            P(),
        ),
        out_specs=(P(every, None), P(every, None), P(every, None)),
        check_vma=False,
    )
```

```python
import math

import jax
import jax.numpy as jnp
from jax import lax
from jax.experimental import pallas as pl
from jax.experimental.pallas import tpu as pltpu
from jax.sharding import Mesh
from jax.sharding import PartitionSpec as P

D = 1024
HEAD = 64
HEADS = 16
STATE = 64
BLOCK = 256
BUFCH = 4
TM = ("y", "x")
LOG2E = math.log2(math.e)
FAR = -1e4
F32, BF16 = jnp.float32, jnp.bfloat16
CNT, OPEN, CLOSE = 16, 32, 48
NT = (((1,), (1,)), ((), ()))
TN = (((0,), (0,)), ((), ()))
NN = (((1,), (0,)), ((), ()))
VMEM_LIMIT = 56 * 1024 * 1024


def mm(a, b, dims=NN):
    return lax.dot_general(a, b, dims, preferred_element_type=F32)


def split(x):
    high = x.astype(BF16)
    return jnp.concatenate([high, (x - high.astype(F32)).astype(BF16)], axis=1)


def spread_matrix():
    row = lax.broadcasted_iota(jnp.int32, (2 * 128, D), 0) & 127
    head = lax.broadcasted_iota(jnp.int32, (2 * 128, D), 1) >> 6
    return jnp.where(row == head, 1.0, 0.0).astype(BF16)


def spread(table, base, matrix):
    return mm(split(pltpu.roll(table, 128 - base, 1)), matrix)


def call(kernel, name, out_shape, grid_spec, flops, nbytes):
    return pl.pallas_call(
        kernel,
        out_shape=out_shape,
        grid_spec=grid_spec,
        name=name,
        compiler_params=pltpu.CompilerParams(vmem_limit_bytes=VMEM_LIMIT),
        cost_estimate=pl.CostEstimate(flops=flops, bytes_accessed=nbytes, transcendentals=0),
    )


def shape(dims, kind):
    return jax.ShapeDtypeStruct(dims, kind)


def valid_rows(fill, width):
    return lax.broadcasted_iota(jnp.int32, (BLOCK, width), 0) < fill


def upstream_kernel(fill, decay, resets, cot, w_out, up, rows, cols, ends):
    b = pl.program_id(0)
    upper = lax.broadcasted_iota(jnp.int32, (BLOCK, BLOCK), 0) <= lax.broadcasted_iota(
        jnp.int32, (BLOCK, BLOCK), 1
    )
    upper = jnp.where(upper, 1.0, 0.0)
    both = jnp.concatenate(
        [decay[...] * LOG2E, jnp.broadcast_to(resets[0].astype(F32), (8, BLOCK))], axis=0
    )
    summed = lax.dot_general(
        both, upper, NN, precision=lax.Precision.HIGHEST, preferred_element_type=F32
    )
    cum, count = summed[:HEADS], summed[HEADS : HEADS + 8]
    two = jnp.concatenate([count, count], axis=0)
    opening = jnp.where(two == 0.0, jnp.exp2(cum), 0.0)
    last = jnp.broadcast_to(cum[:, BLOCK - 1 :], (HEADS, BLOCK))
    last_two = jnp.broadcast_to(two[:, BLOCK - 1 :], (HEADS, BLOCK))
    closing = jnp.where(two == last_two, jnp.exp2(last - cum), 0.0)
    table = jnp.concatenate(
        [cum, two, opening, closing, jnp.zeros((64, BLOCK), F32)], axis=0
    )
    rows[...] = table[:32]
    turned = table.T
    cols[...] = turned
    ends[0] = jnp.broadcast_to(turned[BLOCK - 1 :], (8, 128))
    masked = jnp.where(valid_rows(fill[b], D), cot[0], jnp.zeros((), BF16))
    up[...] = mm(masked, w_out[...], NT).astype(BF16)


def inside(inner, keys, up, rows, cols, ro, gi, pair):
    half = BLOCK // 2
    at = lax.broadcasted_iota(jnp.int32, (BLOCK, BLOCK), 0)
    to = lax.broadcasted_iota(jnp.int32, (BLOCK, BLOCK), 1)
    linked = (to <= at) & (cols[:, CNT : CNT + 1] == rows[CNT : CNT + 1, :])
    bias = jnp.where(linked, 0.0, FAR)
    k = keys[...]
    scores = mm(k[:, STATE:], k[:, :STATE], NT)
    bias_a, bias_b = bias[:half, :half], bias[half:]
    scores_a, scores_b = scores[:half, :half], scores[half:]
    left = lax.broadcasted_iota(jnp.int32, (BLOCK, 128), 1) < HEAD
    zero = jnp.zeros((), BF16)
    turned = up[...].T
    paired_a, paired_b = jnp.zeros((half, half), F32), jnp.zeros((half, BLOCK), F32)
    for q in range(HEADS // 2):
        lanes = slice(128 * q, 128 * q + 128)
        x, u = inner[:, lanes], up[:, lanes]
        grads = []
        for s in range(2):
            h = 2 * q + s
            mine = left if s == 0 else ~left
            xs, us = jnp.where(mine, x, zero), jnp.where(mine, u, zero)
            decays_a = jnp.exp2(cols[:half, h : h + 1] - rows[h : h + 1, :half] + bias_a)
            decays_b = jnp.exp2(cols[half:, h : h + 1] - rows[h : h + 1, :] + bias_b)
            mixing_a, mixing_b = (decays_a * scores_a).astype(BF16), (decays_b * scores_b).astype(BF16)
            paired_a = paired_a + decays_a * mm(us[:half], x[:half], NT)
            paired_b = paired_b + decays_b * mm(us[half:], x, NT)
            a, b = mm(mixing_a, xs[:half]), mm(mixing_b, xs)
            readout_a, readout_b = (a, b) if s == 0 else (readout_a + a, readout_b + b)
            head = turned[HEAD * h : HEAD * h + HEAD]
            g = mm(head[:, half:], mixing_b)
            grads.append(jnp.concatenate([g[:, :half] + mm(head[:, :half], mixing_a), g[:, half:]], axis=1))
        ro[:half, lanes] = readout_a.astype(BF16)
        ro[half:, lanes] = readout_b.astype(BF16)
        gi[:, lanes] = jnp.concatenate(grads, axis=0).astype(BF16).T
    pair[0, :half, :half] = paired_a.astype(BF16)
    pair[0, :half, half:] = jnp.zeros((half, half), BF16)
    pair[0, half:] = paired_b.astype(BF16)


def stage_kernel(count, number, block, source, index, fill, *refs):
    picks = refs[:number]
    w_in, w_bc, up, rows, cols = refs[number : number + 5]
    outs = refs[-9:]
    taken, inner, keys, ro, gi, pair, push_in, push_out, matrix = outs
    i = pl.program_id(0)

    @pl.when(i == 0)
    def _():
        matrix[...] = spread_matrix()

    @pl.when(i < count[0])
    def _():
        valid = valid_rows(fill[jnp.minimum(block[i], fill.shape[0] - 1)], D)
        for n in range(number):

            @pl.when(source[i] == n)
            def _(n=n):
                taken[...] = jnp.where(valid, picks[n][...], jnp.zeros((), BF16))

        got = taken[...]
        x = mm(got, w_in[...]).astype(BF16)
        k = mm(got, w_bc[...]).astype(BF16)
        inner[...] = x
        keys[...] = k
        table = cols[...]
        opening = spread(table, OPEN, matrix[...])
        closing = spread(table, CLOSE, matrix[...])
        into = (closing * x.astype(F32)).astype(BF16)
        out = (opening * up[...].astype(F32)).astype(BF16)
        turned = k.astype(F32).T.astype(BF16)
        push_in[0] = mm(turned[:STATE], into)
        push_out[0] = mm(turned[STATE:], out)
        inside(inner, keys, up, rows, cols, ro, gi, pair)


def local_kernel(push_in, push_out, ends, starts, gains, total, factors, state):
    b = pl.program_id(0)

    @pl.when(b == 0)
    def _():
        table = ends[...].reshape(factors.shape[0], 128)
        factors[...] = spread(table, OPEN, spread_matrix())
        state[:128] = jnp.zeros((128, D), F32)
        state[128:] = jnp.ones((8, D), F32)

    each = starts.shape[0]
    for n in range(each):
        factor = factors[pl.ds((b * each + n) * 8, 8)]
        before = state[128:]
        starts[n] = state[:64]
        gains[n] = jnp.concatenate([factor, before], axis=0)
        state[:64] = state[:64] * factor[:1] + push_in[n]
        state[64:128] = state[64:128] + before[:1] * push_out[n]
        state[128:] = before * factor

    @pl.when(b == pl.num_programs(0) - 1)
    def _():
        gain = state[128:]
        high = gain.astype(BF16).astype(F32)
        top = lax.broadcasted_iota(jnp.int32, gain.shape, 0) == 0
        gain = jnp.where(top, high, gain - high)
        for n in range(total.shape[0]):
            total[n] = jnp.concatenate([state[8 * n : 8 * n + 8], gain], axis=0).astype(BF16)


def scan_kernel(which, terms, entering, forth):
    shards = terms.shape[0]
    part = lambda t: terms[t].astype(F32)
    gain = lambda v: v[8:9] + v[9:10]
    state = jnp.zeros((8, D), F32)
    for t in range(shards):
        forth[t] = state
        v = part(t)
        state = state * gain(v) + v[:8]
    back = jnp.zeros((8, D), F32)
    ahead = jnp.full((8, D), which[0], jnp.int32) < shards // 2
    for t in reversed(range(shards)):
        entering[t] = jnp.where(ahead, forth[t], back).astype(BF16)
        v = part(t)
        back = back * gain(v) + v[:8]


def store_halves(core, acc, keep, give):
    scale = 1.0 / 512.0
    keep[...] = (acc[:, core[0]] * scale).reshape(keep.shape)
    give[...] = (acc[:, 1 - core[0]] * scale).reshape(give.shape).astype(BF16)


def gradient_kernel(
    core, fill, cot, taken, inner, up, keys, cols, ro, gi, pair, starts, push_out, gains, enter,
    keep, give, acc_in, acc_out, left, right, masked, finish, matrix,
):
    step = pl.program_id(0)
    last = pl.num_programs(0) - 1

    @pl.when(step == 0)
    def _():
        matrix[...] = spread_matrix()
        finish[...] = enter[64:].astype(F32)
        acc_in[...] = jnp.zeros_like(acc_in)
        acc_out[...] = jnp.zeros_like(acc_out)

    for n in (1, 0):
        at = slice(n * BLOCK, n * BLOCK + BLOCK)
        factor, before = gains[n, 0:1], gains[n, 8:9]
        start = (starts[n] + before * enter[:64].astype(F32)).astype(BF16)
        end = finish[...].astype(BF16)
        finish[...] = finish[...] * factor + push_out[n]
        table = cols[at]
        opening = spread(table, OPEN, matrix[...])
        closing = spread(table, CLOSE, matrix[...])
        k = keys[at]
        write, read = k[:, :STATE], k[:, STATE:]
        left[at] = (ro[at].astype(F32) + opening * mm(read, start)).astype(BF16)
        masked[at] = jnp.where(valid_rows(fill[2 * (last - step) + n], D), cot[0, at], jnp.zeros((), BF16))
        right[at, :D] = (gi[at].astype(F32) + closing * mm(write, end)).astype(BF16)
        into = (closing * inner[at].astype(F32)).astype(BF16)
        out = (opening * up[at].astype(F32)).astype(BF16)
        g = pair[n]
        grad_write = mm(g, read, TN) + mm(into, end, NT)
        grad_read = mm(g, write) + mm(out, start, NT)
        right[at, D:] = jnp.concatenate([grad_write, grad_read], axis=1).astype(BF16)
    acc_out[...] += mm(left[...], masked[...], TN).reshape(acc_out.shape)
    acc_in[...] += mm(taken[...], right[...], TN).reshape(acc_in.shape)

    @pl.when(step == last)
    def _():
        scale = 1.0 / 512.0
        for acc, columns in ((acc_in, slice(0, D + 128)), (acc_out, slice(D + 128, None))):
            mine, other = acc[:, core[0]] * scale, acc[:, 1 - core[0]] * scale
            keep[:, columns] = mine.reshape(keep.shape[0], -1)
            give[:, columns] = other.reshape(give.shape[0], -1).astype(BF16)


def ring(axis, by):
    size = lax.axis_size(axis)
    return [(k, (k + by) % size) for k in range(size)]


CHIPS = ("y", "x", "z")


def over_chip(keep, give):
    got = lax.ppermute(give, "c", ring("c", 1))
    half = (keep + got.astype(F32)).astype(BF16)
    return half.reshape(lax.axis_size(CHIPS), 8, -1)


def over_chips(half):
    return lax.all_to_all(half, CHIPS, 0, 0).astype(F32).sum(0)


def on_device(
    replay, block_owner, block_slot, block_fill, log_decay, resets, cotangent, w_in, w_bc, w_out
):
    shards = lax.axis_size(TM)
    core, z = lax.axis_index("c"), lax.axis_index("z")
    my_lane = z * 2 + core
    blocks = block_fill.shape[2]
    steps = blocks * BLOCK
    fill = block_fill[0, 0]
    owner = lax.dynamic_index_in_dim(block_owner[0, :, :, 0], my_lane, 0, keepdims=False)
    slot = lax.dynamic_index_in_dim(block_slot[0], my_lane, 0, keepdims=False)

    mine = replay[0, 0].reshape(BUFCH, BLOCK, D)
    swap = lambda v: lax.ppermute(v, "c", ring("c", 1))
    up_z = lambda v: lax.ppermute(v, "z", ring("z", 1))
    down_z = lambda v: lax.ppermute(v, "z", ring("z", -1))
    first, second = mine[:2], mine[2:]
    below_a, above_a = up_z(first), down_z(second)
    other = swap(mine)
    away = (owner // 2 - z) % 4
    same = owner % 2 == core
    low = slot < 2
    stage = jnp.where(away == 0, 0, jnp.where(away == 2, 2, 1))
    side = jnp.where(away == 2, jnp.where(low, 0, 1), jnp.where(away == 3, 0, 1))
    late = (away % 2 == 1) & ((away == 3) != low)
    source = jnp.where(away == 0, 0, side + jnp.where(late, 4, 0)) + jnp.where(
        same, 0, jnp.where(away == 0, 1, 2)
    )
    index = jnp.where(away == 0, slot, slot % 2)
    ids = jnp.arange(blocks)
    rank = jnp.sum((stage[None] == stage[:, None]) & (ids[None] < ids[:, None]), axis=1)
    counts = jnp.sum(stage[None] == jnp.arange(3)[:, None], axis=1)
    most = (4, blocks, 4)
    turn = jnp.minimum(jnp.arange(blocks)[None], counts[:, None] - 1)
    chosen = (stage[None, None] == jnp.arange(3)[:, None, None]) & (rank[None, None] == turn[:, :, None])
    of = lambda v: jnp.sum(jnp.where(chosen, v[None, None], 0), axis=2)
    block = jnp.where(counts[:, None] > 0, of(ids), blocks).astype(jnp.int32)
    source, index = of(source).astype(jnp.int32), of(index).astype(jnp.int32)
    counts = counts.astype(jnp.int32)

    whole = lambda *dims: pl.BlockSpec(dims, lambda b, *_: (0,) * len(dims))
    tall = lambda width: pl.BlockSpec((BLOCK, width), lambda b, *_: (b, 0))
    lead = lambda *dims: pl.BlockSpec((1, *dims), lambda b, *_: (b,) + (0,) * len(dims))
    table_rows = pl.BlockSpec((32, BLOCK), lambda b, *_: (0, b))
    vmem = lambda kind, *dims: pltpu.VMEM(dims, kind)

    up, rows, cols, ends = call(
        upstream_kernel,
        "upstream",
        (
            shape((steps, D), BF16),
            shape((32, steps), F32),
            shape((steps, 128), F32),
            shape((blocks, 8, 128), F32),
        ),
        pltpu.PrefetchScalarGridSpec(
            num_scalar_prefetch=1,
            grid=(blocks,),
            in_specs=[
                pl.BlockSpec((HEADS, BLOCK), lambda b, *_: (0, b)),
                pl.BlockSpec((1, 1, BLOCK), lambda b, *_: (b, 0, 0)),
                pl.BlockSpec((1, BLOCK, D), lambda b, *_: (0, b, 0)),
                whole(D, D),
            ],
            out_specs=[tall(D), table_rows, tall(128), lead(8, 128)],
        ),
        2 * steps * D * D,
        12 << 20,
    )(fill, log_decay[0], resets.reshape(blocks, 1, BLOCK), cotangent, w_out)

    room = steps + BLOCK
    made = None
    for s in range(3):
        if s == 0:
            below_a, above_a, second, first, up = lax.optimization_barrier(
                (below_a, above_a, second, first, up)
            )
            below_b, above_b = up_z(second), down_z(first)
            sources, near = (mine, other), (below_a, above_a, swap(below_a), swap(above_a))
        elif s == 1:
            below_b, above_b, below_a, above_a, made = lax.optimization_barrier(
                (below_b, above_b, below_a, above_a, made)
            )
            far_low, far_high = up_z(below_a), down_z(above_a)
            sources = (*near, below_b, above_b, swap(below_b), swap(above_b))
        else:
            far_low, far_high, made = lax.optimization_barrier((far_low, far_high, made))
            sources = (far_low, far_high, swap(far_low), swap(far_high))
        number = len(sources)
        at = lambda i, block, *_: block[i]
        inside_at = lambda i, block, *_: jnp.minimum(block[i], blocks - 1)
        out_rows = lambda width: pl.BlockSpec((BLOCK, width), lambda i, block, *_: (block[i], 0))
        out_lead = lambda *dims: pl.BlockSpec((1, *dims), lambda i, block, *_: (block[i], 0, 0))
        in_rows = lambda width: pl.BlockSpec(
            (BLOCK, width), lambda i, block, *_: (jnp.minimum(block[i], blocks - 1), 0)
        )
        pick = lambda n: pl.BlockSpec(
            (pl.squeezed, BLOCK, D),
            lambda i, block, source, index, *_: (jnp.where(source[i] == n, index[i], 0), 0, 0),
        )
        kept = [] if made is None else list(made)
        body = lambda block, source, index, fill, count, *refs, number=number: stage_kernel(
            count, number, block, source, index, fill, *refs
        )
        made = pl.pallas_call(
            body,
            out_shape=(
                shape((room, D), BF16),
                shape((room, D), BF16),
                shape((room, 128), BF16),
                shape((room, D), BF16),
                shape((room, D), BF16),
                shape((blocks + 1, BLOCK, BLOCK), BF16),
                shape((blocks + 1, STATE, D), F32),
                shape((blocks + 1, STATE, D), F32),
            ),
            grid_spec=pltpu.PrefetchScalarGridSpec(
                num_scalar_prefetch=5,
                grid=(most[s],),
                in_specs=[pick(n) for n in range(number)]
                + [
                    whole(D, D),
                    whole(D, 128),
                    in_rows(D),
                    pl.BlockSpec((32, BLOCK), lambda i, block, *_: (0, jnp.minimum(block[i], blocks - 1))),
                    in_rows(128),
                ]
                + [pl.BlockSpec(memory_space=pl.ANY)] * len(kept),
                out_specs=[
                    out_rows(D),
                    out_rows(D),
                    out_rows(128),
                    out_rows(D),
                    out_rows(D),
                    out_lead(BLOCK, BLOCK),
                    out_lead(STATE, D),
                    out_lead(STATE, D),
                ],
                scratch_shapes=[vmem(BF16, 256, D)],
            ),
            input_output_aliases={5 + number + 5 + n: n for n in range(len(kept))},
            name=f"stage_{s}",
            compiler_params=pltpu.CompilerParams(vmem_limit_bytes=VMEM_LIMIT),
            cost_estimate=pl.CostEstimate(
                flops=4 * BLOCK * D * (D + 1024) + 4 * HEADS * 3 * BLOCK**3,
                bytes_accessed=16 << 20,
                transcendentals=0,
            ),
        )(block[s], source[s], index[s], fill, counts[s : s + 1], *sources, w_in, w_bc, up, rows, cols, *kept)
    taken, inner, keys, ro, gi, pair, push_in, push_out = made

    some = lambda *dims: pl.BlockSpec((blocks // 2, *dims), lambda b, *_: (b, 0, 0))
    starts, gains, total = call(
        local_kernel,
        "local",
        (shape((blocks, STATE, D), F32), shape((blocks, 16, D), F32), shape((shards, 16, D), BF16)),
        pl.GridSpec(
            grid=(2,),
            in_specs=[some(STATE, D), some(STATE, D), whole(blocks, 8, 128)],
            out_specs=[some(STATE, D), some(16, D), whole(shards, 16, D)],
            scratch_shapes=[vmem(F32, blocks * 8, D), vmem(F32, 136, D)],
        ),
        1 << 24,
        7 << 20,
    )(push_in, push_out, ends)

    terms = lax.all_to_all(total, TM, 0, 0)
    entering = call(
        scan_kernel,
        "scan",
        shape((shards, 8, D), BF16),
        pltpu.PrefetchScalarGridSpec(
            num_scalar_prefetch=1,
            grid=(1,),
            in_specs=[whole(shards, 16, D)],
            out_specs=whole(shards, 8, D),
            scratch_shapes=[vmem(F32, shards, 8, D)],
        ),
        1 << 20,
        1 << 20,
    )(lax.axis_index(TM).reshape(1), terms)
    enter = lax.all_to_all(entering, TM, 0, 0).reshape(128, D)

    own_core = core.reshape(1)
    two = lambda width: pl.BlockSpec((2 * BLOCK, width), lambda b, *_: (b, 0))
    pairs = lambda *dims: pl.BlockSpec((2, *dims), lambda b, *_: (b, 0, 0))
    back = lambda spec: pl.BlockSpec(
        spec.block_shape, lambda s, *refs: spec.index_map(blocks // 2 - 1 - s, *refs)
    )
    wide = D + 128
    both = wide + D
    keep, give = call(
        gradient_kernel,
        "gradient",
        (shape((D // 2, both), F32), shape((D // 2, both), BF16)),
        pltpu.PrefetchScalarGridSpec(
            num_scalar_prefetch=2,
            grid=(blocks // 2,),
            in_specs=[
                back(s)
                for s in (
                    pl.BlockSpec((1, 2 * BLOCK, D), lambda b, *_: (0, b, 0)),
                    two(D),
                    two(D),
                    two(D),
                    two(128),
                    two(128),
                    two(D),
                    two(D),
                    pairs(BLOCK, BLOCK),
                    pairs(STATE, D),
                    pairs(STATE, D),
                    pairs(16, D),
                    whole(128, D),
                )
            ],
            out_specs=[whole(D // 2, both), whole(D // 2, both)],
            scratch_shapes=[
                vmem(F32, D // 16, 2, 8, wide),
                vmem(F32, D // 16, 2, 8, D),
                vmem(BF16, 2 * BLOCK, D),
                vmem(BF16, 2 * BLOCK, wide),
                vmem(BF16, 2 * BLOCK, D),
                vmem(F32, STATE, D),
                vmem(BF16, 256, D),
            ],
        ),
        2 * steps * D * (2 * D + 1280),
        36 << 20,
    )(own_core, fill, cotangent, taken, inner, up, keys, cols, ro, gi, pair, starts, push_out, gains, enter)

    grads = over_chips(over_chip(keep, give))
    return (grads[:, :D], grads[:, D:wide], grads[:, wide:])


def solution(mesh):
    torus = Mesh(mesh.devices.reshape(4, 4, 4, 2), ("y", "x", "z", "c"))
    lane = ("z", "c")
    every = TM + lane
    return jax.shard_map(
        on_device,
        mesh=torus,
        in_specs=(
            P(lane, TM, None, None),
            P(TM, None, None, None),
            P(TM, None, None),
            P(lane, TM, None),
            P(lane, None, TM),
            P(lane, TM),
            P(lane, TM, None),
            P(),
            P(),
            P(),
        ),
        out_specs=(P(every, None), P(every, None), P(every, None)),
        check_vma=False,
    )
```

```python
import math

import jax
import jax.numpy as jnp
from jax import lax
from jax.experimental import pallas as pl
from jax.experimental.pallas import tpu as pltpu
from jax.sharding import Mesh
from jax.sharding import PartitionSpec as P

D = 1024
HEAD = 64
HEADS = 16
STATE = 64
BLOCK = 256
BUFCH = 4
TM = ("y", "x")
LOG2E = math.log2(math.e)
FAR = -1e4
F32, BF16 = jnp.float32, jnp.bfloat16
CNT, OPEN, CLOSE = 16, 32, 48
NT = (((1,), (1,)), ((), ()))
TN = (((0,), (0,)), ((), ()))
NN = (((1,), (0,)), ((), ()))
MIB = 1024 * 1024
GRADIENT_ROOM = 36


def mm(a, b, dims=NN):
    return lax.dot_general(a, b, dims, preferred_element_type=F32)


def split(x):
    high = x.astype(BF16)
    return jnp.concatenate([high, (x - high.astype(F32)).astype(BF16)], axis=1)


def spread_matrix():
    row = lax.broadcasted_iota(jnp.int32, (2 * 128, D), 0) & 127
    head = lax.broadcasted_iota(jnp.int32, (2 * 128, D), 1) >> 6
    return jnp.where(row == head, 1.0, 0.0).astype(BF16)


def spread(table, base, matrix):
    return mm(split(pltpu.roll(table, 128 - base, 1)), matrix)


def call(kernel, name, out_shape, grid_spec, flops, nbytes, room=24):
    return pl.pallas_call(
        kernel,
        out_shape=out_shape,
        grid_spec=grid_spec,
        name=name,
        compiler_params=pltpu.CompilerParams(vmem_limit_bytes=room * MIB),
        cost_estimate=pl.CostEstimate(flops=flops, bytes_accessed=nbytes, transcendentals=0),
    )


def shape(dims, kind):
    return jax.ShapeDtypeStruct(dims, kind)


def valid_rows(fill, width):
    return lax.broadcasted_iota(jnp.int32, (BLOCK, width), 0) < fill


def upstream_kernel(fill, decay, resets, cot, w_out, up, rows, cols, ends):
    b = pl.program_id(0)
    upper = lax.broadcasted_iota(jnp.int32, (BLOCK, BLOCK), 0) <= lax.broadcasted_iota(
        jnp.int32, (BLOCK, BLOCK), 1
    )
    upper = jnp.where(upper, 1.0, 0.0)
    both = jnp.concatenate(
        [decay[...] * LOG2E, jnp.broadcast_to(resets[0].astype(F32), (8, BLOCK))], axis=0
    )
    summed = lax.dot_general(
        both, upper, NN, precision=lax.Precision.HIGHEST, preferred_element_type=F32
    )
    cum, count = summed[:HEADS], summed[HEADS : HEADS + 8]
    two = jnp.concatenate([count, count], axis=0)
    opening = jnp.where(two == 0.0, jnp.exp2(cum), 0.0)
    last = jnp.broadcast_to(cum[:, BLOCK - 1 :], (HEADS, BLOCK))
    last_two = jnp.broadcast_to(two[:, BLOCK - 1 :], (HEADS, BLOCK))
    closing = jnp.where(two == last_two, jnp.exp2(last - cum), 0.0)
    table = jnp.concatenate(
        [cum, two, opening, closing, jnp.zeros((64, BLOCK), F32)], axis=0
    )
    rows[...] = table[:32]
    turned = table.T
    cols[...] = turned
    ends[0] = jnp.broadcast_to(turned[BLOCK - 1 :], (8, 128))
    masked = jnp.where(valid_rows(fill[b], D), cot[0], jnp.zeros((), BF16))
    up[...] = mm(masked, w_out[...], NT).astype(BF16)


def inside(inner, keys, up, rows, cols, ro, gi, pair):
    half = BLOCK // 2
    at = lax.broadcasted_iota(jnp.int32, (BLOCK, BLOCK), 0)
    to = lax.broadcasted_iota(jnp.int32, (BLOCK, BLOCK), 1)
    linked = (to <= at) & (cols[:, CNT : CNT + 1] == rows[CNT : CNT + 1, :])
    bias = jnp.where(linked, 0.0, FAR)
    k = keys[...]
    scores = mm(k[:, STATE:], k[:, :STATE], NT)
    bias_a, bias_b = bias[:half, :half], bias[half:]
    scores_a, scores_b = scores[:half, :half], scores[half:]
    left = lax.broadcasted_iota(jnp.int32, (BLOCK, 128), 1) < HEAD
    zero = jnp.zeros((), BF16)
    turned = up[...].T
    paired_a, paired_b = jnp.zeros((half, half), F32), jnp.zeros((half, BLOCK), F32)
    for q in range(HEADS // 2):
        lanes = slice(128 * q, 128 * q + 128)
        x, u = inner[:, lanes], up[:, lanes]
        grads = []
        for s in range(2):
            h = 2 * q + s
            mine = left if s == 0 else ~left
            xs, us = jnp.where(mine, x, zero), jnp.where(mine, u, zero)
            decays_a = jnp.exp2(cols[:half, h : h + 1] - rows[h : h + 1, :half] + bias_a)
            decays_b = jnp.exp2(cols[half:, h : h + 1] - rows[h : h + 1, :] + bias_b)
            mixing_a, mixing_b = (decays_a * scores_a).astype(BF16), (decays_b * scores_b).astype(BF16)
            paired_a = paired_a + decays_a * mm(us[:half], x[:half], NT)
            paired_b = paired_b + decays_b * mm(us[half:], x, NT)
            a, b = mm(mixing_a, xs[:half]), mm(mixing_b, xs)
            readout_a, readout_b = (a, b) if s == 0 else (readout_a + a, readout_b + b)
            head = turned[HEAD * h : HEAD * h + HEAD]
            g = mm(head[:, half:], mixing_b)
            grads.append(jnp.concatenate([g[:, :half] + mm(head[:, :half], mixing_a), g[:, half:]], axis=1))
        ro[:half, lanes] = readout_a.astype(BF16)
        ro[half:, lanes] = readout_b.astype(BF16)
        gi[:, lanes] = jnp.concatenate(grads, axis=0).astype(BF16).T
    pair[0, :half, :half] = paired_a.astype(BF16)
    pair[0, :half, half:] = jnp.zeros((half, half), BF16)
    pair[0, half:] = paired_b.astype(BF16)


def stage_kernel(count, number, block, source, index, fill, *refs):
    picks = refs[:number]
    w_in, w_bc, up, rows, cols = refs[number : number + 5]
    outs = refs[-9:]
    taken, inner, keys, ro, gi, pair, push_in, push_out, matrix = outs
    i = pl.program_id(0)

    @pl.when(i == 0)
    def _():
        matrix[...] = spread_matrix()

    @pl.when(i < count[0])
    def _():
        valid = valid_rows(fill[jnp.minimum(block[i], fill.shape[0] - 1)], D)
        for n in range(number):

            @pl.when(source[i] == n)
            def _(n=n):
                taken[...] = jnp.where(valid, picks[n][...], jnp.zeros((), BF16))

        got = taken[...]
        x = mm(got, w_in[...]).astype(BF16)
        k = mm(got, w_bc[...]).astype(BF16)
        inner[...] = x
        keys[...] = k
        table = cols[...]
        opening = spread(table, OPEN, matrix[...])
        closing = spread(table, CLOSE, matrix[...])
        into = (closing * x.astype(F32)).astype(BF16)
        out = (opening * up[...].astype(F32)).astype(BF16)
        turned = k.astype(F32).T.astype(BF16)
        push_in[0] = mm(turned[:STATE], into)
        push_out[0] = mm(turned[STATE:], out)
        inside(inner, keys, up, rows, cols, ro, gi, pair)


def local_kernel(push_in, push_out, ends, starts, gains, total, factors, state):
    b = pl.program_id(0)

    @pl.when(b == 0)
    def _():
        table = ends[...].reshape(factors.shape[0], 128)
        factors[...] = spread(table, OPEN, spread_matrix())
        state[:128] = jnp.zeros((128, D), F32)
        state[128:] = jnp.ones((8, D), F32)

    each = starts.shape[0]
    for n in range(each):
        factor = factors[pl.ds((b * each + n) * 8, 8)]
        before = state[128:]
        starts[n] = state[:64]
        gains[n] = jnp.concatenate([factor, before], axis=0)
        state[:64] = state[:64] * factor[:1] + push_in[n]
        state[64:128] = state[64:128] + before[:1] * push_out[n]
        state[128:] = before * factor

    @pl.when(b == pl.num_programs(0) - 1)
    def _():
        gain = state[128:]
        high = gain.astype(BF16).astype(F32)
        top = lax.broadcasted_iota(jnp.int32, gain.shape, 0) == 0
        gain = jnp.where(top, high, gain - high)
        for n in range(total.shape[0]):
            total[n] = jnp.concatenate([state[8 * n : 8 * n + 8], gain], axis=0).astype(BF16)


def scan_kernel(which, terms, entering, forth):
    shards = terms.shape[0]
    part = lambda t: terms[t].astype(F32)
    gain = lambda v: v[8:9] + v[9:10]
    state = jnp.zeros((8, D), F32)
    for t in range(shards):
        forth[t] = state
        v = part(t)
        state = state * gain(v) + v[:8]
    back = jnp.zeros((8, D), F32)
    ahead = jnp.full((8, D), which[0], jnp.int32) < shards // 2
    for t in reversed(range(shards)):
        entering[t] = jnp.where(ahead, forth[t], back).astype(BF16)
        v = part(t)
        back = back * gain(v) + v[:8]


def store_halves(core, acc, keep, give):
    scale = 1.0 / 512.0
    keep[...] = (acc[:, core[0]] * scale).reshape(keep.shape)
    give[...] = (acc[:, 1 - core[0]] * scale).reshape(give.shape).astype(BF16)


def gradient_kernel(
    core, fill, cot, taken, inner, up, keys, cols, ro, gi, pair, starts, push_out, gains, enter,
    keep, give, acc_in, acc_out, left, right, masked, took, finish, matrix,
):
    step = pl.program_id(0)
    last = pl.num_programs(0) - 1

    @pl.when(step == 0)
    def _():
        matrix[...] = spread_matrix()
        finish[...] = enter[64:].astype(F32)
        acc_in[...] = jnp.zeros_like(acc_in)
        acc_out[...] = jnp.zeros_like(acc_out)

    at = pl.ds(pl.multiple_of((step & 1) * BLOCK, BLOCK), BLOCK)
    factor, before = gains[0, 0:1], gains[0, 8:9]
    start = (starts[0] + before * enter[:64].astype(F32)).astype(BF16)
    end = finish[...].astype(BF16)
    finish[...] = finish[...] * factor + push_out[0]
    table = cols[...]
    opening = spread(table, OPEN, matrix[...])
    closing = spread(table, CLOSE, matrix[...])
    k = keys[...]
    write, read = k[:, :STATE], k[:, STATE:]
    left[at] = (ro[...].astype(F32) + opening * mm(read, start)).astype(BF16)
    masked[at] = jnp.where(valid_rows(fill[last - step], D), cot[0], jnp.zeros((), BF16))
    took[at] = taken[...]
    right[at, :D] = (gi[...].astype(F32) + closing * mm(write, end)).astype(BF16)
    into = (closing * inner[...].astype(F32)).astype(BF16)
    out = (opening * up[...].astype(F32)).astype(BF16)
    g = pair[0]
    grad_write = mm(g, read, TN) + mm(into, end, NT)
    grad_read = mm(g, write) + mm(out, start, NT)
    right[at, D:] = jnp.concatenate([grad_write, grad_read], axis=1).astype(BF16)

    @pl.when((step & 1) == 1)
    def _():
        acc_out[...] += mm(left[...], masked[...], TN).reshape(acc_out.shape)
        acc_in[...] += mm(took[...], right[...], TN).reshape(acc_in.shape)

    @pl.when(step == last)
    def _():
        scale = 1.0 / 512.0
        for acc, columns in ((acc_in, slice(0, D + 128)), (acc_out, slice(D + 128, None))):
            mine, other = acc[:, core[0]] * scale, acc[:, 1 - core[0]] * scale
            keep[:, columns] = mine.reshape(keep.shape[0], -1)
            give[:, columns] = other.reshape(give.shape[0], -1).astype(BF16)


def ring(axis, by):
    size = lax.axis_size(axis)
    return [(k, (k + by) % size) for k in range(size)]


CHIPS = ("y", "x", "z")


def over_chip(keep, give):
    got = lax.ppermute(give, "c", ring("c", 1))
    half = (keep + got.astype(F32)).astype(BF16)
    return half.reshape(lax.axis_size(CHIPS), 8, -1)


def over_chips(half):
    return lax.all_to_all(half, CHIPS, 0, 0).astype(F32).sum(0)


def on_device(
    replay, block_owner, block_slot, block_fill, log_decay, resets, cotangent, w_in, w_bc, w_out
):
    shards = lax.axis_size(TM)
    core, z = lax.axis_index("c"), lax.axis_index("z")
    my_lane = z * 2 + core
    blocks = block_fill.shape[2]
    steps = blocks * BLOCK
    fill = block_fill[0, 0]
    owner = lax.dynamic_index_in_dim(block_owner[0, :, :, 0], my_lane, 0, keepdims=False)
    slot = lax.dynamic_index_in_dim(block_slot[0], my_lane, 0, keepdims=False)

    mine = replay[0, 0].reshape(BUFCH, BLOCK, D)
    swap = lambda v: lax.ppermute(v, "c", ring("c", 1))
    up_z = lambda v: lax.ppermute(v, "z", ring("z", 1))
    down_z = lambda v: lax.ppermute(v, "z", ring("z", -1))
    first, second = mine[:2], mine[2:]
    below_a, above_a = up_z(first), down_z(second)
    other = swap(mine)
    away = (owner // 2 - z) % 4
    same = owner % 2 == core
    low = slot < 2
    stage = jnp.where(away == 0, 0, jnp.where(away == 2, 2, 1))
    side = jnp.where(away == 2, jnp.where(low, 0, 1), jnp.where(away == 3, 0, 1))
    late = (away % 2 == 1) & ((away == 3) != low)
    source = jnp.where(away == 0, 0, side + jnp.where(late, 4, 0)) + jnp.where(
        same, 0, jnp.where(away == 0, 1, 2)
    )
    index = jnp.where(away == 0, slot, slot % 2)
    ids = jnp.arange(blocks)
    rank = jnp.sum((stage[None] == stage[:, None]) & (ids[None] < ids[:, None]), axis=1)
    counts = jnp.sum(stage[None] == jnp.arange(3)[:, None], axis=1)
    most = (4, blocks, 4)
    turn = jnp.minimum(jnp.arange(blocks)[None], counts[:, None] - 1)
    chosen = (stage[None, None] == jnp.arange(3)[:, None, None]) & (rank[None, None] == turn[:, :, None])
    of = lambda v: jnp.sum(jnp.where(chosen, v[None, None], 0), axis=2)
    block = jnp.where(counts[:, None] > 0, of(ids), blocks).astype(jnp.int32)
    source, index = of(source).astype(jnp.int32), of(index).astype(jnp.int32)
    counts = counts.astype(jnp.int32)

    whole = lambda *dims: pl.BlockSpec(dims, lambda b, *_: (0,) * len(dims))
    tall = lambda width: pl.BlockSpec((BLOCK, width), lambda b, *_: (b, 0))
    lead = lambda *dims: pl.BlockSpec((1, *dims), lambda b, *_: (b,) + (0,) * len(dims))
    table_rows = pl.BlockSpec((32, BLOCK), lambda b, *_: (0, b))
    vmem = lambda kind, *dims: pltpu.VMEM(dims, kind)

    up, rows, cols, ends = call(
        upstream_kernel,
        "upstream",
        (
            shape((steps, D), BF16),
            shape((32, steps), F32),
            shape((steps, 128), F32),
            shape((blocks, 8, 128), F32),
        ),
        pltpu.PrefetchScalarGridSpec(
            num_scalar_prefetch=1,
            grid=(blocks,),
            in_specs=[
                pl.BlockSpec((HEADS, BLOCK), lambda b, *_: (0, b)),
                pl.BlockSpec((1, 1, BLOCK), lambda b, *_: (b, 0, 0)),
                pl.BlockSpec((1, BLOCK, D), lambda b, *_: (0, b, 0)),
                whole(D, D),
            ],
            out_specs=[tall(D), table_rows, tall(128), lead(8, 128)],
        ),
        2 * steps * D * D,
        12 << 20,
    )(fill, log_decay[0], resets.reshape(blocks, 1, BLOCK), cotangent, w_out)

    room = steps + BLOCK
    made = None
    for s in range(3):
        if s == 0:
            below_a, above_a, second, first, up = lax.optimization_barrier(
                (below_a, above_a, second, first, up)
            )
            below_b, above_b = up_z(second), down_z(first)
            sources, near = (mine, other), (below_a, above_a, swap(below_a), swap(above_a))
        elif s == 1:
            below_b, above_b, below_a, above_a, made = lax.optimization_barrier(
                (below_b, above_b, below_a, above_a, made)
            )
            far_low, far_high = up_z(below_a), down_z(above_a)
            sources = (*near, below_b, above_b, swap(below_b), swap(above_b))
        else:
            far_low, far_high, made = lax.optimization_barrier((far_low, far_high, made))
            sources = (far_low, far_high, swap(far_low), swap(far_high))
        number = len(sources)
        at = lambda i, block, *_: block[i]
        inside_at = lambda i, block, *_: jnp.minimum(block[i], blocks - 1)
        out_rows = lambda width: pl.BlockSpec((BLOCK, width), lambda i, block, *_: (block[i], 0))
        out_lead = lambda *dims: pl.BlockSpec((1, *dims), lambda i, block, *_: (block[i], 0, 0))
        in_rows = lambda width: pl.BlockSpec(
            (BLOCK, width), lambda i, block, *_: (jnp.minimum(block[i], blocks - 1), 0)
        )
        pick = lambda n: pl.BlockSpec(
            (pl.squeezed, BLOCK, D),
            lambda i, block, source, index, *_: (jnp.where(source[i] == n, index[i], 0), 0, 0),
        )
        kept = [] if made is None else list(made)
        body = lambda block, source, index, fill, count, *refs, number=number: stage_kernel(
            count, number, block, source, index, fill, *refs
        )
        made = pl.pallas_call(
            body,
            out_shape=(
                shape((room, D), BF16),
                shape((room, D), BF16),
                shape((room, 128), BF16),
                shape((room, D), BF16),
                shape((room, D), BF16),
                shape((blocks + 1, BLOCK, BLOCK), BF16),
                shape((blocks + 1, STATE, D), F32),
                shape((blocks + 1, STATE, D), F32),
            ),
            grid_spec=pltpu.PrefetchScalarGridSpec(
                num_scalar_prefetch=5,
                grid=(most[s],),
                in_specs=[pick(n) for n in range(number)]
                + [
                    whole(D, D),
                    whole(D, 128),
                    in_rows(D),
                    pl.BlockSpec((32, BLOCK), lambda i, block, *_: (0, jnp.minimum(block[i], blocks - 1))),
                    in_rows(128),
                ]
                + [pl.BlockSpec(memory_space=pl.ANY)] * len(kept),
                out_specs=[
                    out_rows(D),
                    out_rows(D),
                    out_rows(128),
                    out_rows(D),
                    out_rows(D),
                    out_lead(BLOCK, BLOCK),
                    out_lead(STATE, D),
                    out_lead(STATE, D),
                ],
                scratch_shapes=[vmem(BF16, 256, D)],
            ),
            input_output_aliases={5 + number + 5 + n: n for n in range(len(kept))},
            name=f"stage_{s}",
            compiler_params=pltpu.CompilerParams(vmem_limit_bytes=32 * MIB),
            cost_estimate=pl.CostEstimate(
                flops=4 * BLOCK * D * (D + 1024) + 4 * HEADS * 3 * BLOCK**3,
                bytes_accessed=16 << 20,
                transcendentals=0,
            ),
        )(block[s], source[s], index[s], fill, counts[s : s + 1], *sources, w_in, w_bc, up, rows, cols, *kept)
    taken, inner, keys, ro, gi, pair, push_in, push_out = made

    some = lambda *dims: pl.BlockSpec((blocks // 2, *dims), lambda b, *_: (b, 0, 0))
    starts, gains, total = call(
        local_kernel,
        "local",
        (shape((blocks, STATE, D), F32), shape((blocks, 16, D), F32), shape((shards, 16, D), BF16)),
        pl.GridSpec(
            grid=(2,),
            in_specs=[some(STATE, D), some(STATE, D), whole(blocks, 8, 128)],
            out_specs=[some(STATE, D), some(16, D), whole(shards, 16, D)],
            scratch_shapes=[vmem(F32, blocks * 8, D), vmem(F32, 136, D)],
        ),
        1 << 24,
        7 << 20,
    )(push_in, push_out, ends)

    terms = lax.all_to_all(total, TM, 0, 0)
    entering = call(
        scan_kernel,
        "scan",
        shape((shards, 8, D), BF16),
        pltpu.PrefetchScalarGridSpec(
            num_scalar_prefetch=1,
            grid=(1,),
            in_specs=[whole(shards, 16, D)],
            out_specs=whole(shards, 8, D),
            scratch_shapes=[vmem(F32, shards, 8, D)],
        ),
        1 << 20,
        1 << 20,
    )(lax.axis_index(TM).reshape(1), terms)
    enter = lax.all_to_all(entering, TM, 0, 0).reshape(128, D)

    own_core = core.reshape(1)
    back = lambda spec: pl.BlockSpec(
        spec.block_shape, lambda s, *refs: spec.index_map(blocks - 1 - s, *refs)
    )
    wide = D + 128
    both = wide + D
    keep, give = call(
        gradient_kernel,
        "gradient",
        (shape((D // 2, both), F32), shape((D // 2, both), BF16)),
        pltpu.PrefetchScalarGridSpec(
            num_scalar_prefetch=2,
            grid=(blocks,),
            in_specs=[
                back(s)
                for s in (
                    pl.BlockSpec((1, BLOCK, D), lambda b, *_: (0, b, 0)),
                    tall(D),
                    tall(D),
                    tall(D),
                    tall(128),
                    tall(128),
                    tall(D),
                    tall(D),
                    lead(BLOCK, BLOCK),
                    lead(STATE, D),
                    lead(STATE, D),
                    lead(16, D),
                    whole(128, D),
                )
            ],
            out_specs=[whole(D // 2, both), whole(D // 2, both)],
            scratch_shapes=[
                vmem(F32, D // 16, 2, 8, wide),
                vmem(F32, D // 16, 2, 8, D),
                vmem(BF16, 2 * BLOCK, D),
                vmem(BF16, 2 * BLOCK, wide),
                vmem(BF16, 2 * BLOCK, D),
                vmem(BF16, 2 * BLOCK, D),
                vmem(F32, STATE, D),
                vmem(BF16, 256, D),
            ],
        ),
        2 * steps * D * (2 * D + 1280),
        36 << 20,
        room=GRADIENT_ROOM,
    )(own_core, fill, cotangent, taken, inner, up, keys, cols, ro, gi, pair, starts, push_out, gains, enter)

    grads = over_chips(over_chip(keep, give))
    return (grads[:, :D], grads[:, D:wide], grads[:, wide:])


def solution(mesh):
    torus = Mesh(mesh.devices.reshape(4, 4, 4, 2), ("y", "x", "z", "c"))
    lane = ("z", "c")
    every = TM + lane
    return jax.shard_map(
        on_device,
        mesh=torus,
        in_specs=(
            P(lane, TM, None, None),
            P(TM, None, None, None),
            P(TM, None, None),
            P(lane, TM, None),
            P(lane, None, TM),
            P(lane, TM),
            P(lane, TM, None),
            P(),
            P(),
            P(),
        ),
        out_specs=(P(every, None), P(every, None), P(every, None)),
        check_vma=False,
    )
```

```python
import math

import jax
import jax.numpy as jnp
from jax import lax
from jax.experimental import pallas as pl
from jax.experimental.pallas import tpu as pltpu
from jax.sharding import Mesh
from jax.sharding import PartitionSpec as P

D = 1024
HEAD = 64
HEADS = 16
STATE = 64
BLOCK = 256
BUFCH = 4
TM = ("y", "x")
LOG2E = math.log2(math.e)
FAR = -1e4
F32, BF16 = jnp.float32, jnp.bfloat16
CNT, OPEN, CLOSE = 16, 32, 48
NT = (((1,), (1,)), ((), ()))
TN = (((0,), (0,)), ((), ()))
NN = (((1,), (0,)), ((), ()))
MIB = 1024 * 1024
GRADIENT_ROOM = 56


def mm(a, b, dims=NN):
    return lax.dot_general(a, b, dims, preferred_element_type=F32)


def split(x):
    high = x.astype(BF16)
    return jnp.concatenate([high, (x - high.astype(F32)).astype(BF16)], axis=1)


def spread_matrix():
    row = lax.broadcasted_iota(jnp.int32, (2 * 128, D), 0) & 127
    head = lax.broadcasted_iota(jnp.int32, (2 * 128, D), 1) >> 6
    return jnp.where(row == head, 1.0, 0.0).astype(BF16)


def spread(table, base, matrix):
    return mm(split(pltpu.roll(table, 128 - base, 1)), matrix)


def call(kernel, name, out_shape, grid_spec, flops, nbytes, room=24):
    return pl.pallas_call(
        kernel,
        out_shape=out_shape,
        grid_spec=grid_spec,
        name=name,
        compiler_params=pltpu.CompilerParams(vmem_limit_bytes=room * MIB),
        cost_estimate=pl.CostEstimate(flops=flops, bytes_accessed=nbytes, transcendentals=0),
    )


def shape(dims, kind):
    return jax.ShapeDtypeStruct(dims, kind)


def valid_rows(fill, width):
    return lax.broadcasted_iota(jnp.int32, (BLOCK, width), 0) < fill


def upstream_kernel(fill, decay, resets, cot, w_out, up, rows, cols, ends):
    b = pl.program_id(0)
    upper = lax.broadcasted_iota(jnp.int32, (BLOCK, BLOCK), 0) <= lax.broadcasted_iota(
        jnp.int32, (BLOCK, BLOCK), 1
    )
    upper = jnp.where(upper, 1.0, 0.0)
    both = jnp.concatenate(
        [decay[...] * LOG2E, jnp.broadcast_to(resets[0].astype(F32), (8, BLOCK))], axis=0
    )
    summed = lax.dot_general(
        both, upper, NN, precision=lax.Precision.HIGHEST, preferred_element_type=F32
    )
    cum, count = summed[:HEADS], summed[HEADS : HEADS + 8]
    two = jnp.concatenate([count, count], axis=0)
    opening = jnp.where(two == 0.0, jnp.exp2(cum), 0.0)
    last = jnp.broadcast_to(cum[:, BLOCK - 1 :], (HEADS, BLOCK))
    last_two = jnp.broadcast_to(two[:, BLOCK - 1 :], (HEADS, BLOCK))
    closing = jnp.where(two == last_two, jnp.exp2(last - cum), 0.0)
    table = jnp.concatenate(
        [cum, two, opening, closing, jnp.zeros((64, BLOCK), F32)], axis=0
    )
    rows[...] = table[:32]
    turned = table.T
    cols[...] = turned
    ends[0] = jnp.broadcast_to(turned[BLOCK - 1 :], (8, 128))
    masked = jnp.where(valid_rows(fill[b], D), cot[0], jnp.zeros((), BF16))
    up[...] = mm(masked, w_out[...], NT).astype(BF16)


def inside(inner, keys, up, rows, cols, ro, gi, pair):
    half = BLOCK // 2
    at = lax.broadcasted_iota(jnp.int32, (BLOCK, BLOCK), 0)
    to = lax.broadcasted_iota(jnp.int32, (BLOCK, BLOCK), 1)
    linked = (to <= at) & (cols[:, CNT : CNT + 1] == rows[CNT : CNT + 1, :])
    bias = jnp.where(linked, 0.0, FAR)
    k = keys[...]
    scores = mm(k[:, STATE:], k[:, :STATE], NT)
    bias_a, bias_b = bias[:half, :half], bias[half:]
    scores_a, scores_b = scores[:half, :half], scores[half:]
    left = lax.broadcasted_iota(jnp.int32, (BLOCK, 128), 1) < HEAD
    zero = jnp.zeros((), BF16)
    turned = up[...].T
    paired_a, paired_b = jnp.zeros((half, half), F32), jnp.zeros((half, BLOCK), F32)
    for q in range(HEADS // 2):
        lanes = slice(128 * q, 128 * q + 128)
        x, u = inner[:, lanes], up[:, lanes]
        grads = []
        for s in range(2):
            h = 2 * q + s
            mine = left if s == 0 else ~left
            xs, us = jnp.where(mine, x, zero), jnp.where(mine, u, zero)
            decays_a = jnp.exp2(cols[:half, h : h + 1] - rows[h : h + 1, :half] + bias_a)
            decays_b = jnp.exp2(cols[half:, h : h + 1] - rows[h : h + 1, :] + bias_b)
            mixing_a, mixing_b = (decays_a * scores_a).astype(BF16), (decays_b * scores_b).astype(BF16)
            paired_a = paired_a + decays_a * mm(us[:half], x[:half], NT)
            paired_b = paired_b + decays_b * mm(us[half:], x, NT)
            a, b = mm(mixing_a, xs[:half]), mm(mixing_b, xs)
            readout_a, readout_b = (a, b) if s == 0 else (readout_a + a, readout_b + b)
            head = turned[HEAD * h : HEAD * h + HEAD]
            g = mm(head[:, half:], mixing_b)
            grads.append(jnp.concatenate([g[:, :half] + mm(head[:, :half], mixing_a), g[:, half:]], axis=1))
        ro[:half, lanes] = readout_a.astype(BF16)
        ro[half:, lanes] = readout_b.astype(BF16)
        gi[:, lanes] = jnp.concatenate(grads, axis=0).astype(BF16).T
    pair[0, :half, :half] = paired_a.astype(BF16)
    pair[0, :half, half:] = jnp.zeros((half, half), BF16)
    pair[0, half:] = paired_b.astype(BF16)


def stage_kernel(count, number, block, source, index, fill, *refs):
    picks = refs[:number]
    w_in, w_bc, up, rows, cols = refs[number : number + 5]
    outs = refs[-9:]
    taken, inner, keys, ro, gi, pair, push_in, push_out, matrix = outs
    i = pl.program_id(0)

    @pl.when(i == 0)
    def _():
        matrix[...] = spread_matrix()

    @pl.when(i < count[0])
    def _():
        valid = valid_rows(fill[jnp.minimum(block[i], fill.shape[0] - 1)], D)
        for n in range(number):

            @pl.when(source[i] == n)
            def _(n=n):
                taken[...] = jnp.where(valid, picks[n][...], jnp.zeros((), BF16))

        got = taken[...]
        x = mm(got, w_in[...]).astype(BF16)
        k = mm(got, w_bc[...]).astype(BF16)
        inner[...] = x
        keys[...] = k
        table = cols[...]
        opening = spread(table, OPEN, matrix[...])
        closing = spread(table, CLOSE, matrix[...])
        into = (closing * x.astype(F32)).astype(BF16)
        out = (opening * up[...].astype(F32)).astype(BF16)
        turned = k.astype(F32).T.astype(BF16)
        push_in[0] = mm(turned[:STATE], into)
        push_out[0] = mm(turned[STATE:], out)
        inside(inner, keys, up, rows, cols, ro, gi, pair)


def local_kernel(push_in, push_out, ends, starts, gains, total, factors, state):
    b = pl.program_id(0)

    @pl.when(b == 0)
    def _():
        table = ends[...].reshape(factors.shape[0], 128)
        factors[...] = spread(table, OPEN, spread_matrix())
        state[:128] = jnp.zeros((128, D), F32)
        state[128:] = jnp.ones((8, D), F32)

    each = starts.shape[0]
    for n in range(each):
        factor = factors[pl.ds((b * each + n) * 8, 8)]
        before = state[128:]
        starts[n] = state[:64]
        gains[n] = jnp.concatenate([factor, before], axis=0)
        state[:64] = state[:64] * factor[:1] + push_in[n]
        state[64:128] = state[64:128] + before[:1] * push_out[n]
        state[128:] = before * factor

    @pl.when(b == pl.num_programs(0) - 1)
    def _():
        gain = state[128:]
        high = gain.astype(BF16).astype(F32)
        top = lax.broadcasted_iota(jnp.int32, gain.shape, 0) == 0
        gain = jnp.where(top, high, gain - high)
        for n in range(total.shape[0]):
            total[n] = jnp.concatenate([state[8 * n : 8 * n + 8], gain], axis=0).astype(BF16)


def scan_kernel(which, terms, entering, forth):
    shards = terms.shape[0]
    part = lambda t: terms[t].astype(F32)
    gain = lambda v: v[8:9] + v[9:10]
    state = jnp.zeros((8, D), F32)
    for t in range(shards):
        forth[t] = state
        v = part(t)
        state = state * gain(v) + v[:8]
    back = jnp.zeros((8, D), F32)
    ahead = jnp.full((8, D), which[0], jnp.int32) < shards // 2
    for t in reversed(range(shards)):
        entering[t] = jnp.where(ahead, forth[t], back).astype(BF16)
        v = part(t)
        back = back * gain(v) + v[:8]


def store_halves(core, acc, keep, give):
    scale = 1.0 / 512.0
    keep[...] = (acc[:, core[0]] * scale).reshape(keep.shape)
    give[...] = (acc[:, 1 - core[0]] * scale).reshape(give.shape).astype(BF16)


def gradient_kernel(
    core, fill, cot, taken, inner, up, keys, cols, ro, gi, pair, starts, push_out, gains, enter,
    keep, give, acc_in, acc_out, left, right, masked, took, finish, matrix,
):
    step = pl.program_id(0)
    last = pl.num_programs(0) - 1

    @pl.when(step == 0)
    def _():
        matrix[...] = spread_matrix()
        finish[...] = enter[64:].astype(F32)
        acc_in[...] = jnp.zeros_like(acc_in)
        acc_out[...] = jnp.zeros_like(acc_out)

    at = pl.ds(pl.multiple_of((step & 1) * BLOCK, BLOCK), BLOCK)
    factor, before = gains[0, 0:1], gains[0, 8:9]
    start = (starts[0] + before * enter[:64].astype(F32)).astype(BF16)
    end = finish[...].astype(BF16)
    finish[...] = finish[...] * factor + push_out[0]
    table = cols[...]
    opening = spread(table, OPEN, matrix[...])
    closing = spread(table, CLOSE, matrix[...])
    k = keys[...]
    write, read = k[:, :STATE], k[:, STATE:]
    left[at] = (ro[...].astype(F32) + opening * mm(read, start)).astype(BF16)
    masked[at] = jnp.where(valid_rows(fill[last - step], D), cot[0], jnp.zeros((), BF16))
    took[at] = taken[...]
    right[at, :D] = (gi[...].astype(F32) + closing * mm(write, end)).astype(BF16)
    into = (closing * inner[...].astype(F32)).astype(BF16)
    out = (opening * up[...].astype(F32)).astype(BF16)
    g = pair[0]
    grad_write = mm(g, read, TN) + mm(into, end, NT)
    grad_read = mm(g, write) + mm(out, start, NT)
    right[at, D:] = jnp.concatenate([grad_write, grad_read], axis=1).astype(BF16)

    @pl.when((step & 1) == 1)
    def _():
        acc_out[...] += mm(left[...], masked[...], TN)
        acc_in[...] += mm(took[...], right[...], TN)

    @pl.when(step == last)
    def _():
        scale = 1.0 / 512.0
        for acc, columns in ((acc_in, slice(0, D + 128)), (acc_out, slice(D + 128, None))):
            halves = acc.reshape(D // 16, 2, 8, acc.shape[1])
            mine, other = halves[:, core[0]] * scale, halves[:, 1 - core[0]] * scale
            keep[:, columns] = mine.reshape(keep.shape[0], -1)
            give[:, columns] = other.reshape(give.shape[0], -1).astype(BF16)


def ring(axis, by):
    size = lax.axis_size(axis)
    return [(k, (k + by) % size) for k in range(size)]


CHIPS = ("y", "x", "z")


def over_chip(keep, give):
    got = lax.ppermute(give, "c", ring("c", 1))
    half = (keep + got.astype(F32)).astype(BF16)
    return half.reshape(lax.axis_size(CHIPS), 8, -1)


def over_chips(half):
    return lax.all_to_all(half, CHIPS, 0, 0).astype(F32).sum(0)


def on_device(
    replay, block_owner, block_slot, block_fill, log_decay, resets, cotangent, w_in, w_bc, w_out
):
    shards = lax.axis_size(TM)
    core, z = lax.axis_index("c"), lax.axis_index("z")
    my_lane = z * 2 + core
    blocks = block_fill.shape[2]
    steps = blocks * BLOCK
    fill = block_fill[0, 0]
    owner = lax.dynamic_index_in_dim(block_owner[0, :, :, 0], my_lane, 0, keepdims=False)
    slot = lax.dynamic_index_in_dim(block_slot[0], my_lane, 0, keepdims=False)

    mine = replay[0, 0].reshape(BUFCH, BLOCK, D)
    swap = lambda v: lax.ppermute(v, "c", ring("c", 1))
    up_z = lambda v: lax.ppermute(v, "z", ring("z", 1))
    down_z = lambda v: lax.ppermute(v, "z", ring("z", -1))
    first, second = mine[:2], mine[2:]
    below_a, above_a = up_z(first), down_z(second)
    other = swap(mine)
    away = (owner // 2 - z) % 4
    same = owner % 2 == core
    low = slot < 2
    stage = jnp.where(away == 0, 0, jnp.where(away == 2, 2, 1))
    side = jnp.where(away == 2, jnp.where(low, 0, 1), jnp.where(away == 3, 0, 1))
    late = (away % 2 == 1) & ((away == 3) != low)
    source = jnp.where(away == 0, 0, side + jnp.where(late, 4, 0)) + jnp.where(
        same, 0, jnp.where(away == 0, 1, 2)
    )
    index = jnp.where(away == 0, slot, slot % 2)
    ids = jnp.arange(blocks)
    rank = jnp.sum((stage[None] == stage[:, None]) & (ids[None] < ids[:, None]), axis=1)
    counts = jnp.sum(stage[None] == jnp.arange(3)[:, None], axis=1)
    most = (4, blocks, 4)
    turn = jnp.minimum(jnp.arange(blocks)[None], counts[:, None] - 1)
    chosen = (stage[None, None] == jnp.arange(3)[:, None, None]) & (rank[None, None] == turn[:, :, None])
    of = lambda v: jnp.sum(jnp.where(chosen, v[None, None], 0), axis=2)
    block = jnp.where(counts[:, None] > 0, of(ids), blocks).astype(jnp.int32)
    source, index = of(source).astype(jnp.int32), of(index).astype(jnp.int32)
    counts = counts.astype(jnp.int32)

    whole = lambda *dims: pl.BlockSpec(dims, lambda b, *_: (0,) * len(dims))
    tall = lambda width: pl.BlockSpec((BLOCK, width), lambda b, *_: (b, 0))
    lead = lambda *dims: pl.BlockSpec((1, *dims), lambda b, *_: (b,) + (0,) * len(dims))
    table_rows = pl.BlockSpec((32, BLOCK), lambda b, *_: (0, b))
    vmem = lambda kind, *dims: pltpu.VMEM(dims, kind)

    up, rows, cols, ends = call(
        upstream_kernel,
        "upstream",
        (
            shape((steps, D), BF16),
            shape((32, steps), F32),
            shape((steps, 128), F32),
            shape((blocks, 8, 128), F32),
        ),
        pltpu.PrefetchScalarGridSpec(
            num_scalar_prefetch=1,
            grid=(blocks,),
            in_specs=[
                pl.BlockSpec((HEADS, BLOCK), lambda b, *_: (0, b)),
                pl.BlockSpec((1, 1, BLOCK), lambda b, *_: (b, 0, 0)),
                pl.BlockSpec((1, BLOCK, D), lambda b, *_: (0, b, 0)),
                whole(D, D),
            ],
            out_specs=[tall(D), table_rows, tall(128), lead(8, 128)],
        ),
        2 * steps * D * D,
        12 << 20,
    )(fill, log_decay[0], resets.reshape(blocks, 1, BLOCK), cotangent, w_out)

    room = steps + BLOCK
    made = None
    for s in range(3):
        if s == 0:
            below_a, above_a, second, first, up = lax.optimization_barrier(
                (below_a, above_a, second, first, up)
            )
            below_b, above_b = up_z(second), down_z(first)
            sources, near = (mine, other), (below_a, above_a, swap(below_a), swap(above_a))
        elif s == 1:
            below_b, above_b, below_a, above_a, made = lax.optimization_barrier(
                (below_b, above_b, below_a, above_a, made)
            )
            far_low, far_high = up_z(below_a), down_z(above_a)
            sources = (*near, below_b, above_b, swap(below_b), swap(above_b))
        else:
            far_low, far_high, made = lax.optimization_barrier((far_low, far_high, made))
            sources = (far_low, far_high, swap(far_low), swap(far_high))
        number = len(sources)
        at = lambda i, block, *_: block[i]
        inside_at = lambda i, block, *_: jnp.minimum(block[i], blocks - 1)
        out_rows = lambda width: pl.BlockSpec((BLOCK, width), lambda i, block, *_: (block[i], 0))
        out_lead = lambda *dims: pl.BlockSpec((1, *dims), lambda i, block, *_: (block[i], 0, 0))
        in_rows = lambda width: pl.BlockSpec(
            (BLOCK, width), lambda i, block, *_: (jnp.minimum(block[i], blocks - 1), 0)
        )
        pick = lambda n: pl.BlockSpec(
            (pl.squeezed, BLOCK, D),
            lambda i, block, source, index, *_: (jnp.where(source[i] == n, index[i], 0), 0, 0),
        )
        kept = [] if made is None else list(made)
        body = lambda block, source, index, fill, count, *refs, number=number: stage_kernel(
            count, number, block, source, index, fill, *refs
        )
        made = pl.pallas_call(
            body,
            out_shape=(
                shape((room, D), BF16),
                shape((room, D), BF16),
                shape((room, 128), BF16),
                shape((room, D), BF16),
                shape((room, D), BF16),
                shape((blocks + 1, BLOCK, BLOCK), BF16),
                shape((blocks + 1, STATE, D), F32),
                shape((blocks + 1, STATE, D), F32),
            ),
            grid_spec=pltpu.PrefetchScalarGridSpec(
                num_scalar_prefetch=5,
                grid=(most[s],),
                in_specs=[pick(n) for n in range(number)]
                + [
                    whole(D, D),
                    whole(D, 128),
                    in_rows(D),
                    pl.BlockSpec((32, BLOCK), lambda i, block, *_: (0, jnp.minimum(block[i], blocks - 1))),
                    in_rows(128),
                ]
                + [pl.BlockSpec(memory_space=pl.ANY)] * len(kept),
                out_specs=[
                    out_rows(D),
                    out_rows(D),
                    out_rows(128),
                    out_rows(D),
                    out_rows(D),
                    out_lead(BLOCK, BLOCK),
                    out_lead(STATE, D),
                    out_lead(STATE, D),
                ],
                scratch_shapes=[vmem(BF16, 256, D)],
            ),
            input_output_aliases={5 + number + 5 + n: n for n in range(len(kept))},
            name=f"stage_{s}",
            compiler_params=pltpu.CompilerParams(vmem_limit_bytes=32 * MIB),
            cost_estimate=pl.CostEstimate(
                flops=4 * BLOCK * D * (D + 1024) + 4 * HEADS * 3 * BLOCK**3,
                bytes_accessed=16 << 20,
                transcendentals=0,
            ),
        )(block[s], source[s], index[s], fill, counts[s : s + 1], *sources, w_in, w_bc, up, rows, cols, *kept)
    taken, inner, keys, ro, gi, pair, push_in, push_out = made

    some = lambda *dims: pl.BlockSpec((blocks // 2, *dims), lambda b, *_: (b, 0, 0))
    starts, gains, total = call(
        local_kernel,
        "local",
        (shape((blocks, STATE, D), F32), shape((blocks, 16, D), F32), shape((shards, 16, D), BF16)),
        pl.GridSpec(
            grid=(2,),
            in_specs=[some(STATE, D), some(STATE, D), whole(blocks, 8, 128)],
            out_specs=[some(STATE, D), some(16, D), whole(shards, 16, D)],
            scratch_shapes=[vmem(F32, blocks * 8, D), vmem(F32, 136, D)],
        ),
        1 << 24,
        7 << 20,
    )(push_in, push_out, ends)

    terms = lax.all_to_all(total, TM, 0, 0)
    entering = call(
        scan_kernel,
        "scan",
        shape((shards, 8, D), BF16),
        pltpu.PrefetchScalarGridSpec(
            num_scalar_prefetch=1,
            grid=(1,),
            in_specs=[whole(shards, 16, D)],
            out_specs=whole(shards, 8, D),
            scratch_shapes=[vmem(F32, shards, 8, D)],
        ),
        1 << 20,
        1 << 20,
    )(lax.axis_index(TM).reshape(1), terms)
    enter = lax.all_to_all(entering, TM, 0, 0).reshape(128, D)

    own_core = core.reshape(1)
    back = lambda spec: pl.BlockSpec(
        spec.block_shape, lambda s, *refs: spec.index_map(blocks - 1 - s, *refs)
    )
    wide = D + 128
    both = wide + D
    keep, give = call(
        gradient_kernel,
        "gradient",
        (shape((D // 2, both), F32), shape((D // 2, both), BF16)),
        pltpu.PrefetchScalarGridSpec(
            num_scalar_prefetch=2,
            grid=(blocks,),
            in_specs=[
                back(s)
                for s in (
                    pl.BlockSpec((1, BLOCK, D), lambda b, *_: (0, b, 0)),
                    tall(D),
                    tall(D),
                    tall(D),
                    tall(128),
                    tall(128),
                    tall(D),
                    tall(D),
                    lead(BLOCK, BLOCK),
                    lead(STATE, D),
                    lead(STATE, D),
                    lead(16, D),
                    whole(128, D),
                )
            ],
            out_specs=[whole(D // 2, both), whole(D // 2, both)],
            scratch_shapes=[
                vmem(F32, D, wide),
                vmem(F32, D, D),
                vmem(BF16, 2 * BLOCK, D),
                vmem(BF16, 2 * BLOCK, wide),
                vmem(BF16, 2 * BLOCK, D),
                vmem(BF16, 2 * BLOCK, D),
                vmem(F32, STATE, D),
                vmem(BF16, 256, D),
            ],
        ),
        2 * steps * D * (2 * D + 1280),
        36 << 20,
        room=GRADIENT_ROOM,
    )(own_core, fill, cotangent, taken, inner, up, keys, cols, ro, gi, pair, starts, push_out, gains, enter)

    grads = over_chips(over_chip(keep, give))
    return (grads[:, :D], grads[:, D:wide], grads[:, wide:])


def solution(mesh):
    torus = Mesh(mesh.devices.reshape(4, 4, 4, 2), ("y", "x", "z", "c"))
    lane = ("z", "c")
    every = TM + lane
    return jax.shard_map(
        on_device,
        mesh=torus,
        in_specs=(
            P(lane, TM, None, None),
            P(TM, None, None, None),
            P(TM, None, None),
            P(lane, TM, None),
            P(lane, None, TM),
            P(lane, TM),
            P(lane, TM, None),
            P(),
            P(),
            P(),
        ),
        out_specs=(P(every, None), P(every, None), P(every, None)),
        check_vma=False,
    )
```

```python
import math

import jax
import jax.numpy as jnp
from jax import lax
from jax.experimental import pallas as pl
from jax.experimental.pallas import tpu as pltpu
from jax.sharding import Mesh
from jax.sharding import PartitionSpec as P

D = 1024
HEAD = 64
HEADS = 16
STATE = 64
BLOCK = 256
BUFCH = 4
TM = ("y", "x")
LOG2E = math.log2(math.e)
FAR = -1e4
F32, BF16 = jnp.float32, jnp.bfloat16
CNT, OPEN, CLOSE = 16, 32, 48
NT = (((1,), (1,)), ((), ()))
TN = (((0,), (0,)), ((), ()))
NN = (((1,), (0,)), ((), ()))
MIB = 1024 * 1024
GRADIENT_ROOM = 56


def mm(a, b, dims=NN):
    return lax.dot_general(a, b, dims, preferred_element_type=F32)


def split(x):
    high = x.astype(BF16)
    return jnp.concatenate([high, (x - high.astype(F32)).astype(BF16)], axis=1)


def spread_matrix():
    row = lax.broadcasted_iota(jnp.int32, (2 * 128, D), 0) & 127
    head = lax.broadcasted_iota(jnp.int32, (2 * 128, D), 1) >> 6
    return jnp.where(row == head, 1.0, 0.0).astype(BF16)


def spread(table, base, matrix):
    return mm(split(pltpu.roll(table, 128 - base, 1)), matrix)


def call(kernel, name, out_shape, grid_spec, flops, nbytes, room=24):
    return pl.pallas_call(
        kernel,
        out_shape=out_shape,
        grid_spec=grid_spec,
        name=name,
        compiler_params=pltpu.CompilerParams(vmem_limit_bytes=room * MIB),
        cost_estimate=pl.CostEstimate(flops=flops, bytes_accessed=nbytes, transcendentals=0),
    )


def shape(dims, kind):
    return jax.ShapeDtypeStruct(dims, kind)


def valid_rows(fill, width):
    return lax.broadcasted_iota(jnp.int32, (BLOCK, width), 0) < fill


def upstream_kernel(fill, decay, resets, cot, w_out, up, rows, cols, ends):
    b = pl.program_id(0)
    upper = lax.broadcasted_iota(jnp.int32, (BLOCK, BLOCK), 0) <= lax.broadcasted_iota(
        jnp.int32, (BLOCK, BLOCK), 1
    )
    upper = jnp.where(upper, 1.0, 0.0)
    both = jnp.concatenate(
        [decay[...] * LOG2E, jnp.broadcast_to(resets[0].astype(F32), (8, BLOCK))], axis=0
    )
    summed = lax.dot_general(
        both, upper, NN, precision=lax.Precision.HIGHEST, preferred_element_type=F32
    )
    cum, count = summed[:HEADS], summed[HEADS : HEADS + 8]
    two = jnp.concatenate([count, count], axis=0)
    opening = jnp.where(two == 0.0, jnp.exp2(cum), 0.0)
    last = jnp.broadcast_to(cum[:, BLOCK - 1 :], (HEADS, BLOCK))
    last_two = jnp.broadcast_to(two[:, BLOCK - 1 :], (HEADS, BLOCK))
    closing = jnp.where(two == last_two, jnp.exp2(last - cum), 0.0)
    table = jnp.concatenate(
        [cum, two, opening, closing, jnp.zeros((64, BLOCK), F32)], axis=0
    )
    rows[...] = table[:32]
    turned = table.T
    cols[...] = turned
    ends[0] = jnp.broadcast_to(turned[BLOCK - 1 :], (8, 128))
    masked = jnp.where(valid_rows(fill[b], D), cot[0], jnp.zeros((), BF16))
    up[...] = mm(masked, w_out[...], NT).astype(BF16)


def inside(inner, keys, up, rows, cols, ro, gi, pair):
    half = BLOCK // 2
    at = lax.broadcasted_iota(jnp.int32, (BLOCK, BLOCK), 0)
    to = lax.broadcasted_iota(jnp.int32, (BLOCK, BLOCK), 1)
    linked = (to <= at) & (cols[:, CNT : CNT + 1] == rows[CNT : CNT + 1, :])
    bias = jnp.where(linked, 0.0, FAR)
    k = keys[...]
    scores = mm(k[:, STATE:], k[:, :STATE], NT)
    bias_a, bias_b = bias[:half, :half], bias[half:]
    scores_a, scores_b = scores[:half, :half], scores[half:]
    left = lax.broadcasted_iota(jnp.int32, (BLOCK, 128), 1) < HEAD
    zero = jnp.zeros((), BF16)
    turned = up[...].T
    paired_a, paired_b = jnp.zeros((half, half), F32), jnp.zeros((half, BLOCK), F32)
    for q in range(HEADS // 2):
        lanes = slice(128 * q, 128 * q + 128)
        x, u = inner[:, lanes], up[:, lanes]
        grads = []
        for s in range(2):
            h = 2 * q + s
            mine = left if s == 0 else ~left
            xs, us = jnp.where(mine, x, zero), jnp.where(mine, u, zero)
            decays_a = jnp.exp2(cols[:half, h : h + 1] - rows[h : h + 1, :half] + bias_a)
            decays_b = jnp.exp2(cols[half:, h : h + 1] - rows[h : h + 1, :] + bias_b)
            mixing_a, mixing_b = (decays_a * scores_a).astype(BF16), (decays_b * scores_b).astype(BF16)
            paired_a = paired_a + decays_a * mm(us[:half], x[:half], NT)
            paired_b = paired_b + decays_b * mm(us[half:], x, NT)
            a, b = mm(mixing_a, xs[:half]), mm(mixing_b, xs)
            readout_a, readout_b = (a, b) if s == 0 else (readout_a + a, readout_b + b)
            head = turned[HEAD * h : HEAD * h + HEAD]
            g = mm(head[:, half:], mixing_b)
            grads.append(jnp.concatenate([g[:, :half] + mm(head[:, :half], mixing_a), g[:, half:]], axis=1))
        ro[:half, lanes] = readout_a.astype(BF16)
        ro[half:, lanes] = readout_b.astype(BF16)
        gi[:, lanes] = jnp.concatenate(grads, axis=0).astype(BF16).T
    pair[0, :half, :half] = paired_a.astype(BF16)
    pair[0, :half, half:] = jnp.zeros((half, half), BF16)
    pair[0, half:] = paired_b.astype(BF16)


def stage_kernel(count, number, block, source, index, fill, *refs):
    picks = refs[:number]
    w_in, w_bc, up, rows, cols = refs[number : number + 5]
    outs = refs[-9:]
    taken, inner, keys, ro, gi, pair, push_in, push_out, matrix = outs
    i = pl.program_id(0)

    @pl.when(i == 0)
    def _():
        matrix[...] = spread_matrix()

    @pl.when(i < count[0])
    def _():
        valid = valid_rows(fill[jnp.minimum(block[i], fill.shape[0] - 1)], D)
        for n in range(number):

            @pl.when(source[i] == n)
            def _(n=n):
                taken[...] = jnp.where(valid, picks[n][...], jnp.zeros((), BF16))

        got = taken[...]
        x = mm(got, w_in[...]).astype(BF16)
        k = mm(got, w_bc[...]).astype(BF16)
        inner[...] = x
        keys[...] = k
        table = cols[...]
        opening = spread(table, OPEN, matrix[...])
        closing = spread(table, CLOSE, matrix[...])
        into = (closing * x.astype(F32)).astype(BF16)
        out = (opening * up[...].astype(F32)).astype(BF16)
        turned = k.astype(F32).T.astype(BF16)
        push_in[0] = mm(turned[:STATE], into)
        push_out[0] = mm(turned[STATE:], out)
        inside(inner, keys, up, rows, cols, ro, gi, pair)


def local_kernel(push_in, push_out, ends, starts, gains, total, factors, state):
    b = pl.program_id(0)

    @pl.when(b == 0)
    def _():
        table = ends[...].reshape(factors.shape[0], 128)
        factors[...] = spread(table, OPEN, spread_matrix())
        state[:128] = jnp.zeros((128, D), F32)
        state[128:] = jnp.ones((8, D), F32)

    each = starts.shape[0]
    for n in range(each):
        factor = factors[pl.ds((b * each + n) * 8, 8)]
        before = state[128:]
        starts[n] = state[:64]
        gains[n] = jnp.concatenate([factor, before], axis=0)
        state[:64] = state[:64] * factor[:1] + push_in[n]
        state[64:128] = state[64:128] + before[:1] * push_out[n]
        state[128:] = before * factor

    @pl.when(b == pl.num_programs(0) - 1)
    def _():
        gain = state[128:]
        high = gain.astype(BF16).astype(F32)
        top = lax.broadcasted_iota(jnp.int32, gain.shape, 0) == 0
        gain = jnp.where(top, high, gain - high)
        for n in range(total.shape[0]):
            total[n] = jnp.concatenate([state[8 * n : 8 * n + 8], gain], axis=0).astype(BF16)


def scan_kernel(which, terms, entering, forth):
    shards = terms.shape[0]
    part = lambda t: terms[t].astype(F32)
    gain = lambda v: v[8:9] + v[9:10]
    state = jnp.zeros((8, D), F32)
    for t in range(shards):
        forth[t] = state
        v = part(t)
        state = state * gain(v) + v[:8]
    back = jnp.zeros((8, D), F32)
    ahead = jnp.full((8, D), which[0], jnp.int32) < shards // 2
    for t in reversed(range(shards)):
        entering[t] = jnp.where(ahead, forth[t], back).astype(BF16)
        v = part(t)
        back = back * gain(v) + v[:8]


def store_halves(core, acc, keep, give):
    scale = 1.0 / 512.0
    keep[...] = (acc[:, core[0]] * scale).reshape(keep.shape)
    give[...] = (acc[:, 1 - core[0]] * scale).reshape(give.shape).astype(BF16)


def gradient_kernel(
    core, fill, cot, taken, inner, up, keys, cols, ro, gi, pair, starts, push_out, gains, enter,
    keep, give, acc_in, acc_out, left, right, masked, finish, matrix,
):
    step = pl.program_id(0)
    last = pl.num_programs(0) - 1

    @pl.when(step == 0)
    def _():
        matrix[...] = spread_matrix()
        finish[...] = enter[64:].astype(F32)
        acc_in[...] = jnp.zeros_like(acc_in)
        acc_out[...] = jnp.zeros_like(acc_out)

    for n in (1, 0):
        at = slice(n * BLOCK, n * BLOCK + BLOCK)
        factor, before = gains[n, 0:1], gains[n, 8:9]
        start = (starts[n] + before * enter[:64].astype(F32)).astype(BF16)
        end = finish[...].astype(BF16)
        finish[...] = finish[...] * factor + push_out[n]
        table = cols[at]
        opening = spread(table, OPEN, matrix[...])
        closing = spread(table, CLOSE, matrix[...])
        k = keys[at]
        write, read = k[:, :STATE], k[:, STATE:]
        left[at] = (ro[at].astype(F32) + opening * mm(read, start)).astype(BF16)
        masked[at] = jnp.where(valid_rows(fill[2 * (last - step) + n], D), cot[0, at], jnp.zeros((), BF16))
        right[at, :D] = (gi[at].astype(F32) + closing * mm(write, end)).astype(BF16)
        into = (closing * inner[at].astype(F32)).astype(BF16)
        out = (opening * up[at].astype(F32)).astype(BF16)
        g = pair[n]
        grad_write = mm(g, read, TN) + mm(into, end, NT)
        grad_read = mm(g, write) + mm(out, start, NT)
        right[at, D:] = jnp.concatenate([grad_write, grad_read], axis=1).astype(BF16)
    acc_out[...] += mm(left[...], masked[...], TN).reshape(acc_out.shape)
    acc_in[...] += mm(taken[...], right[...], TN).reshape(acc_in.shape)

    @pl.when(step == last)
    def _():
        scale = 1.0 / 512.0
        for acc, columns in ((acc_in, slice(0, D + 128)), (acc_out, slice(D + 128, None))):
            mine, other = acc[:, core[0]] * scale, acc[:, 1 - core[0]] * scale
            keep[:, columns] = mine.reshape(keep.shape[0], -1)
            give[:, columns] = other.reshape(give.shape[0], -1).astype(BF16)


def ring(axis, by):
    size = lax.axis_size(axis)
    return [(k, (k + by) % size) for k in range(size)]


CHIPS = ("y", "x", "z")


def over_chip(keep, give):
    got = lax.ppermute(give, "c", ring("c", 1))
    half = (keep + got.astype(F32)).astype(BF16)
    return half.reshape(lax.axis_size(CHIPS), 8, -1)


def over_chips(half):
    return lax.all_to_all(half, CHIPS, 0, 0).astype(F32).sum(0)


def on_device(
    replay, block_owner, block_slot, block_fill, log_decay, resets, cotangent, w_in, w_bc, w_out
):
    shards = lax.axis_size(TM)
    core, z = lax.axis_index("c"), lax.axis_index("z")
    my_lane = z * 2 + core
    blocks = block_fill.shape[2]
    steps = blocks * BLOCK
    fill = block_fill[0, 0]
    owner = lax.dynamic_index_in_dim(block_owner[0, :, :, 0], my_lane, 0, keepdims=False)
    slot = lax.dynamic_index_in_dim(block_slot[0], my_lane, 0, keepdims=False)

    mine = replay[0, 0].reshape(BUFCH, BLOCK, D)
    swap = lambda v: lax.ppermute(v, "c", ring("c", 1))
    up_z = lambda v: lax.ppermute(v, "z", ring("z", 1))
    down_z = lambda v: lax.ppermute(v, "z", ring("z", -1))
    first, second = mine[:2], mine[2:]
    below_a, above_a = up_z(first), down_z(second)
    other = swap(mine)
    away = (owner // 2 - z) % 4
    same = owner % 2 == core
    low = slot < 2
    stage = jnp.where(away == 0, 0, jnp.where(away == 2, 2, 1))
    side = jnp.where(away == 2, jnp.where(low, 0, 1), jnp.where(away == 3, 0, 1))
    late = (away % 2 == 1) & ((away == 3) != low)
    source = jnp.where(away == 0, 0, side + jnp.where(late, 4, 0)) + jnp.where(
        same, 0, jnp.where(away == 0, 1, 2)
    )
    index = jnp.where(away == 0, slot, slot % 2)
    ids = jnp.arange(blocks)
    rank = jnp.sum((stage[None] == stage[:, None]) & (ids[None] < ids[:, None]), axis=1)
    counts = jnp.sum(stage[None] == jnp.arange(3)[:, None], axis=1)
    most = (4, blocks, 4)
    turn = jnp.minimum(jnp.arange(blocks)[None], counts[:, None] - 1)
    chosen = (stage[None, None] == jnp.arange(3)[:, None, None]) & (rank[None, None] == turn[:, :, None])
    of = lambda v: jnp.sum(jnp.where(chosen, v[None, None], 0), axis=2)
    block = jnp.where(counts[:, None] > 0, of(ids), blocks).astype(jnp.int32)
    source, index = of(source).astype(jnp.int32), of(index).astype(jnp.int32)
    counts = counts.astype(jnp.int32)

    whole = lambda *dims: pl.BlockSpec(dims, lambda b, *_: (0,) * len(dims))
    tall = lambda width: pl.BlockSpec((BLOCK, width), lambda b, *_: (b, 0))
    lead = lambda *dims: pl.BlockSpec((1, *dims), lambda b, *_: (b,) + (0,) * len(dims))
    table_rows = pl.BlockSpec((32, BLOCK), lambda b, *_: (0, b))
    vmem = lambda kind, *dims: pltpu.VMEM(dims, kind)

    up, rows, cols, ends = call(
        upstream_kernel,
        "upstream",
        (
            shape((steps, D), BF16),
            shape((32, steps), F32),
            shape((steps, 128), F32),
            shape((blocks, 8, 128), F32),
        ),
        pltpu.PrefetchScalarGridSpec(
            num_scalar_prefetch=1,
            grid=(blocks,),
            in_specs=[
                pl.BlockSpec((HEADS, BLOCK), lambda b, *_: (0, b)),
                pl.BlockSpec((1, 1, BLOCK), lambda b, *_: (b, 0, 0)),
                pl.BlockSpec((1, BLOCK, D), lambda b, *_: (0, b, 0)),
                whole(D, D),
            ],
            out_specs=[tall(D), table_rows, tall(128), lead(8, 128)],
        ),
        2 * steps * D * D,
        12 << 20,
    )(fill, log_decay[0], resets.reshape(blocks, 1, BLOCK), cotangent, w_out)

    room = steps + BLOCK
    made = None
    for s in range(3):
        if s == 0:
            below_a, above_a, second, first, up = lax.optimization_barrier(
                (below_a, above_a, second, first, up)
            )
            below_b, above_b = up_z(second), down_z(first)
            sources, near = (mine, other), (below_a, above_a, swap(below_a), swap(above_a))
        elif s == 1:
            below_b, above_b, below_a, above_a, made = lax.optimization_barrier(
                (below_b, above_b, below_a, above_a, made)
            )
            far_low, far_high = up_z(below_a), down_z(above_a)
            sources = (*near, below_b, above_b, swap(below_b), swap(above_b))
        else:
            far_low, far_high, made = lax.optimization_barrier((far_low, far_high, made))
            sources = (far_low, far_high, swap(far_low), swap(far_high))
        number = len(sources)
        at = lambda i, block, *_: block[i]
        inside_at = lambda i, block, *_: jnp.minimum(block[i], blocks - 1)
        out_rows = lambda width: pl.BlockSpec((BLOCK, width), lambda i, block, *_: (block[i], 0))
        out_lead = lambda *dims: pl.BlockSpec((1, *dims), lambda i, block, *_: (block[i], 0, 0))
        in_rows = lambda width: pl.BlockSpec(
            (BLOCK, width), lambda i, block, *_: (jnp.minimum(block[i], blocks - 1), 0)
        )
        pick = lambda n: pl.BlockSpec(
            (pl.squeezed, BLOCK, D),
            lambda i, block, source, index, *_: (jnp.where(source[i] == n, index[i], 0), 0, 0),
        )
        kept = [] if made is None else list(made)
        body = lambda block, source, index, fill, count, *refs, number=number: stage_kernel(
            count, number, block, source, index, fill, *refs
        )
        made = pl.pallas_call(
            body,
            out_shape=(
                shape((room, D), BF16),
                shape((room, D), BF16),
                shape((room, 128), BF16),
                shape((room, D), BF16),
                shape((room, D), BF16),
                shape((blocks + 1, BLOCK, BLOCK), BF16),
                shape((blocks + 1, STATE, D), F32),
                shape((blocks + 1, STATE, D), F32),
            ),
            grid_spec=pltpu.PrefetchScalarGridSpec(
                num_scalar_prefetch=5,
                grid=(most[s],),
                in_specs=[pick(n) for n in range(number)]
                + [
                    whole(D, D),
                    whole(D, 128),
                    in_rows(D),
                    pl.BlockSpec((32, BLOCK), lambda i, block, *_: (0, jnp.minimum(block[i], blocks - 1))),
                    in_rows(128),
                ]
                + [pl.BlockSpec(memory_space=pl.ANY)] * len(kept),
                out_specs=[
                    out_rows(D),
                    out_rows(D),
                    out_rows(128),
                    out_rows(D),
                    out_rows(D),
                    out_lead(BLOCK, BLOCK),
                    out_lead(STATE, D),
                    out_lead(STATE, D),
                ],
                scratch_shapes=[vmem(BF16, 256, D)],
            ),
            input_output_aliases={5 + number + 5 + n: n for n in range(len(kept))},
            name=f"stage_{s}",
            compiler_params=pltpu.CompilerParams(vmem_limit_bytes=32 * MIB),
            cost_estimate=pl.CostEstimate(
                flops=4 * BLOCK * D * (D + 1024) + 4 * HEADS * 3 * BLOCK**3,
                bytes_accessed=16 << 20,
                transcendentals=0,
            ),
        )(block[s], source[s], index[s], fill, counts[s : s + 1], *sources, w_in, w_bc, up, rows, cols, *kept)
    taken, inner, keys, ro, gi, pair, push_in, push_out = made

    some = lambda *dims: pl.BlockSpec((blocks // 2, *dims), lambda b, *_: (b, 0, 0))
    starts, gains, total = call(
        local_kernel,
        "local",
        (shape((blocks, STATE, D), F32), shape((blocks, 16, D), F32), shape((shards, 16, D), BF16)),
        pl.GridSpec(
            grid=(2,),
            in_specs=[some(STATE, D), some(STATE, D), whole(blocks, 8, 128)],
            out_specs=[some(STATE, D), some(16, D), whole(shards, 16, D)],
            scratch_shapes=[vmem(F32, blocks * 8, D), vmem(F32, 136, D)],
        ),
        1 << 24,
        7 << 20,
    )(push_in, push_out, ends)

    terms = lax.all_to_all(total, TM, 0, 0)
    entering = call(
        scan_kernel,
        "scan",
        shape((shards, 8, D), BF16),
        pltpu.PrefetchScalarGridSpec(
            num_scalar_prefetch=1,
            grid=(1,),
            in_specs=[whole(shards, 16, D)],
            out_specs=whole(shards, 8, D),
            scratch_shapes=[vmem(F32, shards, 8, D)],
        ),
        1 << 20,
        1 << 20,
    )(lax.axis_index(TM).reshape(1), terms)
    enter = lax.all_to_all(entering, TM, 0, 0).reshape(128, D)

    own_core = core.reshape(1)
    two = lambda width: pl.BlockSpec((2 * BLOCK, width), lambda b, *_: (b, 0))
    pairs = lambda *dims: pl.BlockSpec((2, *dims), lambda b, *_: (b, 0, 0))
    back = lambda spec: pl.BlockSpec(
        spec.block_shape, lambda s, *refs: spec.index_map(blocks // 2 - 1 - s, *refs)
    )
    wide = D + 128
    both = wide + D
    keep, give = call(
        gradient_kernel,
        "gradient",
        (shape((D // 2, both), F32), shape((D // 2, both), BF16)),
        pltpu.PrefetchScalarGridSpec(
            num_scalar_prefetch=2,
            grid=(blocks // 2,),
            in_specs=[
                back(s)
                for s in (
                    pl.BlockSpec((1, 2 * BLOCK, D), lambda b, *_: (0, b, 0)),
                    two(D),
                    two(D),
                    two(D),
                    two(128),
                    two(128),
                    two(D),
                    two(D),
                    pairs(BLOCK, BLOCK),
                    pairs(STATE, D),
                    pairs(STATE, D),
                    pairs(16, D),
                    whole(128, D),
                )
            ],
            out_specs=[whole(D // 2, both), whole(D // 2, both)],
            scratch_shapes=[
                vmem(F32, D // 16, 2, 8, wide),
                vmem(F32, D // 16, 2, 8, D),
                vmem(BF16, 2 * BLOCK, D),
                vmem(BF16, 2 * BLOCK, wide),
                vmem(BF16, 2 * BLOCK, D),
                vmem(F32, STATE, D),
                vmem(BF16, 256, D),
            ],
        ),
        2 * steps * D * (2 * D + 1280),
        36 << 20,
        room=GRADIENT_ROOM,
    )(own_core, fill, cotangent, taken, inner, up, keys, cols, ro, gi, pair, starts, push_out, gains, enter)

    grads = over_chips(over_chip(keep, give))
    return (grads[:, :D], grads[:, D:wide], grads[:, wide:])


def solution(mesh):
    torus = Mesh(mesh.devices.reshape(4, 4, 4, 2), ("y", "x", "z", "c"))
    lane = ("z", "c")
    every = TM + lane
    return jax.shard_map(
        on_device,
        mesh=torus,
        in_specs=(
            P(lane, TM, None, None),
            P(TM, None, None, None),
            P(TM, None, None),
            P(lane, TM, None),
            P(lane, None, TM),
            P(lane, TM),
            P(lane, TM, None),
            P(),
            P(),
            P(),
        ),
        out_specs=(P(every, None), P(every, None), P(every, None)),
        check_vma=False,
    )
```

```python
import math

import jax
import jax.numpy as jnp
from jax import lax
from jax.experimental import pallas as pl
from jax.experimental.pallas import tpu as pltpu
from jax.sharding import Mesh
from jax.sharding import PartitionSpec as P

D = 1024
HEAD = 64
HEADS = 16
STATE = 64
BLOCK = 256
BUFCH = 4
TM = ("y", "x")
LOG2E = math.log2(math.e)
FAR = -1e4
F32, BF16 = jnp.float32, jnp.bfloat16
CNT, OPEN, CLOSE = 16, 32, 48
NT = (((1,), (1,)), ((), ()))
TN = (((0,), (0,)), ((), ()))
NN = (((1,), (0,)), ((), ()))
MIB = 1024 * 1024
GRADIENT_ROOM = 56


def mm(a, b, dims=NN):
    return lax.dot_general(a, b, dims, preferred_element_type=F32)


def split(x):
    high = x.astype(BF16)
    return jnp.concatenate([high, (x - high.astype(F32)).astype(BF16)], axis=1)


def spread_matrix():
    row = lax.broadcasted_iota(jnp.int32, (2 * 128, D), 0) & 127
    head = lax.broadcasted_iota(jnp.int32, (2 * 128, D), 1) >> 6
    return jnp.where(row == head, 1.0, 0.0).astype(BF16)


def spread(table, base, matrix):
    return mm(split(pltpu.roll(table, 128 - base, 1)), matrix)


def call(kernel, name, out_shape, grid_spec, flops, nbytes, room=24):
    return pl.pallas_call(
        kernel,
        out_shape=out_shape,
        grid_spec=grid_spec,
        name=name,
        compiler_params=pltpu.CompilerParams(vmem_limit_bytes=room * MIB),
        cost_estimate=pl.CostEstimate(flops=flops, bytes_accessed=nbytes, transcendentals=0),
    )


def shape(dims, kind):
    return jax.ShapeDtypeStruct(dims, kind)


def valid_rows(fill, width):
    return lax.broadcasted_iota(jnp.int32, (BLOCK, width), 0) < fill


def upstream_kernel(fill, decay, resets, cot, w_out, up, rows, cols, ends):
    b = pl.program_id(0)
    upper = lax.broadcasted_iota(jnp.int32, (BLOCK, BLOCK), 0) <= lax.broadcasted_iota(
        jnp.int32, (BLOCK, BLOCK), 1
    )
    upper = jnp.where(upper, 1.0, 0.0)
    both = jnp.concatenate(
        [decay[...] * LOG2E, jnp.broadcast_to(resets[0].astype(F32), (8, BLOCK))], axis=0
    )
    summed = lax.dot_general(
        both, upper, NN, precision=lax.Precision.HIGHEST, preferred_element_type=F32
    )
    cum, count = summed[:HEADS], summed[HEADS : HEADS + 8]
    two = jnp.concatenate([count, count], axis=0)
    opening = jnp.where(two == 0.0, jnp.exp2(cum), 0.0)
    last = jnp.broadcast_to(cum[:, BLOCK - 1 :], (HEADS, BLOCK))
    last_two = jnp.broadcast_to(two[:, BLOCK - 1 :], (HEADS, BLOCK))
    closing = jnp.where(two == last_two, jnp.exp2(last - cum), 0.0)
    table = jnp.concatenate(
        [cum, two, opening, closing, jnp.zeros((64, BLOCK), F32)], axis=0
    )
    rows[...] = table[:32]
    turned = table.T
    cols[...] = turned
    ends[0] = jnp.broadcast_to(turned[BLOCK - 1 :], (8, 128))
    masked = jnp.where(valid_rows(fill[b], D), cot[0], jnp.zeros((), BF16))
    up[...] = mm(masked, w_out[...], NT).astype(BF16)


def inside(inner, keys, up, rows, cols, ro, gi, pair):
    half = BLOCK // 2
    at = lax.broadcasted_iota(jnp.int32, (BLOCK, BLOCK), 0)
    to = lax.broadcasted_iota(jnp.int32, (BLOCK, BLOCK), 1)
    linked = (to <= at) & (cols[:, CNT : CNT + 1] == rows[CNT : CNT + 1, :])
    bias = jnp.where(linked, 0.0, FAR)
    k = keys[...]
    scores = mm(k[:, STATE:], k[:, :STATE], NT)
    bias_a, bias_b = bias[:half, :half], bias[half:]
    scores_a, scores_b = scores[:half, :half], scores[half:]
    left = lax.broadcasted_iota(jnp.int32, (BLOCK, 128), 1) < HEAD
    zero = jnp.zeros((), BF16)
    turned = up[...].T
    paired_a, paired_b = jnp.zeros((half, half), F32), jnp.zeros((half, BLOCK), F32)
    for q in range(HEADS // 2):
        lanes = slice(128 * q, 128 * q + 128)
        x, u = inner[:, lanes], up[:, lanes]
        grads = []
        for s in range(2):
            h = 2 * q + s
            mine = left if s == 0 else ~left
            xs, us = jnp.where(mine, x, zero), jnp.where(mine, u, zero)
            decays_a = jnp.exp2(cols[:half, h : h + 1] - rows[h : h + 1, :half] + bias_a)
            decays_b = jnp.exp2(cols[half:, h : h + 1] - rows[h : h + 1, :] + bias_b)
            mixing_a, mixing_b = (decays_a * scores_a).astype(BF16), (decays_b * scores_b).astype(BF16)
            paired_a = paired_a + decays_a * mm(us[:half], x[:half], NT)
            paired_b = paired_b + decays_b * mm(us[half:], x, NT)
            a, b = mm(mixing_a, xs[:half]), mm(mixing_b, xs)
            readout_a, readout_b = (a, b) if s == 0 else (readout_a + a, readout_b + b)
            head = turned[HEAD * h : HEAD * h + HEAD]
            g = mm(head[:, half:], mixing_b)
            grads.append(jnp.concatenate([g[:, :half] + mm(head[:, :half], mixing_a), g[:, half:]], axis=1))
        ro[:half, lanes] = readout_a.astype(BF16)
        ro[half:, lanes] = readout_b.astype(BF16)
        gi[:, lanes] = jnp.concatenate(grads, axis=0).astype(BF16).T
    pair[0, :half, :half] = paired_a.astype(BF16)
    pair[0, :half, half:] = jnp.zeros((half, half), BF16)
    pair[0, half:] = paired_b.astype(BF16)


def stage_kernel(count, number, block, source, index, fill, *refs):
    picks = refs[:number]
    w_in, w_bc, up, rows, cols = refs[number : number + 5]
    outs = refs[-9:]
    taken, inner, keys, ro, gi, pair, push_in, push_out, matrix = outs
    i = pl.program_id(0)

    @pl.when(i == 0)
    def _():
        matrix[...] = spread_matrix()

    @pl.when(i < count[0])
    def _():
        valid = valid_rows(fill[jnp.minimum(block[i], fill.shape[0] - 1)], D)
        for n in range(number):

            @pl.when(source[i] == n)
            def _(n=n):
                taken[...] = jnp.where(valid, picks[n][...], jnp.zeros((), BF16))

        got = taken[...]
        x = mm(got, w_in[...]).astype(BF16)
        k = mm(got, w_bc[...]).astype(BF16)
        inner[...] = x
        keys[...] = k
        table = cols[...]
        opening = spread(table, OPEN, matrix[...])
        closing = spread(table, CLOSE, matrix[...])
        into = (closing * x.astype(F32)).astype(BF16)
        out = (opening * up[...].astype(F32)).astype(BF16)
        turned = k.astype(F32).T.astype(BF16)
        push_in[0] = mm(turned[:STATE], into)
        push_out[0] = mm(turned[STATE:], out)
        inside(inner, keys, up, rows, cols, ro, gi, pair)


def local_kernel(push_in, push_out, ends, starts, gains, total, factors, state):
    b = pl.program_id(0)

    @pl.when(b == 0)
    def _():
        table = ends[...].reshape(factors.shape[0], 128)
        factors[...] = spread(table, OPEN, spread_matrix())
        state[:128] = jnp.zeros((128, D), F32)
        state[128:] = jnp.ones((8, D), F32)

    each = starts.shape[0]
    for n in range(each):
        factor = factors[pl.ds((b * each + n) * 8, 8)]
        before = state[128:]
        starts[n] = state[:64]
        gains[n] = jnp.concatenate([factor, before], axis=0)
        state[:64] = state[:64] * factor[:1] + push_in[n]
        state[64:128] = state[64:128] + before[:1] * push_out[n]
        state[128:] = before * factor

    @pl.when(b == pl.num_programs(0) - 1)
    def _():
        gain = state[128:129]
        high = gain.astype(BF16).astype(F32)
        cut = lambda v: [v[:, 128 * c : 128 * c + 128] for c in range(D // 128)]
        parts = cut(high) + cut(gain - high)
        for n in range(total.shape[0]):
            total[n] = jnp.concatenate(cut(state[8 * n : 8 * n + 8]) + parts, axis=0).astype(BF16)


def scan_kernel(which, terms, entering, forth):
    shards = terms.shape[0]
    part = lambda t: terms[t].astype(F32)
    chunks = range(D // 128)
    gain = lambda v: jnp.concatenate([v[64 + c : 65 + c] + v[72 + c : 73 + c] for c in chunks], axis=1)
    rows = lambda v: jnp.concatenate([v[8 * c : 8 * c + 8] for c in chunks], axis=1)
    state = jnp.zeros((8, D), F32)
    for t in range(shards):
        forth[t] = state
        v = part(t)
        state = state * gain(v) + rows(v)
    back = jnp.zeros((8, D), F32)
    ahead = jnp.full((8, D), which[0], jnp.int32) < shards // 2
    for t in reversed(range(shards)):
        entering[t] = jnp.where(ahead, forth[t], back).astype(BF16)
        v = part(t)
        back = back * gain(v) + rows(v)


def store_halves(core, acc, keep, give):
    scale = 1.0 / 512.0
    keep[...] = (acc[:, core[0]] * scale).reshape(keep.shape)
    give[...] = (acc[:, 1 - core[0]] * scale).reshape(give.shape).astype(BF16)


def gradient_kernel(
    core, fill, cot, taken, inner, up, keys, cols, ro, gi, pair, starts, push_out, gains, enter,
    keep, give, acc_in, acc_out, left, right, masked, finish, matrix,
):
    step = pl.program_id(0)
    last = pl.num_programs(0) - 1

    @pl.when(step == 0)
    def _():
        matrix[...] = spread_matrix()
        finish[...] = enter[64:].astype(F32)
        acc_in[...] = jnp.zeros_like(acc_in)
        acc_out[...] = jnp.zeros_like(acc_out)

    for n in (1, 0):
        at = slice(n * BLOCK, n * BLOCK + BLOCK)
        factor, before = gains[n, 0:1], gains[n, 8:9]
        start = (starts[n] + before * enter[:64].astype(F32)).astype(BF16)
        end = finish[...].astype(BF16)
        finish[...] = finish[...] * factor + push_out[n]
        table = cols[at]
        opening = spread(table, OPEN, matrix[...])
        closing = spread(table, CLOSE, matrix[...])
        k = keys[at]
        write, read = k[:, :STATE], k[:, STATE:]
        left[at] = (ro[at].astype(F32) + opening * mm(read, start)).astype(BF16)
        masked[at] = jnp.where(valid_rows(fill[2 * (last - step) + n], D), cot[0, at], jnp.zeros((), BF16))
        right[at, :D] = (gi[at].astype(F32) + closing * mm(write, end)).astype(BF16)
        into = (closing * inner[at].astype(F32)).astype(BF16)
        out = (opening * up[at].astype(F32)).astype(BF16)
        g = pair[n]
        grad_write = mm(g, read, TN) + mm(into, end, NT)
        grad_read = mm(g, write) + mm(out, start, NT)
        right[at, D:] = jnp.concatenate([grad_write, grad_read], axis=1).astype(BF16)
    acc_out[...] += mm(left[...], masked[...], TN).reshape(acc_out.shape)
    acc_in[...] += mm(taken[...], right[...], TN).reshape(acc_in.shape)

    @pl.when(step == last)
    def _():
        scale = 1.0 / 512.0
        for acc, columns in ((acc_in, slice(0, D + 128)), (acc_out, slice(D + 128, None))):
            mine, other = acc[:, core[0]] * scale, acc[:, 1 - core[0]] * scale
            keep[:, columns] = mine.reshape(keep.shape[0], -1)
            give[:, columns] = other.reshape(give.shape[0], -1).astype(BF16)


def ring(axis, by):
    size = lax.axis_size(axis)
    return [(k, (k + by) % size) for k in range(size)]


CHIPS = ("y", "x", "z")


def over_chip(keep, give):
    got = lax.ppermute(give, "c", ring("c", 1))
    half = (keep + got.astype(F32)).astype(BF16)
    return half.reshape(lax.axis_size(CHIPS), 8, -1)


def over_chips(half):
    return lax.all_to_all(half, CHIPS, 0, 0).astype(F32).sum(0)


def on_device(
    replay, block_owner, block_slot, block_fill, log_decay, resets, cotangent, w_in, w_bc, w_out
):
    shards = lax.axis_size(TM)
    core, z = lax.axis_index("c"), lax.axis_index("z")
    my_lane = z * 2 + core
    blocks = block_fill.shape[2]
    steps = blocks * BLOCK
    fill = block_fill[0, 0]
    owner = lax.dynamic_index_in_dim(block_owner[0, :, :, 0], my_lane, 0, keepdims=False)
    slot = lax.dynamic_index_in_dim(block_slot[0], my_lane, 0, keepdims=False)

    mine = replay[0, 0].reshape(BUFCH, BLOCK, D)
    swap = lambda v: lax.ppermute(v, "c", ring("c", 1))
    up_z = lambda v: lax.ppermute(v, "z", ring("z", 1))
    down_z = lambda v: lax.ppermute(v, "z", ring("z", -1))
    first, second = mine[:2], mine[2:]
    below_a, above_a = up_z(first), down_z(second)
    other = swap(mine)
    away = (owner // 2 - z) % 4
    same = owner % 2 == core
    low = slot < 2
    stage = jnp.where(away == 0, 0, jnp.where(away == 2, 2, 1))
    side = jnp.where(away == 2, jnp.where(low, 0, 1), jnp.where(away == 3, 0, 1))
    late = (away % 2 == 1) & ((away == 3) != low)
    source = jnp.where(away == 0, 0, side + jnp.where(late, 4, 0)) + jnp.where(
        same, 0, jnp.where(away == 0, 1, 2)
    )
    index = jnp.where(away == 0, slot, slot % 2)
    ids = jnp.arange(blocks)
    rank = jnp.sum((stage[None] == stage[:, None]) & (ids[None] < ids[:, None]), axis=1)
    counts = jnp.sum(stage[None] == jnp.arange(3)[:, None], axis=1)
    most = (4, blocks, 4)
    turn = jnp.minimum(jnp.arange(blocks)[None], counts[:, None] - 1)
    chosen = (stage[None, None] == jnp.arange(3)[:, None, None]) & (rank[None, None] == turn[:, :, None])
    of = lambda v: jnp.sum(jnp.where(chosen, v[None, None], 0), axis=2)
    block = jnp.where(counts[:, None] > 0, of(ids), blocks).astype(jnp.int32)
    source, index = of(source).astype(jnp.int32), of(index).astype(jnp.int32)
    counts = counts.astype(jnp.int32)

    whole = lambda *dims: pl.BlockSpec(dims, lambda b, *_: (0,) * len(dims))
    tall = lambda width: pl.BlockSpec((BLOCK, width), lambda b, *_: (b, 0))
    lead = lambda *dims: pl.BlockSpec((1, *dims), lambda b, *_: (b,) + (0,) * len(dims))
    table_rows = pl.BlockSpec((32, BLOCK), lambda b, *_: (0, b))
    vmem = lambda kind, *dims: pltpu.VMEM(dims, kind)

    up, rows, cols, ends = call(
        upstream_kernel,
        "upstream",
        (
            shape((steps, D), BF16),
            shape((32, steps), F32),
            shape((steps, 128), F32),
            shape((blocks, 8, 128), F32),
        ),
        pltpu.PrefetchScalarGridSpec(
            num_scalar_prefetch=1,
            grid=(blocks,),
            in_specs=[
                pl.BlockSpec((HEADS, BLOCK), lambda b, *_: (0, b)),
                pl.BlockSpec((1, 1, BLOCK), lambda b, *_: (b, 0, 0)),
                pl.BlockSpec((1, BLOCK, D), lambda b, *_: (0, b, 0)),
                whole(D, D),
            ],
            out_specs=[tall(D), table_rows, tall(128), lead(8, 128)],
        ),
        2 * steps * D * D,
        12 << 20,
    )(fill, log_decay[0], resets.reshape(blocks, 1, BLOCK), cotangent, w_out)

    room = steps + BLOCK
    made = None
    for s in range(3):
        if s == 0:
            below_a, above_a, second, first, up = lax.optimization_barrier(
                (below_a, above_a, second, first, up)
            )
            below_b, above_b = up_z(second), down_z(first)
            sources, near = (mine, other), (below_a, above_a, swap(below_a), swap(above_a))
        elif s == 1:
            below_b, above_b, below_a, above_a, made = lax.optimization_barrier(
                (below_b, above_b, below_a, above_a, made)
            )
            far_low, far_high = up_z(below_a), down_z(above_a)
            sources = (*near, below_b, above_b, swap(below_b), swap(above_b))
        else:
            far_low, far_high, made = lax.optimization_barrier((far_low, far_high, made))
            sources = (far_low, far_high, swap(far_low), swap(far_high))
        number = len(sources)
        at = lambda i, block, *_: block[i]
        inside_at = lambda i, block, *_: jnp.minimum(block[i], blocks - 1)
        out_rows = lambda width: pl.BlockSpec((BLOCK, width), lambda i, block, *_: (block[i], 0))
        out_lead = lambda *dims: pl.BlockSpec((1, *dims), lambda i, block, *_: (block[i], 0, 0))
        in_rows = lambda width: pl.BlockSpec(
            (BLOCK, width), lambda i, block, *_: (jnp.minimum(block[i], blocks - 1), 0)
        )
        pick = lambda n: pl.BlockSpec(
            (pl.squeezed, BLOCK, D),
            lambda i, block, source, index, *_: (jnp.where(source[i] == n, index[i], 0), 0, 0),
        )
        kept = [] if made is None else list(made)
        body = lambda block, source, index, fill, count, *refs, number=number: stage_kernel(
            count, number, block, source, index, fill, *refs
        )
        made = pl.pallas_call(
            body,
            out_shape=(
                shape((room, D), BF16),
                shape((room, D), BF16),
                shape((room, 128), BF16),
                shape((room, D), BF16),
                shape((room, D), BF16),
                shape((blocks + 1, BLOCK, BLOCK), BF16),
                shape((blocks + 1, STATE, D), F32),
                shape((blocks + 1, STATE, D), F32),
            ),
            grid_spec=pltpu.PrefetchScalarGridSpec(
                num_scalar_prefetch=5,
                grid=(most[s],),
                in_specs=[pick(n) for n in range(number)]
                + [
                    whole(D, D),
                    whole(D, 128),
                    in_rows(D),
                    pl.BlockSpec((32, BLOCK), lambda i, block, *_: (0, jnp.minimum(block[i], blocks - 1))),
                    in_rows(128),
                ]
                + [pl.BlockSpec(memory_space=pl.ANY)] * len(kept),
                out_specs=[
                    out_rows(D),
                    out_rows(D),
                    out_rows(128),
                    out_rows(D),
                    out_rows(D),
                    out_lead(BLOCK, BLOCK),
                    out_lead(STATE, D),
                    out_lead(STATE, D),
                ],
                scratch_shapes=[vmem(BF16, 256, D)],
            ),
            input_output_aliases={5 + number + 5 + n: n for n in range(len(kept))},
            name=f"stage_{s}",
            compiler_params=pltpu.CompilerParams(vmem_limit_bytes=32 * MIB),
            cost_estimate=pl.CostEstimate(
                flops=4 * BLOCK * D * (D + 1024) + 4 * HEADS * 3 * BLOCK**3,
                bytes_accessed=16 << 20,
                transcendentals=0,
            ),
        )(block[s], source[s], index[s], fill, counts[s : s + 1], *sources, w_in, w_bc, up, rows, cols, *kept)
    taken, inner, keys, ro, gi, pair, push_in, push_out = made

    some = lambda *dims: pl.BlockSpec((blocks // 2, *dims), lambda b, *_: (b, 0, 0))
    starts, gains, total = call(
        local_kernel,
        "local",
        (shape((blocks, STATE, D), F32), shape((blocks, 16, D), F32), shape((shards, 80, 128), BF16)),
        pl.GridSpec(
            grid=(2,),
            in_specs=[some(STATE, D), some(STATE, D), whole(blocks, 8, 128)],
            out_specs=[some(STATE, D), some(16, D), whole(shards, 80, 128)],
            scratch_shapes=[vmem(F32, blocks * 8, D), vmem(F32, 136, D)],
        ),
        1 << 24,
        7 << 20,
    )(push_in, push_out, ends)

    terms = lax.all_to_all(total, TM, 0, 0)
    entering = call(
        scan_kernel,
        "scan",
        shape((shards, 8, D), BF16),
        pltpu.PrefetchScalarGridSpec(
            num_scalar_prefetch=1,
            grid=(1,),
            in_specs=[whole(shards, 80, 128)],
            out_specs=whole(shards, 8, D),
            scratch_shapes=[vmem(F32, shards, 8, D)],
        ),
        1 << 20,
        1 << 20,
    )(lax.axis_index(TM).reshape(1), terms)
    enter = lax.all_to_all(entering, TM, 0, 0).reshape(128, D)

    own_core = core.reshape(1)
    two = lambda width: pl.BlockSpec((2 * BLOCK, width), lambda b, *_: (b, 0))
    pairs = lambda *dims: pl.BlockSpec((2, *dims), lambda b, *_: (b, 0, 0))
    back = lambda spec: pl.BlockSpec(
        spec.block_shape, lambda s, *refs: spec.index_map(blocks // 2 - 1 - s, *refs)
    )
    wide = D + 128
    both = wide + D
    keep, give = call(
        gradient_kernel,
        "gradient",
        (shape((D // 2, both), F32), shape((D // 2, both), BF16)),
        pltpu.PrefetchScalarGridSpec(
            num_scalar_prefetch=2,
            grid=(blocks // 2,),
            in_specs=[
                back(s)
                for s in (
                    pl.BlockSpec((1, 2 * BLOCK, D), lambda b, *_: (0, b, 0)),
                    two(D),
                    two(D),
                    two(D),
                    two(128),
                    two(128),
                    two(D),
                    two(D),
                    pairs(BLOCK, BLOCK),
                    pairs(STATE, D),
                    pairs(STATE, D),
                    pairs(16, D),
                    whole(128, D),
                )
            ],
            out_specs=[whole(D // 2, both), whole(D // 2, both)],
            scratch_shapes=[
                vmem(F32, D // 16, 2, 8, wide),
                vmem(F32, D // 16, 2, 8, D),
                vmem(BF16, 2 * BLOCK, D),
                vmem(BF16, 2 * BLOCK, wide),
                vmem(BF16, 2 * BLOCK, D),
                vmem(F32, STATE, D),
                vmem(BF16, 256, D),
            ],
        ),
        2 * steps * D * (2 * D + 1280),
        36 << 20,
        room=GRADIENT_ROOM,
    )(own_core, fill, cotangent, taken, inner, up, keys, cols, ro, gi, pair, starts, push_out, gains, enter)

    grads = over_chips(over_chip(keep, give))
    return (grads[:, :D], grads[:, D:wide], grads[:, wide:])


def solution(mesh):
    torus = Mesh(mesh.devices.reshape(4, 4, 4, 2), ("y", "x", "z", "c"))
    lane = ("z", "c")
    every = TM + lane
    return jax.shard_map(
        on_device,
        mesh=torus,
        in_specs=(
            P(lane, TM, None, None),
            P(TM, None, None, None),
            P(TM, None, None),
            P(lane, TM, None),
            P(lane, None, TM),
            P(lane, TM),
            P(lane, TM, None),
            P(),
            P(),
            P(),
        ),
        out_specs=(P(every, None), P(every, None), P(every, None)),
        check_vma=False,
    )
```
